512 devices in a mesh: dp: 128 (over y, z, core), rep: 4 (over x).
Axes of the slice: x: 4, y: 8, z: 8, core: 2. Of those that a mesh axis runs over, the one named last changes fastest.
Arguments:
- grad_parts: bfloat16 [4, 128, 512, 512], P('rep', None, 'dp')
- left_stat: float32 [128, 512, 512], P('dp', 'rep'), may hold values from -6 to 6
- right_stat: float32 [128, 512, 512], P('dp', 'rep'), may hold values from -6 to 6
- left_root: bfloat16 [128, 512, 512], P('dp', 'rep'), as said below
- right_root: bfloat16 [128, 512, 512], P('dp', 'rep'), as said below
- block_slot: int32 [128], replicated, may hold values from 0 to 127, each once
- block_modality: int32 [128], replicated, may hold values from 0 to 1, as said below
- modality_rates: float32 [2], replicated, may hold values from 0.5 to 2
Outputs:
- update: float32 [128, 512, 512], P(None, 'dp')
- left_new: float32 [128, 512, 512], P('dp', 'rep')
- right_new: float32 [128, 512, 512], P('dp', 'rep')
The draws below stay inside these ranges and needn't reach their ends.
Inputs may be any that keep to these rules, and one draw needn't show every extreme that they name: `block_slot`: each device along dp owns exactly one slot: slot s belongs to index s of dp. `block_modality`: both modalities name at least one block. `left_root`: each block is symmetric. `right_root`: each block is symmetric.
All inputs are finite; a program needn't handle non-finite values.
Results may differ from the reference program's by a relative error of at most 0.0003.
Values may be sent and summed in bfloat16 or wider, within the bound.
A program may use at most 64 MiB of HBM per device.

```python
import math
import jax
import jax.numpy as jnp
from jax import lax

BLK = 512
NB = 128
N_REP = 4


def modality_draw(key):
    key = jax.random.fold_in(key, 71)
    key_bits, key_spot, key_quiet = jax.random.split(key, 3)
    labels = jax.random.randint(key_bits, (NB,), 0, 2)
    spot = jax.random.randint(key_spot, (), 0, NB - 1)
    positions = jnp.arange(NB)
    labels = jnp.where(positions == spot, 0, labels)
    labels = jnp.where(positions == spot + 1, 1, labels)
    quiet = jax.random.randint(key_quiet, (), 0, 2)
    return (labels.astype(jnp.int32), quiet)


def draw_grad_parts(key, part):
    labels, quiet = modality_draw(key)
    key = jax.random.fold_in(key, 11)
    key_rows, key_cols, key_blocks, key_base = jax.random.split(key, 4)
    positions = jnp.arange(BLK, dtype=jnp.float32) / BLK
    row_scale = (3.0 ** positions)[None, :] * jnp.exp(jax.random.uniform(key_rows, (NB, BLK), jnp.float32, 0.0, math.log(2.2)))
    col_scale = jnp.exp(jax.random.uniform(key_cols, (NB, BLK), jnp.float32, 0.0, math.log(3.0)))
    block_scale = jnp.exp(jax.random.uniform(key_blocks, (NB,), jnp.float32, 0.0, math.log(3.0)))
    base = 0.25 * jax.random.normal(key_base, (N_REP, NB, BLK, BLK), jnp.float32)
    modality_scale = jnp.where(labels == quiet, 0.037, 0.37)
    block_scale = block_scale * modality_scale
    values = base * row_scale[None, :, :, None] * col_scale[None, :, None, :] * block_scale[None, :, None, None]
    return values.astype(jnp.bfloat16)


def draw_left_root(key, part):
    key = jax.random.fold_in(key, 23)
    key_diag, key_noise = jax.random.split(key)
    diagonal = jnp.exp(jax.random.uniform(key_diag, (NB, BLK), jnp.float32, 0.0, math.log(10.0)))
    noise = jax.random.normal(key_noise, (NB, BLK, BLK), jnp.float32)
    symmetric = (noise + jnp.transpose(noise, (0, 2, 1))) * (0.4 / math.sqrt(2.0 * BLK))
    identity = (jnp.arange(BLK)[:, None] == jnp.arange(BLK)[None, :]).astype(jnp.float32)
    root_half = jnp.sqrt(diagonal)
    values = root_half[:, :, None] * root_half[:, None, :] * (identity[None] + symmetric)
    return values.astype(jnp.bfloat16)


def draw_right_root(key, part):
    key = jax.random.fold_in(key, 37)
    key_diag, key_noise = jax.random.split(key)
    diagonal = jnp.exp(jax.random.uniform(key_diag, (NB, BLK), jnp.float32, 0.0, math.log(10.0)))
    noise = jax.random.normal(key_noise, (NB, BLK, BLK), jnp.float32)
    symmetric = (noise + jnp.transpose(noise, (0, 2, 1))) * (0.4 / math.sqrt(2.0 * BLK))
    identity = (jnp.arange(BLK)[:, None] == jnp.arange(BLK)[None, :]).astype(jnp.float32)
    root_half = jnp.sqrt(diagonal)
    values = root_half[:, :, None] * root_half[:, None, :] * (identity[None] + symmetric)
    return values.astype(jnp.bfloat16)


def draw_block_modality(key, part):
    labels, quiet = modality_draw(key)
    return labels


def level_of(rng, shape, pieces, low, high):
    def one(axis_at, parts):
        heights = jax.random.uniform(jax.random.fold_in(jax.random.fold_in(rng, 6), axis_at), (parts,), jnp.float32, low / len(pieces), high / len(pieces))
        return jnp.repeat(jnp.exp(heights), shape[axis_at] // parts).reshape((-1,) + (1,) * (len(shape) - axis_at - 1))

    factor_of = one(*pieces[0])
    for cut in pieces[1:]:
        factor_of = factor_of * one(*cut)
    return factor_of


def centred(key, shape, scale, most, cuts=(), kind=jnp.bfloat16):
    gain = level_of(key, shape, cuts, -0.22, 0.18) if cuts else 1.0
    drawn = jax.random.normal(key, shape, jnp.float32) * scale * gain
    return jnp.minimum(jnp.maximum(drawn, -most), most).astype(kind)


def setup_inputs(seed: int = 0) -> dict:
    key_list = jax.random.split(jax.random.key(seed), 9)
    grad_parts = draw_grad_parts(jax.random.fold_in(key_list[8], 71), 0)
    left_stat = centred(key_list[1], (NB, BLK, BLK), 1.0, 6.0, ((0, 128), (1, 4)), jnp.float32)
    right_stat = centred(key_list[2], (NB, BLK, BLK), 1.0, 6.0, ((0, 128), (1, 4)), jnp.float32)
    left_root = draw_left_root(jax.random.fold_in(key_list[8], 71), 0)
    right_root = draw_right_root(jax.random.fold_in(key_list[8], 71), 0)
    block_slot = jax.random.permutation(key_list[5], NB).astype(jnp.int32)
    block_modality = draw_block_modality(jax.random.fold_in(key_list[8], 71), 0)
    modality_rates = jnp.clip(jnp.exp(jax.random.uniform(key_list[7], (2,), jnp.float32, math.log(0.5), math.log(2.0))), 0.5, 2.0)
    return {"grad_parts": grad_parts, "left_stat": left_stat, "right_stat": right_stat, "left_root": left_root, "right_root": right_root, "block_slot": block_slot, "block_modality": block_modality, "modality_rates": modality_rates}


beta_decay = 0.95
clip_level = 0.5

def matmul(left, right):
    return jnp.dot(left, right, precision=lax.Precision.HIGHEST, preferred_element_type=jnp.float32)

def reference(grad_parts, left_stat, right_stat, left_root, right_root, block_slot, block_modality, modality_rates):
    gradient = lax.optimization_barrier(jnp.sum(grad_parts.astype(jnp.float32), axis=0))
    count_all = block_slot.shape[0]
    slot_block = jnp.zeros((count_all,), jnp.int32).at[block_slot].set(jnp.arange(count_all, dtype=jnp.int32))

    def per_slot(index):
        block = gradient[slot_block[index]]
        left_next = beta_decay * left_stat[index] + (1.0 - beta_decay) / BLK * matmul(block, block.T)
        right_next = beta_decay * right_stat[index] + (1.0 - beta_decay) / BLK * matmul(block.T, block)
        mixed = matmul(block, right_root[index].astype(jnp.float32))
        precond = matmul(left_root[index].astype(jnp.float32), mixed)
        return (left_next, right_next, precond, jnp.sum(block * block), jnp.sum(precond * precond))
    left_new, right_new, precond, grad_sq, prec_sq = lax.map(per_slot, jnp.arange(count_all, dtype=jnp.int32))
    modality_slot = block_modality[slot_block]
    labels = jnp.arange(2, dtype=jnp.int32)
    onehot = (modality_slot[:, None] == labels[None, :]).astype(jnp.float32)
    totals = lax.optimization_barrier(jnp.sum(onehot * grad_sq[:, None], axis=0))
    counts = lax.optimization_barrier(jnp.sum((block_modality[:, None] == labels[None, :]).astype(jnp.float32), axis=0))
    spread = jnp.sqrt(totals / (counts * BLK * BLK) + 1e-06)
    clipping = jnp.minimum(1.0, clip_level / spread)
    graft = jnp.sqrt(grad_sq / (prec_sq + 1e-06))
    scale = lax.optimization_barrier(jnp.sum(onehot * (modality_rates * clipping)[None, :], axis=1)) * graft
    step_slot = scale[:, None, None] * precond
    update = step_slot[block_slot]
    return (update, left_new, right_new)
```

```python
import functools

import jax
import jax.numpy as jnp
from jax import lax
from jax.experimental import pallas as pl
from jax.experimental.pallas import tpu as pltpu
from jax.sharding import PartitionSpec as P

MESH = pl.DeviceIdType.MESH
DECAY = 0.95
CLIP = 0.5
BLK = 512
F32 = jnp.float32
BF16 = jnp.bfloat16
PIECES = 4


def iota(shape, axis):
    return lax.broadcasted_iota(jnp.int32, shape, axis)


def dot(a, b):
    return jnp.dot(a, b, preferred_element_type=F32)


def dot_nt(a, b):
    return lax.dot_general(a, b, (((1,), (1,)), ((), ())), preferred_element_type=F32)


def halves(value):
    high = value.astype(BF16)
    return high, (value - high.astype(F32)).astype(BF16)


def kernel(
    slot_ref, modality_ref, rates_ref, grad_hbm, lstat_hbm, rstat_hbm, lroot_hbm, rroot_hbm,
    update_hbm, lnew_hbm, rnew_hbm,
    grad, lstat, rstat, rroot, lfull, parts, got, mixed_out, plane, gfull, ghigh, glow,
    back, back_plane, mine, meta_out, meta_in, half, final, spread, update, lnew, rnew,
    in_sem, out_sem, p_send, p_recv, l_send, l_recv, a_send, a_recv, b_send, b_recv,
    g_send, g_recv, h_send, h_recv, c_send, c_recv, d_send, d_recv, m_send, m_recv,
    f_send, f_recv, r_send, r_recv,
):
    x = lax.axis_index("rep")
    d = lax.axis_index("dp")
    c = lax.rem(d, 2)
    z = lax.rem(lax.div(d, 2), 8)
    y = lax.div(d, 16)
    i = y + c * (z - y)
    j = z + c * (y - z)

    def on_plane(a, b):
        return (16 * (a + c * (b - a)) + 2 * (b + c * (a - b)) + c, x)

    def on_column(to_x, to_c):
        return (d - c + to_c, to_x)

    def send(src, dst, s_sem, r_sem, device):
        return pltpu.make_async_remote_copy(
            src_ref=src, dst_ref=dst, send_sem=s_sem, recv_sem=r_sem, device_id=device, device_id_type=MESH
        )

    column = [(dx, dc) for dx in (2, 1, 3, 0) for dc in (0, 1) if (dx, dc) != (0, 0)]

    barrier = pltpu.get_barrier_semaphore()
    for dx, dc in column:
        pl.semaphore_signal(
            barrier, inc=1, device_id=on_column(lax.rem(x + dx, 4), lax.rem(c + dc, 2)), device_id_type=MESH
        )
    for e in range(1, 8):
        pl.semaphore_signal(barrier, inc=1, device_id=on_plane(lax.rem(i + e, 8), j), device_id_type=MESH)
        pl.semaphore_signal(barrier, inc=1, device_id=on_plane(i, lax.rem(j + e, 8)), device_id_type=MESH)

    loads = [
        pltpu.make_async_copy(grad_hbm.at[0], grad, in_sem.at[0]),
        pltpu.make_async_copy(lroot_hbm.at[0], lfull.at[x], in_sem.at[1]),
        pltpu.make_async_copy(rroot_hbm.at[0], rroot, in_sem.at[2]),
        pltpu.make_async_copy(lstat_hbm.at[0], lstat, in_sem.at[3]),
        pltpu.make_async_copy(rstat_hbm.at[0], rstat, in_sem.at[4]),
    ]
    for load in loads:
        load.start()

    slots = slot_ref[...]
    slots8 = jnp.broadcast_to(slots, (8, 128)).astype(F32).astype(BF16)
    widen = (lax.shift_right_logical(iota((128, 512), 1), 2) == iota((128, 512), 0)).astype(F32).astype(BF16)
    code_row = 4 * dot(slots8, widen)[0:1, :].astype(jnp.int32) + (iota((1, 512), 1) & 3)
    row = iota((512, 128), 0)
    row_first = lax.shift_right_logical(row, 5) & 7
    row_second = lax.shift_right_logical(row, 2) & 7
    row_core = lax.shift_right_logical(row, 8)
    row_slot = jnp.where(row_core == 0, 16 * row_first + 2 * row_second, 16 * row_second + 2 * row_first + 1)
    row_code = 4 * row_slot + (row & 3)
    order = jnp.concatenate(
        [(row_code == code_row[:, 128 * t : 128 * t + 128]).astype(F32).astype(BF16) for t in range(4)], axis=1
    )
    loads[0].wait()
    flat = grad[...].reshape(512, 512)
    for q in range(4):
        ordered = dot(order, flat[:, 128 * q : 128 * q + 128]).astype(BF16)
        parts[q, 0] = ordered[:256]
        parts[q, 1] = ordered[256:]
    pl.semaphore_wait(barrier, len(column) + 14)

    first = []
    for dx, dc in column:
        to_x, to_c = lax.rem(x + dx, 4), lax.rem(c + dc, 2)
        copy = send(parts.at[to_x, to_c], got.at[x, c], p_send.at[dx, dc], p_recv.at[dx, c], on_column(to_x, to_c))
        copy.start()
        first.append(copy)
    loads[1].wait()
    roots = []
    for dx in (2, 1, 3):
        to_x = lax.rem(x + dx, 4)
        copy = send(lfull.at[x], lfull.at[x], l_send.at[dx], l_recv.at[dx], on_column(to_x, c))
        roots.append(copy)
    got[x, c] = parts[x, c]
    for dx, dc in column:
        from_c = lax.rem(c + dc, 2)
        send(parts.at[0, 0], got.at[0, 0], p_send.at[dx, dc], p_recv.at[dx, from_c], on_column(x, c)).wait_recv()
    for copy in roots:
        copy.start()
    sums = []
    for core in range(2):
        total = got[0, core].astype(F32)
        for q in range(1, 4):
            total = total + got[q, core].astype(F32)
        sums.append(total.reshape(32, 8, 128))
    upper = iota((32, 8, 128), 1) < 4
    even = jnp.where(upper, sums[0], pltpu.roll(sums[1], 4, 1))
    odd = jnp.where(upper, pltpu.roll(sums[0], 4, 1), sums[1])
    mixed_out[:, :, 0] = even.reshape(8, 4, 8, 128)
    mixed_out[:, :, 1] = odd.reshape(8, 4, 8, 128)

    stage_a = []
    for e in range(1, 8):
        to = lax.rem(i + e, 8)
        copy = send(
            mixed_out.at[to], plane.at[i], a_send.at[e], a_recv.at[e], on_plane(to, j)
        )
        copy.start()
        stage_a.append(copy)
    plane[i] = mixed_out[i]
    for copy in stage_a:
        copy.wait_recv()
    plane_flat = plane.reshape(8, 8, 8, 128)
    stage_b = []
    for e in range(1, 8):
        to = lax.rem(j + e, 8)

        def cut(src, dst, e=e, to=to):
            return send(src, dst, b_send.at[e], b_recv.at[e], on_plane(i, to))

        @pl.when(c == 0)
        def _(cut=cut, to=to):
            cut(plane_flat.at[:, to], gfull.at[x, :, j]).start()

        @pl.when(c == 1)
        def _(cut=cut, to=to):
            cut(plane_flat.at[:, to], gfull.at[x, j]).start()

        stage_b.append(cut(plane_flat.at[:, 0], gfull.at[x, 0]))

    own = plane_flat[:, j]

    @pl.when(c == 0)
    def _():
        gfull[x, :, j] = own

    @pl.when(c == 1)
    def _():
        gfull[x, j] = own

    right, left = lax.rem(x + 1, 4), lax.rem(x + 3, 4)

    def piece(e, q, s_sem, r_sem, to):
        at = lax.rem(j + 8 - e, 8)

        @pl.when(c == 0)
        def _():
            send(gfull.at[q, :, at], gfull.at[q, :, at], s_sem, r_sem, on_column(to, c)).start()

        @pl.when(c == 1)
        def _():
            send(gfull.at[q, at], gfull.at[q, at], s_sem, r_sem, on_column(to, c)).start()

        return send(gfull.at[q, 0], gfull.at[q, 0], s_sem, r_sem, on_column(to, c))

    rightward, leftward, relayed = [], [], []

    def relay(e):
        if e % 2 == 0:
            rightward[e].wait_recv()
            relayed.append(piece(e, left, h_send.at[e], h_recv.at[e], right))
        else:
            leftward[e].wait_recv()
            relayed.append(piece(e, right, h_send.at[e], h_recv.at[e], left))

    for e in range(8):
        if e > 0:
            stage_b[e - 1].wait_recv()
        rightward.append(piece(e, x, g_send.at[0, e], g_recv.at[0, e], right))
        leftward.append(piece(e, x, g_send.at[1, e], g_recv.at[1, e], left))
        if e >= 2:
            relay(e - 2)

    def take(q):
        high, low = halves(gfull[q].reshape(512, 128))
        at = pl.ds(pl.multiple_of(128 * q, 128), 128)
        ghigh[:, at] = high
        glow[:, at] = low
        other = rroot[:, at]
        return dot_nt(high, other) + dot_nt(low, other)

    loads[2].wait()
    own = gfull[x].reshape(512, 128)
    grad_sq = jnp.sum(own * own)
    relay(6)
    relay(7)
    product = take(x)
    for e in range(8):
        if e % 2 == 1:
            rightward[e].wait_recv()
    product = product + take(left)
    for e in range(8):
        if e % 2 == 0:
            leftward[e].wait_recv()
    product = product + take(right)
    for copy in roots:
        copy.wait_recv()
    for copy in relayed:
        copy.wait_recv()
    product = product + take(lax.rem(x + 2, 4))
    product = jnp.concatenate(halves(product), axis=1)
    prec_sq = 0.0
    for q in range(4):
        rows = dot(lfull[q], product)
        rows = rows[:, :128] + rows[:, 128:]
        prec_sq = prec_sq + jnp.sum(rows * rows)
        back[2 * q : 2 * q + 2, 0:8] = rows.reshape(2, 8, 8, 128)
    lane = iota((8, 128), 1)
    sub = iota((8, 128), 0)
    meta = jnp.where(
        sub == i, jnp.where(lane == j, grad_sq, 0.0) + jnp.where(lane == 64 + j, prec_sq, 0.0), 0.0
    )
    for e in range(8):
        back[8, e] = meta
        back[e, 8] = meta

    stage_c = []
    for e in range(1, 8):
        to = lax.rem(i + e, 8)

        def cut(src, e=e, to=to):
            return send(src, back_plane.at[i], c_send.at[e], c_recv.at[e], on_plane(to, j))

        @pl.when(c == 0)
        def _(cut=cut, to=to):
            cut(back.at[to]).start()

        @pl.when(c == 1)
        def _(cut=cut, to=to):
            cut(back.at[:, to]).start()

        stage_c.append(cut(back.at[0]))

    @pl.when(c == 0)
    def _():
        back_plane[i] = back[i]

    @pl.when(c == 1)
    def _():
        back_plane[i] = back[:, i]

    for copy in stage_c:
        copy.wait_recv()
    meta = back_plane[0, 8]
    for e in range(1, 8):
        meta = meta + back_plane[e, 8]
    for e in range(8):
        back_plane[8, e] = meta
    stage_d = []
    for e in range(1, 8):
        to = lax.rem(j + e, 8)
        copy = send(back_plane.at[:, to], mine.at[j], d_send.at[e], d_recv.at[e], on_plane(i, to))
        copy.start()
        stage_d.append(copy)
    mine[j] = back_plane[:, j]

    loads[3].wait()
    loads[4].wait()
    gain = (1.0 - DECAY) / BLK
    mine_rows = pl.ds(pl.multiple_of(128 * x, 128), 128)
    high, low = ghigh[...], glow[...]
    high_rows, low_rows = ghigh[mine_rows, :], glow[mine_rows, :]
    lnew[...] = DECAY * lstat[...] + gain * (dot_nt(high_rows, high) + (dot_nt(high_rows, low) + dot_nt(low_rows, high)))
    turned = gfull[x].reshape(512, 128).T
    high_turned, low_turned = halves(turned)
    rnew[...] = DECAY * rstat[...] + gain * (dot(high_turned, high) + (dot(high_turned, low) + dot(low_turned, high)))
    out_l = pltpu.make_async_copy(lnew, lnew_hbm.at[0], out_sem.at[0])
    out_r = pltpu.make_async_copy(rnew, rnew_hbm.at[0], out_sem.at[1])
    out_l.start()
    out_r.start()

    block_of_row = lax.shift_right_logical(row, 2)
    lanes = iota((512, 128), 1)
    is_block = lanes == block_of_row
    slot_col = jnp.sum(jnp.where(is_block, slots.astype(F32), 0.0), axis=1, keepdims=True)
    code_col = 4 * slot_col.astype(jnp.int32) + (iota((512, 1), 0) & 3)
    col = iota((1, 512), 1)
    col_second = lax.shift_right_logical(col, 5) & 7
    col_first = lax.shift_right_logical(col, 2) & 7
    col_slot = jnp.where(
        lax.shift_right_logical(col, 8) == 0, 16 * col_first + 2 * col_second, 16 * col_second + 2 * col_first + 1
    )
    col_code = 4 * col_slot + (col & 3)
    spread[...] = (code_col == col_code).astype(F32).astype(BF16)

    for copy in stage_d:
        copy.wait_recv()
    meta = mine[0, 8]
    for e in range(1, 8):
        meta = meta + mine[e, 8]
    meta_out[...] = meta
    metas = []
    for dx, dc in column:
        to_x, to_c = lax.rem(x + dx, 4), lax.rem(c + dc, 2)
        copy = send(meta_out, meta_in.at[x, c], m_send.at[dx, dc], m_recv.at[dx, c], on_column(to_x, to_c))
        copy.start()
        metas.append(copy)
    meta_in[x, c] = meta

    tiles = mine[:, 0:8].reshape(32, 2, 8, 128)
    a, b = tiles[:, 0], tiles[:, 1]
    half[0] = jnp.where(upper, a, pltpu.roll(b, 4, 1))
    half[1] = jnp.where(upper, pltpu.roll(a, 4, 1), b)
    size = 32 // PIECES
    cuts = [pl.ds(size * p, size) for p in range(PIECES)]
    sends = []
    for p in range(PIECES):
        for dx in (1, 3, 0):
            for dc in range(2):
                if (dx, dc) == (0, 0):
                    continue
                to_x, to_c = lax.rem(x + dx, 4), lax.rem(c + dc, 2)
                copy = send(
                    half.at[to_c, cuts[p]], final.at[x, c, cuts[p]], f_send.at[dx, dc, p], f_recv.at[dx, c, p],
                    on_column(to_x, to_c),
                )
                copy.start()
                sends.append(copy)
    final[x, c] = half[c]

    def came(dx, core, p):
        send(half.at[0, cuts[p]], final.at[0, 0, cuts[p]], f_send.at[1, 0, p], f_recv.at[dx, core, p], on_column(x, c)).wait_recv()

    for dx, dc in column:
        send(meta_out, meta_in.at[0, 0], m_send.at[dx, dc], m_recv.at[dx, lax.rem(c + dc, 2)], on_column(x, c)).wait_recv()
    grad_b = jnp.zeros((8, 128), F32)
    prec_b = jnp.zeros((8, 128), F32)
    for core in range(2):
        known = meta_in[0, core] + meta_in[1, core] + meta_in[2, core] + meta_in[3, core]
        for e in range(8):
            slot_here = 16 * sub + 2 * e if core == 0 else 16 * e + 2 * sub + 1
            here = slots == slot_here
            grad_b = grad_b + jnp.where(here, known[:, e : e + 1], 0.0)
            prec_b = prec_b + jnp.where(here, known[:, 64 + e : 65 + e], 0.0)
    grad_b = jnp.sum(grad_b, axis=0, keepdims=True)
    prec_b = jnp.sum(prec_b, axis=0, keepdims=True)
    scale = jnp.zeros((1, 128), F32)
    for m in range(2):
        member = modality_ref[...] == m
        total = jnp.sum(jnp.where(member, grad_b, 0.0), axis=1, keepdims=True)
        count = jnp.sum(jnp.where(member, 1.0, 0.0), axis=1, keepdims=True)
        rms = jnp.sqrt(total / (count * (BLK * BLK)) + 1e-6)
        clip = jnp.minimum(1.0, CLIP / rms)
        scale = jnp.where(member, rates_ref[m] * clip, scale)
    scale = scale * jnp.sqrt(grad_b / (prec_b + 1e-6))
    scale_col = jnp.sum(jnp.where(is_block, scale, 0.0), axis=1, keepdims=True)

    outs = []

    def finish(q):
        high, low = halves(final[q].reshape(512, 128))
        both = dot(spread[...], jnp.concatenate([high, low], axis=1))
        rows = (both[:, :128] + both[:, 128:]) * scale_col
        at = pl.ds(pl.multiple_of(128 * q, 128), 128)
        update[:, at] = rows
        copy = pltpu.make_async_copy(update.at[:, at], update_hbm.at[:, at], out_sem.at[2 + len(outs)])
        copy.start()
        outs.append(copy)

    for p in range(PIECES):
        came(1, 0, p)
        copy = send(final.at[left, 0, cuts[p]], final.at[left, 0, cuts[p]], r_send.at[0, p], r_recv.at[0, p], on_column(right, c))
        copy.start()
        sends.append(copy)
        came(3, 1, p)
        copy = send(final.at[right, 1, cuts[p]], final.at[right, 1, cuts[p]], r_send.at[1, p], r_recv.at[1, p], on_column(left, c))
        copy.start()
        sends.append(copy)
    for p in range(PIECES):
        came(0, 1 - c, p)
    finish(x)
    for p in range(PIECES):
        came(1, 1, p)
    finish(left)
    for p in range(PIECES):
        came(3, 0, p)
    finish(right)
    for p in range(PIECES):
        for way in range(2):
            send(half.at[0, cuts[p]], final.at[0, 0, cuts[p]], r_send.at[way, p], r_recv.at[way, p], on_column(x, c)).wait_recv()
    finish(lax.rem(x + 2, 4))

    for copy in first + roots + stage_a + stage_b + rightward + leftward + relayed + stage_c + stage_d + metas + sends:
        copy.wait_send()
    for copy in outs:
        copy.wait()
    out_l.wait()
    out_r.wait()


def local(grad_parts, left_stat, right_stat, left_root, right_root, block_slot, block_modality, modality_rates):
    vmem = pl.BlockSpec(memory_space=pltpu.VMEM)
    smem = pl.BlockSpec(memory_space=pltpu.SMEM)
    hbm = pl.BlockSpec(memory_space=pl.ANY)
    dma = pltpu.SemaphoreType.DMA
    update, left_new, right_new = pl.pallas_call(
        kernel,
        out_shape=(
            jax.ShapeDtypeStruct((512, 512), F32),
            jax.ShapeDtypeStruct(left_stat.shape, F32),
            jax.ShapeDtypeStruct(right_stat.shape, F32),
        ),
        in_specs=[vmem, vmem, smem, hbm, hbm, hbm, hbm, hbm],
        out_specs=(hbm, hbm, hbm),
        scratch_shapes=[
            pltpu.VMEM((128, 4, 512), BF16),
            pltpu.VMEM((128, 512), F32),
            pltpu.VMEM((128, 512), F32),
            pltpu.VMEM((128, 512), BF16),
            pltpu.VMEM((4, 128, 512), BF16),
            pltpu.VMEM((4, 2, 256, 128), BF16),
            pltpu.VMEM((4, 2, 256, 128), BF16),
            pltpu.VMEM((8, 4, 2, 8, 128), F32),
            pltpu.VMEM((8, 4, 2, 8, 128), F32),
            pltpu.VMEM((4, 8, 8, 8, 128), F32),
            pltpu.VMEM((512, 512), BF16),
            pltpu.VMEM((512, 512), BF16),
            pltpu.VMEM((9, 9, 8, 128), F32),
            pltpu.VMEM((9, 9, 8, 128), F32),
            pltpu.VMEM((8, 9, 8, 128), F32),
            pltpu.VMEM((8, 128), F32),
            pltpu.VMEM((4, 2, 8, 128), F32),
            pltpu.VMEM((2, 32, 8, 128), F32),
            pltpu.VMEM((4, 2, 32, 8, 128), F32),
            pltpu.VMEM((512, 512), BF16),
            pltpu.VMEM((512, 512), F32),
            pltpu.VMEM((128, 512), F32),
            pltpu.VMEM((128, 512), F32),
            dma((5,)), dma((6,)),
            dma((4, 2)), dma((4, 2)),
            dma((4,)), dma((4,)),
            dma((8,)), dma((8,)),
            dma((8,)), dma((8,)),
            dma((2, 8)), dma((2, 8)),
            dma((8,)), dma((8,)),
            dma((8,)), dma((8,)),
            dma((8,)), dma((8,)),
            dma((4, 2)), dma((4, 2)),
            dma((4, 2, PIECES)), dma((4, 2, PIECES)),
            dma((2, PIECES)), dma((2, PIECES)),
        ],
        compiler_params=pltpu.CompilerParams(
            collective_id=1, has_side_effects=True, vmem_limit_bytes=48 * 2**20
        ),
        name="shampoo_step",
    )(
        block_slot.reshape(1, 128), block_modality.reshape(1, 128), modality_rates,
        grad_parts, left_stat, right_stat, left_root, right_root,
    )
    return update.reshape(128, 4, 512), left_new, right_new


def solution(mesh):
    owner = P("dp", "rep", None)
    return jax.shard_map(
        local,
        mesh=mesh,
        in_specs=(P("rep", None, "dp", None), owner, owner, owner, owner, P(), P(), P()),
        out_specs=(P(None, "dp", None), owner, owner),
        check_vma=False,
    )
```

```python
import functools

import jax
import jax.numpy as jnp
from jax import lax
from jax.experimental import pallas as pl
from jax.experimental.pallas import tpu as pltpu
from jax.sharding import PartitionSpec as P

MESH = pl.DeviceIdType.MESH
DECAY = 0.95
CLIP = 0.5
BLK = 512
F32 = jnp.float32
BF16 = jnp.bfloat16
PIECES = 2
TOP = 4094 << 14


def iota(shape, axis):
    return lax.broadcasted_iota(jnp.int32, shape, axis)


def dot(a, b):
    return jnp.dot(a, b, preferred_element_type=F32)


def dot_nt(a, b):
    return lax.dot_general(a, b, (((1,), (1,)), ((), ())), preferred_element_type=F32)


def halves(value):
    high = value.astype(BF16)
    return high, (value - high.astype(F32)).astype(BF16)


def encode(value, inverse):
    count = (jnp.abs(value) * inverse + 0.5).astype(jnp.int32)
    shift = jnp.maximum(20 - lax.clz(count), 0)
    code = lax.shift_right_logical(count + lax.shift_right_logical(lax.shift_left(jnp.ones_like(shift), shift), 1), shift)
    code = code + lax.shift_left(shift, 11)
    return jnp.where(value < 0, -code, code).astype(jnp.int16)


def decode(code):
    code = code.astype(jnp.int32)
    size = jnp.abs(code)
    shift = jnp.maximum(lax.shift_right_logical(size, 11) - 1, 0)
    count = lax.shift_left(size - lax.shift_left(shift, 11), shift).astype(F32)
    return jnp.where(code < 0, -count, count)


def kernel(
    slot_ref, modality_ref, rates_ref, grad_hbm, lstat_hbm, rstat_hbm, lroot_hbm, rroot_hbm,
    update_hbm, lnew_hbm, rnew_hbm,
    grad, lstat, rstat, rroot, lfull, parts, got, mixed_out, plane, gfull, ghigh, glow,
    rows_out, back, back_plane, mine, meta_out, meta_plane, meta_mid, meta_mine, meta_own, meta_in, half, final, scale_col, spread, update, lnew, rnew,
    in_sem, out_sem, p_send, p_recv, l_send, l_recv, a_send, a_recv, b_send, b_recv,
    g_send, g_recv, h_send, h_recv, c_send, c_recv, d_send, d_recv, cm_send, cm_recv, dm_send, dm_recv, m_send, m_recv,
    f_send, f_recv, r_send, r_recv,
):
    x = lax.axis_index("rep")
    d = lax.axis_index("dp")
    c = lax.rem(d, 2)
    z = lax.rem(lax.div(d, 2), 8)
    y = lax.div(d, 16)
    i = y + c * (z - y)
    j = z + c * (y - z)

    def on_plane(a, b):
        return (16 * (a + c * (b - a)) + 2 * (b + c * (a - b)) + c, x)

    def on_column(to_x, to_c):
        return (d - c + to_c, to_x)

    def send(src, dst, s_sem, r_sem, device):
        return pltpu.make_async_remote_copy(
            src_ref=src, dst_ref=dst, send_sem=s_sem, recv_sem=r_sem, device_id=device, device_id_type=MESH
        )

    order_of = (4, 3, 5, 2, 6, 1, 7)
    column = [(dx, dc) for dx in (2, 1, 3, 0) for dc in (0, 1) if (dx, dc) != (0, 0)]

    barrier = pltpu.get_barrier_semaphore()
    for dx, dc in column:
        pl.semaphore_signal(
            barrier, inc=1, device_id=on_column(lax.rem(x + dx, 4), lax.rem(c + dc, 2)), device_id_type=MESH
        )
    for e in range(1, 8):
        pl.semaphore_signal(barrier, inc=1, device_id=on_plane(lax.rem(i + e, 8), j), device_id_type=MESH)
        pl.semaphore_signal(barrier, inc=1, device_id=on_plane(i, lax.rem(j + e, 8)), device_id_type=MESH)

    loads = [
        pltpu.make_async_copy(grad_hbm.at[0], grad, in_sem.at[0]),
        pltpu.make_async_copy(lroot_hbm.at[0], lfull.at[x], in_sem.at[1]),
        pltpu.make_async_copy(rroot_hbm.at[0], rroot, in_sem.at[2]),
        pltpu.make_async_copy(lstat_hbm.at[0], lstat, in_sem.at[3]),
        pltpu.make_async_copy(rstat_hbm.at[0], rstat, in_sem.at[4]),
    ]
    for load in loads:
        load.start()

    slots = slot_ref[...]
    slots8 = jnp.broadcast_to(slots, (8, 128)).astype(F32).astype(BF16)
    widen = (lax.shift_right_logical(iota((128, 512), 1), 2) == iota((128, 512), 0)).astype(F32).astype(BF16)
    code_row = 4 * dot(slots8, widen)[0:1, :].astype(jnp.int32) + (iota((1, 512), 1) & 3)
    row = iota((512, 128), 0)
    row_first = lax.shift_right_logical(row, 5) & 7
    row_second = lax.shift_right_logical(row, 2) & 7
    row_core = lax.shift_right_logical(row, 8)
    row_slot = jnp.where(row_core == 0, 16 * row_first + 2 * row_second, 16 * row_second + 2 * row_first + 1)
    row_code = 4 * row_slot + (row & 3)
    order = jnp.concatenate(
        [(row_code == code_row[:, 128 * t : 128 * t + 128]).astype(F32).astype(BF16) for t in range(4)], axis=1
    )
    loads[0].wait()
    flat = grad[...].reshape(512, 512)
    for q in range(4):
        ordered = dot(order, flat[:, 128 * q : 128 * q + 128]).astype(BF16)
        parts[q, 0] = ordered[:256]
        parts[q, 1] = ordered[256:]
    pl.semaphore_wait(barrier, len(column) + 14)

    first = []
    for dx, dc in column:
        to_x, to_c = lax.rem(x + dx, 4), lax.rem(c + dc, 2)
        copy = send(parts.at[to_x, to_c], got.at[x, c], p_send.at[dx, dc], p_recv.at[dx, c], on_column(to_x, to_c))
        copy.start()
        first.append(copy)
    loads[1].wait()
    roots = []
    for dx in (2, 1, 3):
        to_x = lax.rem(x + dx, 4)
        copy = send(lfull.at[x], lfull.at[x], l_send.at[dx], l_recv.at[dx], on_column(to_x, c))
        roots.append(copy)
    got[x, c] = parts[x, c]
    for dx, dc in column:
        from_c = lax.rem(c + dc, 2)
        send(parts.at[0, 0], got.at[0, 0], p_send.at[dx, dc], p_recv.at[dx, from_c], on_column(x, c)).wait_recv()
    for copy in roots:
        copy.start()
    sums = []
    for core in range(2):
        total = got[0, core].astype(F32)
        for q in range(1, 4):
            total = total + got[q, core].astype(F32)
        sums.append(total.reshape(32, 8, 128))
    upper = iota((32, 8, 128), 1) < 4
    even = jnp.where(upper, sums[0], pltpu.roll(sums[1], 4, 1))
    odd = jnp.where(upper, pltpu.roll(sums[0], 4, 1), sums[1])
    mixed_out[:, :, 0] = even.reshape(8, 4, 8, 128)
    mixed_out[:, :, 1] = odd.reshape(8, 4, 8, 128)

    stage_a = []
    for e in order_of:
        to = lax.rem(i + e, 8)
        copy = send(
            mixed_out.at[to], plane.at[i], a_send.at[e], a_recv.at[e], on_plane(to, j)
        )
        copy.start()
        stage_a.append(copy)
    plane[i] = mixed_out[i]
    for copy in stage_a:
        copy.wait_recv()
    plane_flat = plane.reshape(8, 8, 8, 128)
    stage_b = []
    for e in range(1, 8):
        to = lax.rem(j + e, 8)

        def cut(src, dst, e=e, to=to):
            return send(src, dst, b_send.at[e], b_recv.at[e], on_plane(i, to))

        @pl.when(c == 0)
        def _(cut=cut, to=to):
            cut(plane_flat.at[:, to], gfull.at[x, :, j]).start()

        @pl.when(c == 1)
        def _(cut=cut, to=to):
            cut(plane_flat.at[:, to], gfull.at[x, j]).start()

        stage_b.append(cut(plane_flat.at[:, 0], gfull.at[x, 0]))

    own = plane_flat[:, j]

    @pl.when(c == 0)
    def _():
        gfull[x, :, j] = own

    @pl.when(c == 1)
    def _():
        gfull[x, j] = own

    right, left = lax.rem(x + 1, 4), lax.rem(x + 3, 4)

    def piece(e, q, s_sem, r_sem, to):
        at = lax.rem(j + 8 - e, 8)

        @pl.when(c == 0)
        def _():
            send(gfull.at[q, :, at], gfull.at[q, :, at], s_sem, r_sem, on_column(to, c)).start()

        @pl.when(c == 1)
        def _():
            send(gfull.at[q, at], gfull.at[q, at], s_sem, r_sem, on_column(to, c)).start()

        return send(gfull.at[q, 0], gfull.at[q, 0], s_sem, r_sem, on_column(to, c))

    rightward, leftward, relayed = [], [], []

    def relay(e):
        if e % 2 == 0:
            rightward[e].wait_recv()
            relayed.append(piece(e, left, h_send.at[e], h_recv.at[e], right))
        else:
            leftward[e].wait_recv()
            relayed.append(piece(e, right, h_send.at[e], h_recv.at[e], left))

    for e in range(8):
        if e > 0:
            stage_b[e - 1].wait_recv()
        rightward.append(piece(e, x, g_send.at[0, e], g_recv.at[0, e], right))
        leftward.append(piece(e, x, g_send.at[1, e], g_recv.at[1, e], left))
        if e >= 2:
            relay(e - 2)

    def take(q):
        high, low = halves(gfull[q].reshape(512, 128))
        at = pl.ds(pl.multiple_of(128 * q, 128), 128)
        ghigh[:, at] = high
        glow[:, at] = low
        other = rroot[:, at]
        return dot_nt(high, other) + dot_nt(low, other)

    loads[2].wait()
    own = gfull[x].reshape(512, 128)
    grad_sq = jnp.sum(own * own)
    relay(6)
    relay(7)
    product = take(x)
    for e in range(8):
        if e % 2 == 1:
            rightward[e].wait_recv()
    product = product + take(left)
    for e in range(8):
        if e % 2 == 0:
            leftward[e].wait_recv()
    product = product + take(right)
    for copy in roots:
        copy.wait_recv()
    for copy in relayed:
        copy.wait_recv()
    product = product + take(lax.rem(x + 2, 4))
    product = jnp.concatenate(halves(product), axis=1)
    prec_sq = jnp.zeros((8, 128), F32)
    peak = jnp.zeros((8, 128), F32)
    for q in range(4):
        rows = dot(lfull[q], product)
        rows = (rows[:, :128] + rows[:, 128:]).reshape(16, 8, 128)
        prec_sq = prec_sq + jnp.sum(rows * rows, axis=0)
        peak = jnp.maximum(peak, jnp.max(jnp.abs(rows), axis=0))
        rows_out[2 * q : 2 * q + 2] = rows.reshape(2, 8, 8, 128)
    peak = jnp.maximum(jnp.max(jnp.max(peak, axis=0, keepdims=True), axis=1, keepdims=True), 1e-30)
    inverse = TOP / peak
    for e in range(8):
        back[e] = encode(rows_out[e], inverse)

    stage_c = []
    for e in order_of:
        to = lax.rem(i + e, 8)

        def cut(src, e=e, to=to):
            return send(src, back_plane.at[i], c_send.at[e], c_recv.at[e], on_plane(to, j))

        @pl.when(c == 0)
        def _(cut=cut, to=to):
            cut(back.at[to]).start()

        @pl.when(c == 1)
        def _(cut=cut, to=to):
            cut(back.at[:, to]).start()

        stage_c.append(cut(back.at[0]))

    prec_sq = jnp.sum(jnp.sum(prec_sq, axis=0, keepdims=True), axis=1, keepdims=True)
    lane = iota((8, 128), 1)
    sub = iota((8, 128), 0)
    meta = jnp.where(lane == j, grad_sq, jnp.where(lane == 32 + j, peak / TOP, jnp.where(lane == 64 + j, prec_sq, 0.0)))
    meta_out[...] = jnp.where(sub == i, meta, 0.0)
    meta_c = []
    for e in order_of:
        copy = send(meta_out, meta_plane.at[i], cm_send.at[e], cm_recv.at[e], on_plane(lax.rem(i + e, 8), j))
        copy.start()
        meta_c.append(copy)
    meta_plane[i] = meta_out[...]

    @pl.when(c == 0)
    def _():
        back_plane[i] = back[i]

    @pl.when(c == 1)
    def _():
        back_plane[i] = back[:, i]

    for copy in stage_c:
        copy.wait_recv()
    stage_d = []
    for e in order_of:
        to = lax.rem(j + e, 8)
        copy = send(back_plane.at[:, to], mine.at[j], d_send.at[e], d_recv.at[e], on_plane(i, to))
        copy.start()
        stage_d.append(copy)
    mine[j] = back_plane[:, j]
    for copy in meta_c:
        copy.wait_recv()
    meta = meta_plane[0]
    for e in range(1, 8):
        meta = meta + meta_plane[e]
    meta_mid[...] = meta
    meta_d = []
    for e in order_of:
        copy = send(meta_mid, meta_mine.at[j], dm_send.at[e], dm_recv.at[e], on_plane(i, lax.rem(j + e, 8)))
        copy.start()
        meta_d.append(copy)
    meta_mine[j] = meta

    loads[3].wait()
    loads[4].wait()
    gain = (1.0 - DECAY) / BLK
    mine_rows = pl.ds(pl.multiple_of(128 * x, 128), 128)
    high, low = ghigh[...], glow[...]
    high_rows, low_rows = ghigh[mine_rows, :], glow[mine_rows, :]
    lnew[...] = DECAY * lstat[...] + gain * (dot_nt(high_rows, high) + (dot_nt(high_rows, low) + dot_nt(low_rows, high)))
    turned = gfull[x].reshape(512, 128).T
    high_turned, low_turned = halves(turned)
    rnew[...] = DECAY * rstat[...] + gain * (dot(high_turned, high) + (dot(high_turned, low) + dot(low_turned, high)))
    out_l = pltpu.make_async_copy(lnew, lnew_hbm.at[0], out_sem.at[0])
    out_r = pltpu.make_async_copy(rnew, rnew_hbm.at[0], out_sem.at[1])
    out_l.start()
    out_r.start()

    block_of_row = lax.shift_right_logical(row, 2)
    lanes = iota((512, 128), 1)
    is_block = lanes == block_of_row
    slot_col = jnp.sum(jnp.where(is_block, slots.astype(F32), 0.0), axis=1, keepdims=True)
    code_col = 4 * slot_col.astype(jnp.int32) + (iota((512, 1), 0) & 3)
    col = iota((1, 512), 1)
    col_second = lax.shift_right_logical(col, 5) & 7
    col_first = lax.shift_right_logical(col, 2) & 7
    col_slot = jnp.where(
        lax.shift_right_logical(col, 8) == 0, 16 * col_first + 2 * col_second, 16 * col_second + 2 * col_first + 1
    )
    col_code = 4 * col_slot + (col & 3)
    spread[...] = (code_col == col_code).astype(F32).astype(BF16)

    for copy in first + roots + stage_a + stage_b + rightward + leftward + relayed + stage_c + meta_c:
        copy.wait_send()
    for copy in stage_d:
        copy.wait_recv()
    tiles = mine[...].astype(jnp.int32).reshape(32, 2, 8, 128)
    a, b = tiles[:, 0], tiles[:, 1]
    half[0] = jnp.where(upper, a, pltpu.roll(b, 4, 1)).astype(jnp.int16)
    half[1] = jnp.where(upper, pltpu.roll(a, 4, 1), b).astype(jnp.int16)
    size = 32 // PIECES
    cuts = [pl.ds(size * p, size) for p in range(PIECES)]
    sends = []
    for p in range(PIECES):
        for dx in (1, 3, 0):
            for dc in range(2):
                if (dx, dc) == (0, 0):
                    continue
                to_x, to_c = lax.rem(x + dx, 4), lax.rem(c + dc, 2)
                copy = send(
                    half.at[to_c, cuts[p]], final.at[x, c, cuts[p]], f_send.at[dx, dc, p], f_recv.at[dx, c, p],
                    on_column(to_x, to_c),
                )
                copy.start()
                sends.append(copy)
    final[x, c] = half[c]
    for copy in meta_d:
        copy.wait_recv()
    meta = meta_mine[0]
    for e in range(1, 8):
        meta = meta + meta_mine[e]
    meta_own[...] = meta
    metas = []
    for dx, dc in column:
        to_x, to_c = lax.rem(x + dx, 4), lax.rem(c + dc, 2)
        copy = send(meta_own, meta_in.at[x, c], m_send.at[dx, dc], m_recv.at[dx, c], on_column(to_x, to_c))
        copy.start()
        metas.append(copy)
    meta_in[x, c] = meta

    def came(dx, core, p):
        send(half.at[0, cuts[p]], final.at[0, 0, cuts[p]], f_send.at[1, 0, p], f_recv.at[dx, core, p], on_column(x, c)).wait_recv()

    for dx, dc in column:
        send(meta_own, meta_in.at[0, 0], m_send.at[dx, dc], m_recv.at[dx, lax.rem(c + dc, 2)], on_column(x, c)).wait_recv()
    grad_b = jnp.zeros((8, 128), F32)
    prec_b = jnp.zeros((8, 128), F32)
    step_b = [jnp.zeros((8, 128), F32) for _ in range(4)]
    for core in range(2):
        known = [meta_in[q, core] for q in range(4)]
        both = known[0] + known[1] + known[2] + known[3]
        for e in range(8):
            slot_here = 16 * sub + 2 * e if core == 0 else 16 * e + 2 * sub + 1
            here = slots == slot_here
            grad_b = grad_b + jnp.where(here, both[:, e : e + 1], 0.0)
            prec_b = prec_b + jnp.where(here, both[:, 64 + e : 65 + e], 0.0)
            for q in range(4):
                step_b[q] = step_b[q] + jnp.where(here, known[q][:, 32 + e : 33 + e], 0.0)
    grad_b = jnp.sum(grad_b, axis=0, keepdims=True)
    prec_b = jnp.sum(prec_b, axis=0, keepdims=True)
    scale = jnp.zeros((1, 128), F32)
    for m in range(2):
        member = modality_ref[...] == m
        total = jnp.sum(jnp.where(member, grad_b, 0.0), axis=1, keepdims=True)
        count = jnp.sum(jnp.where(member, 1.0, 0.0), axis=1, keepdims=True)
        rms = jnp.sqrt(total / (count * (BLK * BLK)) + 1e-6)
        clip = jnp.minimum(1.0, CLIP / rms)
        scale = jnp.where(member, rates_ref[m] * clip, scale)
    scale = scale * jnp.sqrt(grad_b / (prec_b + 1e-6))
    for q in range(4):
        step = scale * jnp.sum(step_b[q], axis=0, keepdims=True)
        scale_col[q] = jnp.broadcast_to(jnp.sum(jnp.where(is_block, step, 0.0), axis=1, keepdims=True), (512, 128))

    outs = []

    def finish(q):
        high, low = halves(decode(final[q]).reshape(512, 128))
        both = dot(spread[...], jnp.concatenate([high, low], axis=1))
        rows = (both[:, :128] + both[:, 128:]) * scale_col[q]
        at = pl.ds(pl.multiple_of(128 * q, 128), 128)
        update[:, at] = rows
        copy = pltpu.make_async_copy(update.at[:, at], update_hbm.at[:, at], out_sem.at[2 + len(outs)])
        copy.start()
        outs.append(copy)

    for p in range(PIECES):
        came(1, 0, p)
        copy = send(final.at[left, 0, cuts[p]], final.at[left, 0, cuts[p]], r_send.at[0, p], r_recv.at[0, p], on_column(right, c))
        copy.start()
        sends.append(copy)
        came(3, 1, p)
        copy = send(final.at[right, 1, cuts[p]], final.at[right, 1, cuts[p]], r_send.at[1, p], r_recv.at[1, p], on_column(left, c))
        copy.start()
        sends.append(copy)
    for p in range(PIECES):
        came(0, 1 - c, p)
    finish(x)
    for p in range(PIECES):
        came(1, 1, p)
    finish(left)
    for p in range(PIECES):
        came(3, 0, p)
    finish(right)
    for p in range(PIECES):
        for way in range(2):
            send(half.at[0, cuts[p]], final.at[0, 0, cuts[p]], r_send.at[way, p], r_recv.at[way, p], on_column(x, c)).wait_recv()
    finish(lax.rem(x + 2, 4))

    for copy in stage_d + meta_d + metas + sends:
        copy.wait_send()
    for copy in outs:
        copy.wait()
    out_l.wait()
    out_r.wait()


def local(grad_parts, left_stat, right_stat, left_root, right_root, block_slot, block_modality, modality_rates):
    vmem = pl.BlockSpec(memory_space=pltpu.VMEM)
    smem = pl.BlockSpec(memory_space=pltpu.SMEM)
    hbm = pl.BlockSpec(memory_space=pltpu.HBM)
    dma = pltpu.SemaphoreType.DMA
    update, left_new, right_new = pl.pallas_call(
        kernel,
        out_shape=(
            jax.ShapeDtypeStruct((512, 512), F32),
            jax.ShapeDtypeStruct(left_stat.shape, F32),
            jax.ShapeDtypeStruct(right_stat.shape, F32),
        ),
        in_specs=[vmem, vmem, smem, hbm, hbm, hbm, hbm, hbm],
        out_specs=(hbm, hbm, hbm),
        scratch_shapes=[
            pltpu.VMEM((128, 4, 512), BF16),
            pltpu.VMEM((128, 512), F32),
            pltpu.VMEM((128, 512), F32),
            pltpu.VMEM((128, 512), BF16),
            pltpu.VMEM((4, 128, 512), BF16),
            pltpu.VMEM((4, 2, 256, 128), BF16),
            pltpu.VMEM((4, 2, 256, 128), BF16),
            pltpu.VMEM((8, 4, 2, 8, 128), F32),
            pltpu.VMEM((8, 4, 2, 8, 128), F32),
            pltpu.VMEM((4, 8, 8, 8, 128), F32),
            pltpu.VMEM((512, 512), BF16),
            pltpu.VMEM((512, 512), BF16),
            pltpu.VMEM((8, 8, 8, 128), F32),
            pltpu.VMEM((8, 8, 8, 128), jnp.int16),
            pltpu.VMEM((8, 8, 8, 128), jnp.int16),
            pltpu.VMEM((8, 8, 8, 128), jnp.int16),
            pltpu.VMEM((8, 128), F32),
            pltpu.VMEM((8, 8, 128), F32),
            pltpu.VMEM((8, 128), F32),
            pltpu.VMEM((8, 8, 128), F32),
            pltpu.VMEM((8, 128), F32),
            pltpu.VMEM((4, 2, 8, 128), F32),
            pltpu.VMEM((2, 32, 8, 128), jnp.int16),
            pltpu.VMEM((4, 2, 32, 8, 128), jnp.int16),
            pltpu.VMEM((4, 512, 128), F32),
            pltpu.VMEM((512, 512), BF16),
            pltpu.VMEM((512, 512), F32),
            pltpu.VMEM((128, 512), F32),
            pltpu.VMEM((128, 512), F32),
            dma((5,)), dma((6,)),
            dma((4, 2)), dma((4, 2)),
            dma((4,)), dma((4,)),
            dma((8,)), dma((8,)),
            dma((8,)), dma((8,)),
            dma((2, 8)), dma((2, 8)),
            dma((8,)), dma((8,)),
            dma((8,)), dma((8,)),
            dma((8,)), dma((8,)),
            dma((8,)), dma((8,)),
            dma((8,)), dma((8,)),
            dma((4, 2)), dma((4, 2)),
            dma((4, 2, PIECES)), dma((4, 2, PIECES)),
            dma((2, PIECES)), dma((2, PIECES)),
        ],
        compiler_params=pltpu.CompilerParams(
            collective_id=1, has_side_effects=True, vmem_limit_bytes=63 * 2**20
        ),
        name="shampoo_step",
    )(
        block_slot.reshape(1, 128), block_modality.reshape(1, 128), modality_rates,
        grad_parts, left_stat, right_stat, left_root, right_root,
    )
    return update.reshape(128, 4, 512), left_new, right_new


def solution(mesh):
    owner = P("dp", "rep", None)
    return jax.shard_map(
        local,
        mesh=mesh,
        in_specs=(P("rep", None, "dp", None), owner, owner, owner, owner, P(), P(), P()),
        out_specs=(P(None, "dp", None), owner, owner),
        check_vma=False,
    )
```

```python
import functools

import jax
import jax.numpy as jnp
from jax import lax
from jax.experimental import pallas as pl
from jax.experimental.pallas import tpu as pltpu
from jax.sharding import PartitionSpec as P

MESH = pl.DeviceIdType.MESH
DECAY = 0.95
CLIP = 0.5
BLK = 512
F32 = jnp.float32
BF16 = jnp.bfloat16
PIECES = 4
TOP = 4094 << 14
LAG = 8


def iota(shape, axis):
    return lax.broadcasted_iota(jnp.int32, shape, axis)


def dot(a, b):
    return jnp.dot(a, b, preferred_element_type=F32)


def dot_nt(a, b):
    return lax.dot_general(a, b, (((1,), (1,)), ((), ())), preferred_element_type=F32)


def halves(value):
    high = value.astype(BF16)
    return high, (value - high.astype(F32)).astype(BF16)


def encode(value, inverse):
    count = (jnp.abs(value) * inverse + 0.5).astype(jnp.int32)
    shift = jnp.maximum(20 - lax.clz(count), 0)
    code = lax.shift_right_logical(count + lax.shift_right_logical(lax.shift_left(jnp.ones_like(shift), shift), 1), shift)
    code = code + lax.shift_left(shift, 11)
    return jnp.where(value < 0, -code, code).astype(jnp.int16)


def decode(code):
    code = code.astype(jnp.int32)
    size = jnp.abs(code)
    shift = jnp.maximum(lax.shift_right_logical(size, 11) - 1, 0)
    count = lax.shift_left(size - lax.shift_left(shift, 11), shift).astype(F32)
    return jnp.where(code < 0, -count, count)


def kernel(
    slot_ref, modality_ref, rates_ref, grad_hbm, lstat_hbm, rstat_hbm, lroot_hbm, rroot_hbm,
    update_hbm, lnew_hbm, rnew_hbm,
    grad, lstat, rstat, rroot, lfull, parts, got, mixed_out, gfull, ghigh, glow,
    rows_out, back, mine, meta_out, meta_plane, meta_mid, meta_mine, meta_own, meta_in, half, final, scale_col, spread, update, lnew, rnew,
    ready, in_sem, out_sem, p_send, p_recv, l_send, l_recv, a_send, a_recv,
    g_send, g_recv, h_send, h_recv, d_send, d_recv, cm_send, cm_recv, dm_send, dm_recv, m_send, m_recv,
    f_send, f_recv,
):
    x = lax.axis_index("rep")
    d = lax.axis_index("dp")
    c = lax.rem(d, 2)
    z = lax.rem(lax.div(d, 2), 8)
    y = lax.div(d, 16)
    def on_plane(to_y, to_z):
        return (16 * to_y + 2 * to_z + c, x)

    def on_column(to_x, to_c):
        return (d - c + to_c, to_x)

    def send(src, dst, s_sem, r_sem, device):
        return pltpu.make_async_remote_copy(
            src_ref=src, dst_ref=dst, send_sem=s_sem, recv_sem=r_sem, device_id=device, device_id_type=MESH
        )

    column = [(dx, dc) for dx in (2, 1, 3, 0) for dc in (0, 1) if (dx, dc) != (0, 0)]

    loads = [
        pltpu.make_async_copy(grad_hbm.at[0], grad, in_sem.at[0]),
        pltpu.make_async_copy(lroot_hbm.at[0], lfull.at[x], in_sem.at[1]),
        pltpu.make_async_copy(rroot_hbm.at[0], rroot, in_sem.at[2]),
        pltpu.make_async_copy(lstat_hbm.at[0], lstat, in_sem.at[3]),
        pltpu.make_async_copy(rstat_hbm.at[0], rstat, in_sem.at[4]),
    ]
    for load in loads:
        load.start()

    barrier = pltpu.get_barrier_semaphore()
    for dx, dc in column:
        pl.semaphore_signal(
            barrier, inc=1, device_id=on_column(lax.rem(x + dx, 4), lax.rem(c + dc, 2)), device_id_type=MESH
        )
    for e in range(1, 8):
        pl.semaphore_signal(barrier, inc=1, device_id=on_plane(lax.rem(y + e, 8), z), device_id_type=MESH)
        pl.semaphore_signal(barrier, inc=1, device_id=on_plane(y, lax.rem(z + e, 8)), device_id_type=MESH)

    slots = slot_ref[...]
    slots8 = jnp.broadcast_to(slots, (8, 128)).astype(F32).astype(BF16)
    widen = (lax.shift_right_logical(iota((128, 512), 1), 2) == iota((128, 512), 0)).astype(F32).astype(BF16)
    code_row = 4 * dot(slots8, widen)[0:1, :].astype(jnp.int32) + (iota((1, 512), 1) & 3)
    row = iota((512, 128), 0)
    row_slot = lax.shift_right_logical(row, 2) & 63
    row_slot = 2 * row_slot + lax.shift_right_logical(row, 8)
    row_code = 4 * row_slot + (row & 3)
    order = jnp.concatenate(
        [(row_code == code_row[:, 128 * t : 128 * t + 128]).astype(F32).astype(BF16) for t in range(4)], axis=1
    )
    loads[0].wait()
    pl.semaphore_wait(barrier, len(column) + 14)

    first = []
    for dx in (2, 1, 3, 0):
        to_x = lax.rem(x + dx, 4)
        flat = grad[:, :, pl.ds(pl.multiple_of(128 * to_x, 128), 128)].reshape(512, 128)
        ordered = dot(order, flat).astype(BF16)
        parts[to_x, 0] = ordered[:256]
        parts[to_x, 1] = ordered[256:]
        for dc in (0, 1):
            if (dx, dc) == (0, 0):
                continue
            to_c = lax.rem(c + dc, 2)
            copy = send(parts.at[to_x, to_c], got.at[x, c], p_send.at[dx, dc], p_recv.at[dx, c], on_column(to_x, to_c))
            copy.start()
            first.append(copy)
    loads[1].wait()
    roots = []
    for dx in (2, 1, 3):
        to_x = lax.rem(x + dx, 4)
        copy = send(lfull.at[x], lfull.at[x], l_send.at[dx], l_recv.at[dx], on_column(to_x, c))
        roots.append(copy)
    for e in range(1, 8):
        pl.semaphore_signal(ready, inc=1, device_id=on_plane(lax.rem(y + e, 8), z), device_id_type=MESH)
    got[x, c] = parts[x, c]
    for dx, dc in column:
        from_c = lax.rem(c + dc, 2)
        send(parts.at[0, 0], got.at[0, 0], p_send.at[dx, dc], p_recv.at[dx, from_c], on_column(x, c)).wait_recv()
    for copy in roots:
        copy.start()
    sums = []
    for core in range(2):
        total = got[0, core].astype(F32)
        for q in range(1, 4):
            total = total + got[q, core].astype(F32)
        sums.append(total.reshape(32, 8, 128))
    upper = iota((32, 8, 128), 1) < 4
    even = jnp.where(upper, sums[0], pltpu.roll(sums[1], 4, 1))
    odd = jnp.where(upper, pltpu.roll(sums[0], 4, 1), sums[1])
    mixed_out[:, :, 0] = even.reshape(8, 4, 8, 128)
    mixed_out[:, :, 1] = odd.reshape(8, 4, 8, 128)
    pl.semaphore_wait(ready, 7)

    rows_of = mixed_out.reshape(8, 8, 8, 128)
    right, left = lax.rem(x + 1, 4), lax.rem(x + 3, 4)

    def scatter(src, dst, g, s_sem, r_sem):
        to_y = lax.rem(y + 3 * g, 8)

        def one(e, carry):
            to_z = lax.rem(z + e, 8)
            send(src.at[to_y, to_z], dst, s_sem, r_sem, on_plane(to_y, to_z)).start()
            return carry

        lax.fori_loop(1 if g == 0 else 0, 8, one, 0)

    def tiles_of(ref, g):
        return ref.at[0, 1:8] if g == 0 else ref.at[0]

    def piece(g, q, s_sem, r_sem, to):
        at = lax.rem(y + 8 - 3 * g % 8, 8)
        copy = send(gfull.at[q, at], gfull.at[q, at], s_sem, r_sem, on_column(to, c))
        copy.start()
        return copy

    rightward, leftward, relayed = [], [], []

    def forward(g):
        came = tiles_of(gfull.at[0], g)
        send(came, came, a_send.at[g], a_recv.at[g], on_column(x, c)).wait_recv()
        rightward.append(piece(g, x, g_send.at[0, g], g_recv.at[0, g], right))
        leftward.append(piece(g, x, g_send.at[1, g], g_recv.at[1, g], left))

    def relay(g):
        if g % 2 == 0:
            rightward[g].wait_recv()
            relayed.append(piece(g, left, h_send.at[g], h_recv.at[g], right))
        else:
            leftward[g].wait_recv()
            relayed.append(piece(g, right, h_send.at[g], h_recv.at[g], left))

    gfull[x, y, z] = rows_of[y, z]
    for g in range(8):
        scatter(rows_of, gfull.at[x, y, z], g, a_send.at[g], a_recv.at[g])
        if g >= LAG:
            forward(g - LAG)
        if g >= 2 * LAG:
            relay(g - 2 * LAG)
    for g in range(8, 8 + 2 * LAG):
        if g < 8 + LAG:
            forward(g - LAG)
        if 2 * LAG <= g:
            relay(g - 2 * LAG)

    def take(q):
        high, low = halves(gfull[q].reshape(512, 128))
        at = pl.ds(pl.multiple_of(128 * q, 128), 128)
        ghigh[:, at] = high
        glow[:, at] = low
        other = rroot[:, at]
        return dot_nt(high, other) + dot_nt(low, other)

    loads[2].wait()
    own = gfull[x].reshape(512, 128)
    grad_sq = jnp.sum(own * own)
    product = take(x)
    for e in range(8):
        if e % 2 == 1:
            rightward[e].wait_recv()
    product = product + take(left)
    for e in range(8):
        if e % 2 == 0:
            leftward[e].wait_recv()
    product = product + take(right)
    for copy in roots:
        copy.wait_recv()
    for copy in relayed:
        copy.wait_recv()
    product = product + take(lax.rem(x + 2, 4))
    product = jnp.concatenate(halves(product), axis=1)
    prec_sq = jnp.zeros((8, 128), F32)
    peak = jnp.zeros((8, 128), F32)
    for q in range(4):
        rows = dot(lfull[q], product)
        rows = (rows[:, :128] + rows[:, 128:]).reshape(16, 8, 128)
        prec_sq = prec_sq + jnp.sum(rows * rows, axis=0)
        peak = jnp.maximum(peak, jnp.max(jnp.abs(rows), axis=0))
        rows_out[2 * q : 2 * q + 2] = rows.reshape(2, 8, 8, 128)
    peak = jnp.maximum(jnp.max(jnp.max(peak, axis=0, keepdims=True), axis=1, keepdims=True), 1e-30)
    inverse = TOP / peak
    for e in range(8):
        back[e] = encode(rows_out[e], inverse)

    prec_sq = jnp.sum(jnp.sum(prec_sq, axis=0, keepdims=True), axis=1, keepdims=True)
    lane = iota((8, 128), 1)
    sub = iota((8, 128), 0)
    meta = jnp.where(lane == z, grad_sq, jnp.where(lane == 32 + z, peak / TOP, jnp.where(lane == 64 + z, prec_sq, 0.0)))
    meta_out[...] = jnp.where(sub == y, meta, 0.0)
    meta_plane[y] = meta_out[...]

    mine[0, z] = back[y, z]
    for g in range(4):
        scatter(back, mine.at[g, z], g, d_send.at[g], d_recv.at[g])
    meta_c = []
    for e in range(1, 8):
        copy = send(meta_out, meta_plane.at[y], cm_send.at[e], cm_recv.at[e], on_plane(lax.rem(y + e, 8), z))
        copy.start()
        meta_c.append(copy)
    for g in range(4, 8):
        scatter(back, mine.at[g, z], g, d_send.at[g], d_recv.at[g])

    upper = iota((8, 8, 128), 1) < 4
    sends = []

    def hand_on(p):
        for g in (2 * p, 2 * p + 1):
            came = tiles_of(mine, g)
            send(came, came, d_send.at[g], d_recv.at[g], on_column(x, c)).wait_recv()
        tiles = mine[2 * p : 2 * p + 2].astype(jnp.int32).reshape(8, 2, 8, 128)
        a, b = tiles[:, 0], tiles[:, 1]
        half[0, p] = jnp.where(upper, a, pltpu.roll(b, 4, 1)).astype(jnp.int16)
        half[1, p] = jnp.where(upper, pltpu.roll(a, 4, 1), b).astype(jnp.int16)
        for dx, dc in column:
            to_x, to_c = lax.rem(x + dx, 4), lax.rem(c + dc, 2)
            copy = send(half.at[to_c, p], final.at[x, c, p], f_send.at[dx, dc, p], f_recv.at[dx, c, p], on_column(to_x, to_c))
            copy.start()
            sends.append(copy)
        final[x, c, p] = half[c, p]

    def came_on(dx, core, p):
        send(half.at[0, p], final.at[0, 0, p], f_send.at[1, 0, p], f_recv.at[dx, core, p], on_column(x, c)).wait_recv()

    for copy in meta_c:
        copy.wait_recv()
    meta = meta_plane[0]
    for e in range(1, 8):
        meta = meta + meta_plane[e]
    meta_mid[...] = meta
    meta_d = []
    for e in range(1, 8):
        copy = send(meta_mid, meta_mine.at[z], dm_send.at[e], dm_recv.at[e], on_plane(y, lax.rem(z + e, 8)))
        copy.start()
        meta_d.append(copy)
    meta_mine[z] = meta
    hand_on(0)
    hand_on(1)
    hand_on(2)
    for copy in meta_d:
        copy.wait_recv()
    meta = meta_mine[0]
    for e in range(1, 8):
        meta = meta + meta_mine[e]
    meta_own[...] = meta
    metas = []
    for dx, dc in column:
        to_x, to_c = lax.rem(x + dx, 4), lax.rem(c + dc, 2)
        copy = send(meta_own, meta_in.at[x, c], m_send.at[dx, dc], m_recv.at[dx, c], on_column(to_x, to_c))
        copy.start()
        metas.append(copy)
    meta_in[x, c] = meta
    hand_on(3)

    loads[3].wait()
    loads[4].wait()
    gain = (1.0 - DECAY) / BLK
    mine_rows = pl.ds(pl.multiple_of(128 * x, 128), 128)
    high, low = ghigh[...], glow[...]
    high_rows, low_rows = ghigh[mine_rows, :], glow[mine_rows, :]
    lnew[...] = DECAY * lstat[...] + gain * (dot_nt(high_rows, high) + (dot_nt(high_rows, low) + dot_nt(low_rows, high)))
    turned = gfull[x].reshape(512, 128).T
    high_turned, low_turned = halves(turned)
    rnew[...] = DECAY * rstat[...] + gain * (dot(high_turned, high) + (dot(high_turned, low) + dot(low_turned, high)))
    out_l = pltpu.make_async_copy(lnew, lnew_hbm.at[0], out_sem.at[0])
    out_r = pltpu.make_async_copy(rnew, rnew_hbm.at[0], out_sem.at[1])
    out_l.start()
    out_r.start()

    block_of_row = lax.shift_right_logical(row, 2)
    lanes = iota((512, 128), 1)
    is_block = lanes == block_of_row
    slot_col = jnp.sum(jnp.where(is_block, slots.astype(F32), 0.0), axis=1, keepdims=True)
    code_col = 4 * slot_col.astype(jnp.int32) + (iota((512, 1), 0) & 3)
    col = iota((1, 512), 1)
    col_y = (y + 8 - 3 * (lax.shift_right_logical(col, 5) & 7) % 8) & 7
    col_z = lax.shift_right_logical(col, 2) & 7
    col_slot = 16 * col_y + 2 * col_z + lax.shift_right_logical(col, 8)
    col_code = 4 * col_slot + (col & 3)
    spread[...] = (code_col == col_code).astype(F32).astype(BF16)

    for dx, dc in column:
        send(meta_own, meta_in.at[0, 0], m_send.at[dx, dc], m_recv.at[dx, lax.rem(c + dc, 2)], on_column(x, c)).wait_recv()
    grad_b = jnp.zeros((8, 128), F32)
    prec_b = jnp.zeros((8, 128), F32)
    step_b = [jnp.zeros((8, 128), F32) for _ in range(4)]
    for core in range(2):
        known = [meta_in[q, core] for q in range(4)]
        both = known[0] + known[1] + known[2] + known[3]
        for e in range(8):
            here = slots == 16 * sub + 2 * e + core
            grad_b = grad_b + jnp.where(here, both[:, e : e + 1], 0.0)
            prec_b = prec_b + jnp.where(here, both[:, 64 + e : 65 + e], 0.0)
            for q in range(4):
                step_b[q] = step_b[q] + jnp.where(here, known[q][:, 32 + e : 33 + e], 0.0)
    grad_b = jnp.sum(grad_b, axis=0, keepdims=True)
    prec_b = jnp.sum(prec_b, axis=0, keepdims=True)
    scale = jnp.zeros((1, 128), F32)
    for m in range(2):
        member = modality_ref[...] == m
        total = jnp.sum(jnp.where(member, grad_b, 0.0), axis=1, keepdims=True)
        count = jnp.sum(jnp.where(member, 1.0, 0.0), axis=1, keepdims=True)
        rms = jnp.sqrt(total / (count * (BLK * BLK)) + 1e-6)
        clip = jnp.minimum(1.0, CLIP / rms)
        scale = jnp.where(member, rates_ref[m] * clip, scale)
    scale = scale * jnp.sqrt(grad_b / (prec_b + 1e-6))
    for q in range(4):
        step = scale * jnp.sum(step_b[q], axis=0, keepdims=True)
        scale_col[q] = jnp.broadcast_to(jnp.sum(jnp.where(is_block, step, 0.0), axis=1, keepdims=True), (512, 128))

    outs = []

    def finish(q):
        high, low = halves(decode(final[q]).reshape(512, 128))
        both = dot(spread[...], jnp.concatenate([high, low], axis=1))
        rows = (both[:, :128] + both[:, 128:]) * scale_col[q]
        at = pl.ds(pl.multiple_of(128 * q, 128), 128)
        update[:, :, at] = rows.reshape(128, 4, 128)
        copy = pltpu.make_async_copy(update.at[:, :, at], update_hbm.at[:, :, at], out_sem.at[2 + len(outs)])
        copy.start()
        outs.append(copy)

    for p in range(PIECES):
        came_on(0, 1 - c, p)
    finish(x)
    for dx in (1, 3, 2):
        for p in range(PIECES):
            for core in range(2):
                came_on(dx, core, p)
        finish(lax.rem(x + 4 - dx, 4))

    for copy in first + roots + rightward + leftward + relayed + meta_c:
        copy.wait_send()
    for g in range(8):
        for ref, sem in ((rows_of, a_send), (back, d_send)):
            gone = tiles_of(ref, g)
            send(gone, gone, sem.at[g], sem.at[g], on_column(x, c)).wait_send()
    for copy in meta_d + metas + sends:
        copy.wait_send()
    for copy in outs:
        copy.wait()
    out_l.wait()
    out_r.wait()


def place(update, left_new, right_new, update_out, left_out, right_out, held, held_left, held_right, in_sem, out_sem):
    parts = [(update, held, update_out, slice(32 * p, 32 * p + 32)) for p in range(4)]
    parts += [(left_new, held_left, left_out, slice(0, 1)), (right_new, held_right, right_out, slice(0, 1))]
    loads, stores = [], []
    for n, (source, buffer, target, at) in enumerate(parts):
        loads.append(pltpu.make_async_copy(source.at[at], buffer.at[at], in_sem.at[n]))
        stores.append(pltpu.make_async_copy(buffer.at[at], target.at[at], out_sem.at[n]))
    for load in loads:
        load.start()
    for load, store in zip(loads, stores):
        load.wait()
        store.start()
    for store in stores:
        store.wait()


def local(grad_parts, left_stat, right_stat, left_root, right_root, block_slot, block_modality, modality_rates):
    vmem = pl.BlockSpec(memory_space=pltpu.VMEM)
    smem = pl.BlockSpec(memory_space=pltpu.SMEM)
    hbm = pl.BlockSpec(memory_space=pltpu.HBM)
    dma = pltpu.SemaphoreType.DMA
    update, left_new, right_new = pl.pallas_call(
        kernel,
        out_shape=(
            jax.ShapeDtypeStruct((128, 4, 512), F32),
            jax.ShapeDtypeStruct(left_stat.shape, F32),
            jax.ShapeDtypeStruct(right_stat.shape, F32),
        ),
        in_specs=[vmem, vmem, smem, hbm, hbm, hbm, hbm, hbm],
        out_specs=(hbm, hbm, hbm),
        scratch_shapes=[
            pltpu.VMEM((128, 4, 512), BF16),
            pltpu.VMEM((128, 512), F32),
            pltpu.VMEM((128, 512), F32),
            pltpu.VMEM((128, 512), BF16),
            pltpu.VMEM((4, 128, 512), BF16),
            pltpu.VMEM((4, 2, 256, 128), BF16),
            pltpu.VMEM((4, 2, 256, 128), BF16),
            pltpu.VMEM((8, 4, 2, 8, 128), F32),
            pltpu.VMEM((4, 8, 8, 8, 128), F32),
            pltpu.VMEM((512, 512), BF16),
            pltpu.VMEM((512, 512), BF16),
            pltpu.VMEM((8, 8, 8, 128), F32),
            pltpu.VMEM((8, 8, 8, 128), jnp.int16),
            pltpu.VMEM((8, 8, 8, 128), jnp.int16),
            pltpu.VMEM((8, 128), F32),
            pltpu.VMEM((8, 8, 128), F32),
            pltpu.VMEM((8, 128), F32),
            pltpu.VMEM((8, 8, 128), F32),
            pltpu.VMEM((8, 128), F32),
            pltpu.VMEM((4, 2, 8, 128), F32),
            pltpu.VMEM((2, 4, 8, 8, 128), jnp.int16),
            pltpu.VMEM((4, 2, 4, 8, 8, 128), jnp.int16),
            pltpu.VMEM((4, 512, 128), F32),
            pltpu.VMEM((512, 512), BF16),
            pltpu.VMEM((128, 4, 512), F32),
            pltpu.VMEM((128, 512), F32),
            pltpu.VMEM((128, 512), F32),
            pltpu.SemaphoreType.REGULAR,
            dma((5,)), dma((6,)),
            dma((4, 2)), dma((4, 2)),
            dma((4,)), dma((4,)),
            dma((8,)), dma((8,)),
            dma((2, 8)), dma((2, 8)),
            dma((8,)), dma((8,)),
            dma((8,)), dma((8,)),
            dma((8,)), dma((8,)),
            dma((8,)), dma((8,)),
            dma((4, 2)), dma((4, 2)),
            dma((4, 2, PIECES)), dma((4, 2, PIECES)),
        ],
        compiler_params=pltpu.CompilerParams(
            collective_id=1, has_side_effects=True, vmem_limit_bytes=63 * 2**20
        ),
        name="shampoo_step",
    )(
        block_slot.reshape(1, 128), block_modality.reshape(1, 128), modality_rates,
        grad_parts, left_stat, right_stat, left_root, right_root,
    )
    results = (update, left_new, right_new)
    return pl.pallas_call(
        place,
        out_shape=tuple(jax.ShapeDtypeStruct(result.shape, F32) for result in results),
        in_specs=[hbm] * 3,
        out_specs=(hbm,) * 3,
        scratch_shapes=[pltpu.VMEM(result.shape, F32) for result in results] + [dma((6,)), dma((6,))],
        compiler_params=pltpu.CompilerParams(vmem_limit_bytes=63 * 2**20),
        name="place_results",
    )(*results)


def solution(mesh):
    owner = P("dp", "rep", None)
    return jax.shard_map(
        local,
        mesh=mesh,
        in_specs=(P("rep", None, "dp", None), owner, owner, owner, owner, P(), P(), P()),
        out_specs=(P(None, "dp", None), owner, owner),
        check_vma=False,
    )
```

```python
import functools

import jax
import jax.numpy as jnp
from jax import lax
from jax.experimental import pallas as pl
from jax.experimental.pallas import tpu as pltpu
from jax.sharding import PartitionSpec as P

MESH = pl.DeviceIdType.MESH
DECAY = 0.95
CLIP = 0.5
BLK = 512
F32 = jnp.float32
BF16 = jnp.bfloat16
PIECES = 4
TOP = 4094 << 14


def iota(shape, axis):
    return lax.broadcasted_iota(jnp.int32, shape, axis)


def dot(a, b):
    return jnp.dot(a, b, preferred_element_type=F32)


def dot_nt(a, b):
    return lax.dot_general(a, b, (((1,), (1,)), ((), ())), preferred_element_type=F32)


def halves(value):
    high = value.astype(BF16)
    return high, (value - high.astype(F32)).astype(BF16)


def encode(value, inverse):
    count = (jnp.abs(value) * inverse + 0.5).astype(jnp.int32)
    shift = jnp.maximum(20 - lax.clz(count), 0)
    code = lax.shift_right_logical(count + lax.shift_right_logical(lax.shift_left(jnp.ones_like(shift), shift), 1), shift)
    code = code + lax.shift_left(shift, 11)
    return jnp.where(value < 0, -code, code).astype(jnp.int16)


def decode(code):
    code = code.astype(jnp.int32)
    size = jnp.abs(code)
    shift = jnp.maximum(lax.shift_right_logical(size, 11) - 1, 0)
    count = lax.shift_left(size - lax.shift_left(shift, 11), shift).astype(F32)
    return jnp.where(code < 0, -count, count)


def kernel(
    slot_ref, modality_ref, rates_ref, grad_hbm, lstat_hbm, rstat_hbm, lroot_hbm, rroot_hbm,
    update_hbm, lnew_hbm, rnew_hbm,
    grad, lstat, rstat, rroot, lfull, parts, got, mixed_out, gfull, gcode, gstep, ghigh, glow,
    rows_out, back, mine, meta_out, meta_plane, meta_mid, meta_mine, meta_own, meta_in, half, final, scale_col, spread, update, lnew, rnew,
    ready, in_sem, out_sem, p_send, p_recv, l_send, l_recv, a_send, a_recv,
    g_send, g_recv, s_send, s_recv, d_send, d_recv, cm_send, cm_recv, dm_send, dm_recv, m_send, m_recv,
    f_send, f_recv,
):
    x = lax.axis_index("rep")
    d = lax.axis_index("dp")
    c = lax.rem(d, 2)
    z = lax.rem(lax.div(d, 2), 8)
    y = lax.div(d, 16)
    def on_plane(to_y, to_z):
        return (16 * to_y + 2 * to_z + c, x)

    def on_column(to_x, to_c):
        return (d - c + to_c, to_x)

    def send(src, dst, s_sem, r_sem, device):
        return pltpu.make_async_remote_copy(
            src_ref=src, dst_ref=dst, send_sem=s_sem, recv_sem=r_sem, device_id=device, device_id_type=MESH
        )

    column = [(dx, dc) for dx in (2, 1, 3, 0) for dc in (0, 1) if (dx, dc) != (0, 0)]

    loads = [
        pltpu.make_async_copy(grad_hbm.at[0], grad, in_sem.at[0]),
        pltpu.make_async_copy(lroot_hbm.at[0], lfull.at[x], in_sem.at[1]),
        pltpu.make_async_copy(rroot_hbm.at[0], rroot, in_sem.at[2]),
        pltpu.make_async_copy(lstat_hbm.at[0], lstat, in_sem.at[3]),
        pltpu.make_async_copy(rstat_hbm.at[0], rstat, in_sem.at[4]),
    ]
    loads[0].start()

    barrier = pltpu.get_barrier_semaphore()
    for dx, dc in column:
        pl.semaphore_signal(
            barrier, inc=1, device_id=on_column(lax.rem(x + dx, 4), lax.rem(c + dc, 2)), device_id_type=MESH
        )
    for e in range(1, 8):
        pl.semaphore_signal(barrier, inc=1, device_id=on_plane(lax.rem(y + e, 8), z), device_id_type=MESH)
        pl.semaphore_signal(barrier, inc=1, device_id=on_plane(y, lax.rem(z + e, 8)), device_id_type=MESH)

    for load in loads[1:]:
        load.start()

    slots = slot_ref[...]
    slots8 = jnp.broadcast_to(slots, (8, 128)).astype(F32).astype(BF16)
    widen = (lax.shift_right_logical(iota((128, 512), 1), 2) == iota((128, 512), 0)).astype(F32).astype(BF16)
    code_row = 4 * dot(slots8, widen)[0:1, :].astype(jnp.int32) + (iota((1, 512), 1) & 3)
    row = iota((512, 128), 0)
    row_y = (y + lax.shift_right_logical(row, 5)) & 7
    row_z = lax.shift_right_logical(row, 2) & 7
    row_slot = 16 * row_y + 2 * row_z + lax.shift_right_logical(row, 8)
    row_code = 4 * row_slot + (row & 3)
    order = jnp.concatenate(
        [(row_code == code_row[:, 128 * t : 128 * t + 128]).astype(F32).astype(BF16) for t in range(4)], axis=1
    )
    loads[0].wait()
    pl.semaphore_wait(barrier, len(column) + 14)

    first = []
    for dx in (2, 1, 3, 0):
        to_x = lax.rem(x + dx, 4)
        flat = grad[:, :, pl.ds(pl.multiple_of(128 * to_x, 128), 128)].reshape(512, 128)
        parts[to_x] = dot(order, flat).astype(BF16).reshape(2, 2, 128, 128)
        for h in range(2):
            for dc in (0, 1):
                if (dx, dc) == (0, 0):
                    continue
                to_c = lax.rem(c + dc, 2)
                copy = send(
                    parts.at[to_x, to_c, h], got.at[x, c, h], p_send.at[dx, dc, h], p_recv.at[dx, c, h], on_column(to_x, to_c)
                )
                copy.start()
                first.append(copy)
    for e in range(1, 8):
        pl.semaphore_signal(ready, inc=1, device_id=on_plane(lax.rem(y + e, 8), z), device_id_type=MESH)
    got[x, c] = parts[x, c]
    loads[1].wait()
    right, left = lax.rem(x + 1, 4), lax.rem(x + 3, 4)

    def root(n, q, rows, to):
        at = lfull.at[q, rows]
        return send(at, at, l_send.at[n], l_recv.at[n], on_column(to, c))

    every, low_half, high_half = pl.ds(0, 128), pl.ds(0, 64), pl.ds(64, 64)
    roots = [root(0, x, every, right), root(1, x, every, left), root(2, left, low_half, right), root(3, right, high_half, left)]
    upper = iota((16, 8, 128), 1) < 4

    def add_up(h):
        for dx, dc in column:
            from_c = lax.rem(c + dc, 2)
            send(parts.at[0, 0, h], got.at[0, 0, h], p_send.at[dx, dc, h], p_recv.at[dx, from_c, h], on_column(x, c)).wait_recv()
        sums = []
        for core in range(2):
            total = got[0, core, h].astype(F32)
            for q in range(1, 4):
                total = total + got[q, core, h].astype(F32)
            sums.append(total.reshape(16, 8, 128))
        even = jnp.where(upper, sums[0], pltpu.roll(sums[1], 4, 1))
        odd = jnp.where(upper, pltpu.roll(sums[0], 4, 1), sums[1])
        mixed_out[4 * h : 4 * h + 4, :, 0] = even.reshape(4, 4, 8, 128)
        mixed_out[4 * h : 4 * h + 4, :, 1] = odd.reshape(4, 4, 8, 128)

    rows_of = mixed_out.reshape(8, 8, 8, 128)

    def scatter(src, dst, g, s_sem, r_sem):
        to_y = lax.rem(y + g, 8)

        def one(e, carry):
            to_z = lax.rem(z + e, 8)
            send(src(to_y).at[to_z], dst, s_sem, r_sem, on_plane(to_y, to_z)).start()
            return carry

        lax.fori_loop(1 if g == 0 else 0, 8, one, 0)

    def tiles_of(ref, g):
        return ref.at[0, 1:8] if g == 0 else ref.at[0]

    lane = iota((8, 128), 1)
    sub = iota((8, 128), 0)
    quarters = []

    def forward(g, steps):
        came = tiles_of(gfull, g)
        send(came, came, a_send.at[g], a_recv.at[g], on_column(x, c)).wait_recv()
        at = lax.rem(y + 8 - g, 8)
        value = gfull[at]
        top = jnp.maximum(jnp.max(jnp.abs(value), axis=2, keepdims=True), 1e-30)
        scaled = value * (32767.0 / top)
        gcode[x, at] = (scaled + jnp.where(scaled < 0, -0.5, 0.5)).astype(jnp.int32).astype(jnp.int16)
        for dx in (2, 1, 3):
            to = lax.rem(x + dx, 4)
            copy = send(gcode.at[x, at], gcode.at[x, at], g_send.at[dx, g], g_recv.at[dx, g], on_column(to, c))
            copy.start()
            quarters.append(copy)
        for t in range(8):
            steps = jnp.where(lane == 8 * at + t, top[t] / 32767.0, steps)
        return steps

    def first_scatter(g):
        scatter(lambda to_y: rows_of.at[g], gfull.at[y, z], g, a_send.at[g], a_recv.at[g])

    add_up(0)
    gfull[y, z] = rows_of[0, z]
    pl.semaphore_wait(ready, 7)
    for g in range(4):
        first_scatter(g)
    add_up(1)
    roots[0].start()
    roots[1].start()
    for g in range(4, 8):
        first_scatter(g)
    steps = jnp.zeros((8, 128), F32)
    for g in range(8):
        steps = forward(g, steps)
        if g == 4:
            roots[0].wait_recv()
            roots[2].start()
            roots[1].wait_recv()
            roots[3].start()
    gstep[x] = steps
    for dx in (2, 1, 3):
        copy = send(gstep.at[x], gstep.at[x], s_send.at[dx], s_recv.at[dx], on_column(lax.rem(x + dx, 4), c))
        copy.start()
        quarters.append(copy)

    def take(q, block):
        high, low = halves(block)
        at = pl.ds(pl.multiple_of(128 * q, 128), 128)
        ghigh[:, at] = high
        glow[:, at] = low
        other = rroot[:, at]
        return dot_nt(high, other) + dot_nt(low, other)

    def other_quarter(dx):
        q = lax.rem(x + 4 - dx, 4)
        for g in range(8):
            send(gcode.at[0, 0], gcode.at[0, 0], g_send.at[dx, g], g_recv.at[dx, g], on_column(x, c)).wait_recv()
        send(gstep.at[0], gstep.at[0], s_send.at[dx], s_recv.at[dx], on_column(x, c)).wait_recv()
        code = gcode[q].astype(jnp.int32).astype(F32).reshape(64, 8, 128)
        step = gstep[q]
        return take(q, jnp.concatenate([code[k] * step[:, k : k + 1] for k in range(64)], axis=0))

    loads[2].wait()
    own = gfull[...].reshape(512, 128)
    grad_sq = jnp.sum(own * own)
    product = take(x, own)
    product = product + other_quarter(1)
    product = product + other_quarter(3)
    product = product + other_quarter(2)
    roots[2].wait_recv()
    roots[3].wait_recv()
    product = jnp.concatenate(halves(product), axis=1)
    prec_sq = jnp.zeros((8, 128), F32)
    peak = jnp.zeros((8, 128), F32)
    for q in range(4):
        rows = dot(lfull[q], product)
        rows = (rows[:, :128] + rows[:, 128:]).reshape(16, 8, 128)
        prec_sq = prec_sq + jnp.sum(rows * rows, axis=0)
        peak = jnp.maximum(peak, jnp.max(jnp.abs(rows), axis=0))
        rows_out[2 * q : 2 * q + 2] = rows.reshape(2, 8, 8, 128)
    peak = jnp.maximum(jnp.max(jnp.max(peak, axis=0, keepdims=True), axis=1, keepdims=True), 1e-30)
    inverse = TOP / peak
    for e in range(8):
        back[e] = encode(rows_out[e], inverse)

    prec_sq = jnp.sum(jnp.sum(prec_sq, axis=0, keepdims=True), axis=1, keepdims=True)
    meta = jnp.where(lane == z, grad_sq, jnp.where(lane == 32 + z, peak / TOP, jnp.where(lane == 64 + z, prec_sq, 0.0)))
    meta_out[...] = jnp.where(sub == y, meta, 0.0)
    meta_plane[y] = meta_out[...]

    mine[0, z] = back[y, z]
    for g in range(4):
        scatter(lambda to_y: back.at[to_y], mine.at[g, z], g, d_send.at[g], d_recv.at[g])
    meta_c = []
    for e in range(1, 8):
        copy = send(meta_out, meta_plane.at[y], cm_send.at[e], cm_recv.at[e], on_plane(lax.rem(y + e, 8), z))
        copy.start()
        meta_c.append(copy)
    for g in range(4, 8):
        scatter(lambda to_y: back.at[to_y], mine.at[g, z], g, d_send.at[g], d_recv.at[g])

    upper = iota((8, 8, 128), 1) < 4
    sends = []

    def hand_on(p):
        for g in (2 * p, 2 * p + 1):
            came = tiles_of(mine, g)
            send(came, came, d_send.at[g], d_recv.at[g], on_column(x, c)).wait_recv()
        tiles = mine[2 * p : 2 * p + 2].astype(jnp.int32).reshape(8, 2, 8, 128)
        a, b = tiles[:, 0], tiles[:, 1]
        half[0, p] = jnp.where(upper, a, pltpu.roll(b, 4, 1)).astype(jnp.int16)
        half[1, p] = jnp.where(upper, pltpu.roll(a, 4, 1), b).astype(jnp.int16)
        for dx, dc in column:
            to_x, to_c = lax.rem(x + dx, 4), lax.rem(c + dc, 2)
            copy = send(half.at[to_c, p], final.at[x, c, p], f_send.at[dx, dc, p], f_recv.at[dx, c, p], on_column(to_x, to_c))
            copy.start()
            sends.append(copy)
        final[x, c, p] = half[c, p]

    def came_on(dx, core, p):
        send(half.at[0, p], final.at[0, 0, p], f_send.at[1, 0, p], f_recv.at[dx, core, p], on_column(x, c)).wait_recv()

    for copy in meta_c:
        copy.wait_recv()
    meta = meta_plane[0]
    for e in range(1, 8):
        meta = meta + meta_plane[e]
    meta_mid[...] = meta
    meta_d = []
    for e in range(1, 8):
        copy = send(meta_mid, meta_mine.at[z], dm_send.at[e], dm_recv.at[e], on_plane(y, lax.rem(z + e, 8)))
        copy.start()
        meta_d.append(copy)
    meta_mine[z] = meta
    hand_on(0)
    hand_on(1)
    hand_on(2)
    for copy in meta_d:
        copy.wait_recv()
    meta = meta_mine[0]
    for e in range(1, 8):
        meta = meta + meta_mine[e]
    meta_own[...] = meta
    metas = []
    for dx, dc in column:
        to_x, to_c = lax.rem(x + dx, 4), lax.rem(c + dc, 2)
        copy = send(meta_own, meta_in.at[x, c], m_send.at[dx, dc], m_recv.at[dx, c], on_column(to_x, to_c))
        copy.start()
        metas.append(copy)
    meta_in[x, c] = meta
    hand_on(3)

    loads[3].wait()
    loads[4].wait()
    gain = (1.0 - DECAY) / BLK
    mine_rows = pl.ds(pl.multiple_of(128 * x, 128), 128)
    high, low = ghigh[...], glow[...]
    high_rows, low_rows = ghigh[mine_rows, :], glow[mine_rows, :]
    lnew[...] = DECAY * lstat[...] + gain * (dot_nt(high_rows, high) + (dot_nt(high_rows, low) + dot_nt(low_rows, high)))
    turned = gfull[...].reshape(512, 128).T
    high_turned, low_turned = halves(turned)
    rnew[...] = DECAY * rstat[...] + gain * (dot(high_turned, high) + (dot(high_turned, low) + dot(low_turned, high)))
    out_l = pltpu.make_async_copy(lnew, lnew_hbm.at[0], out_sem.at[0])
    out_r = pltpu.make_async_copy(rnew, rnew_hbm.at[0], out_sem.at[1])
    out_l.start()
    out_r.start()

    block_of_row = lax.shift_right_logical(row, 2)
    lanes = iota((512, 128), 1)
    is_block = lanes == block_of_row
    slot_col = jnp.sum(jnp.where(is_block, slots.astype(F32), 0.0), axis=1, keepdims=True)
    code_col = 4 * slot_col.astype(jnp.int32) + (iota((512, 1), 0) & 3)
    col = iota((1, 512), 1)
    col_y = (y + 8 - (lax.shift_right_logical(col, 5) & 7)) & 7
    col_z = lax.shift_right_logical(col, 2) & 7
    col_slot = 16 * col_y + 2 * col_z + lax.shift_right_logical(col, 8)
    col_code = 4 * col_slot + (col & 3)
    spread[...] = (code_col == col_code).astype(F32).astype(BF16)

    for dx, dc in column:
        send(meta_own, meta_in.at[0, 0], m_send.at[dx, dc], m_recv.at[dx, lax.rem(c + dc, 2)], on_column(x, c)).wait_recv()
    grad_b = jnp.zeros((8, 128), F32)
    prec_b = jnp.zeros((8, 128), F32)
    step_b = [jnp.zeros((8, 128), F32) for _ in range(4)]
    for core in range(2):
        known = [meta_in[q, core] for q in range(4)]
        both = known[0] + known[1] + known[2] + known[3]
        for e in range(8):
            here = slots == 16 * sub + 2 * e + core
            grad_b = grad_b + jnp.where(here, both[:, e : e + 1], 0.0)
            prec_b = prec_b + jnp.where(here, both[:, 64 + e : 65 + e], 0.0)
            for q in range(4):
                step_b[q] = step_b[q] + jnp.where(here, known[q][:, 32 + e : 33 + e], 0.0)
    grad_b = jnp.sum(grad_b, axis=0, keepdims=True)
    prec_b = jnp.sum(prec_b, axis=0, keepdims=True)
    scale = jnp.zeros((1, 128), F32)
    for m in range(2):
        member = modality_ref[...] == m
        total = jnp.sum(jnp.where(member, grad_b, 0.0), axis=1, keepdims=True)
        count = jnp.sum(jnp.where(member, 1.0, 0.0), axis=1, keepdims=True)
        rms = jnp.sqrt(total / (count * (BLK * BLK)) + 1e-6)
        clip = jnp.minimum(1.0, CLIP / rms)
        scale = jnp.where(member, rates_ref[m] * clip, scale)
    scale = scale * jnp.sqrt(grad_b / (prec_b + 1e-6))
    for q in range(4):
        step = scale * jnp.sum(step_b[q], axis=0, keepdims=True)
        scale_col[q] = jnp.broadcast_to(jnp.sum(jnp.where(is_block, step, 0.0), axis=1, keepdims=True), (512, 128))

    outs = []

    def finish(q):
        high, low = halves(decode(final[q]).reshape(512, 128))
        both = dot(spread[...], jnp.concatenate([high, low], axis=1))
        rows = (both[:, :128] + both[:, 128:]) * scale_col[q]
        at = pl.ds(pl.multiple_of(128 * q, 128), 128)
        update[:, :, at] = rows.reshape(128, 4, 128)
        copy = pltpu.make_async_copy(update.at[:, :, at], update_hbm.at[:, :, at], out_sem.at[2 + len(outs)])
        copy.start()
        outs.append(copy)

    for p in range(PIECES):
        came_on(0, 1 - c, p)
    finish(x)
    for dx in (1, 3, 2):
        for p in range(PIECES):
            for core in range(2):
                came_on(dx, core, p)
        finish(lax.rem(x + 4 - dx, 4))

    for copy in first + roots + quarters + meta_c:
        copy.wait_send()
    for g in range(8):
        for ref, sem in ((rows_of, a_send), (back, d_send)):
            gone = tiles_of(ref, g)
            send(gone, gone, sem.at[g], sem.at[g], on_column(x, c)).wait_send()
    for copy in meta_d + metas + sends:
        copy.wait_send()
    for copy in outs:
        copy.wait()
    out_l.wait()
    out_r.wait()


def place(update, left_new, right_new, update_out, left_out, right_out, held, held_left, held_right, in_sem, out_sem):
    parts = [(update, held, update_out, slice(32 * p, 32 * p + 32)) for p in range(4)]
    parts += [(left_new, held_left, left_out, slice(0, 1)), (right_new, held_right, right_out, slice(0, 1))]
    loads, stores = [], []
    for n, (source, buffer, target, at) in enumerate(parts):
        loads.append(pltpu.make_async_copy(source.at[at], buffer.at[at], in_sem.at[n]))
        stores.append(pltpu.make_async_copy(buffer.at[at], target.at[at], out_sem.at[n]))
    for load in loads:
        load.start()
    for load, store in zip(loads, stores):
        load.wait()
        store.start()
    for store in stores:
        store.wait()


def local(grad_parts, left_stat, right_stat, left_root, right_root, block_slot, block_modality, modality_rates):
    vmem = pl.BlockSpec(memory_space=pltpu.VMEM)
    smem = pl.BlockSpec(memory_space=pltpu.SMEM)
    hbm = pl.BlockSpec(memory_space=pltpu.HBM)
    dma = pltpu.SemaphoreType.DMA
    update, left_new, right_new = pl.pallas_call(
        kernel,
        out_shape=(
            jax.ShapeDtypeStruct((128, 4, 512), F32),
            jax.ShapeDtypeStruct(left_stat.shape, F32),
            jax.ShapeDtypeStruct(right_stat.shape, F32),
        ),
        in_specs=[vmem, vmem, smem, hbm, hbm, hbm, hbm, hbm],
        out_specs=(hbm, hbm, hbm),
        scratch_shapes=[
            pltpu.VMEM((128, 4, 512), BF16),
            pltpu.VMEM((128, 512), F32),
            pltpu.VMEM((128, 512), F32),
            pltpu.VMEM((128, 512), BF16),
            pltpu.VMEM((4, 128, 512), BF16),
            pltpu.VMEM((4, 2, 2, 128, 128), BF16),
            pltpu.VMEM((4, 2, 2, 128, 128), BF16),
            pltpu.VMEM((8, 4, 2, 8, 128), F32),
            pltpu.VMEM((8, 8, 8, 128), F32),
            pltpu.VMEM((4, 8, 8, 8, 128), jnp.int16),
            pltpu.VMEM((4, 8, 128), F32),
            pltpu.VMEM((512, 512), BF16),
            pltpu.VMEM((512, 512), BF16),
            pltpu.VMEM((8, 8, 8, 128), F32),
            pltpu.VMEM((8, 8, 8, 128), jnp.int16),
            pltpu.VMEM((8, 8, 8, 128), jnp.int16),
            pltpu.VMEM((8, 128), F32),
            pltpu.VMEM((8, 8, 128), F32),
            pltpu.VMEM((8, 128), F32),
            pltpu.VMEM((8, 8, 128), F32),
            pltpu.VMEM((8, 128), F32),
            pltpu.VMEM((4, 2, 8, 128), F32),
            pltpu.VMEM((2, 4, 8, 8, 128), jnp.int16),
            pltpu.VMEM((4, 2, 4, 8, 8, 128), jnp.int16),
            pltpu.VMEM((4, 512, 128), F32),
            pltpu.VMEM((512, 512), BF16),
            pltpu.VMEM((128, 4, 512), F32),
            pltpu.VMEM((128, 512), F32),
            pltpu.VMEM((128, 512), F32),
            pltpu.SemaphoreType.REGULAR,
            dma((5,)), dma((6,)),
            dma((4, 2, 2)), dma((4, 2, 2)),
            dma((4,)), dma((4,)),
            dma((8,)), dma((8,)),
            dma((4, 8)), dma((4, 8)),
            dma((4,)), dma((4,)),
            dma((8,)), dma((8,)),
            dma((8,)), dma((8,)),
            dma((8,)), dma((8,)),
            dma((4, 2)), dma((4, 2)),
            dma((4, 2, PIECES)), dma((4, 2, PIECES)),
        ],
        compiler_params=pltpu.CompilerParams(
            collective_id=1, has_side_effects=True, vmem_limit_bytes=63 * 2**20
        ),
        name="shampoo_step",
    )(
        block_slot.reshape(1, 128), block_modality.reshape(1, 128), modality_rates,
        grad_parts, left_stat, right_stat, left_root, right_root,
    )
    results = (update, left_new, right_new)
    return pl.pallas_call(
        place,
        out_shape=tuple(jax.ShapeDtypeStruct(result.shape, F32) for result in results),
        in_specs=[hbm] * 3,
        out_specs=(hbm,) * 3,
        scratch_shapes=[pltpu.VMEM(result.shape, F32) for result in results] + [dma((6,)), dma((6,))],
        compiler_params=pltpu.CompilerParams(vmem_limit_bytes=63 * 2**20),
        name="place_results",
    )(*results)


def solution(mesh):
    owner = P("dp", "rep", None)
    return jax.shard_map(
        local,
        mesh=mesh,
        in_specs=(P("rep", None, "dp", None), owner, owner, owner, owner, P(), P(), P()),
        out_specs=(P(None, "dp", None), owner, owner),
        check_vma=False,
    )
```

```python
import functools

import jax
import jax.numpy as jnp
from jax import lax
from jax.experimental import pallas as pl
from jax.experimental.pallas import tpu as pltpu
from jax.sharding import PartitionSpec as P

MESH = pl.DeviceIdType.MESH
DECAY = 0.95
CLIP = 0.5
BLK = 512
F32 = jnp.float32
BF16 = jnp.bfloat16
PIECES = 4
TOP = 4094 << 14


def iota(shape, axis):
    return lax.broadcasted_iota(jnp.int32, shape, axis)


def dot(a, b):
    return jnp.dot(a, b, preferred_element_type=F32)


def dot_nt(a, b):
    return lax.dot_general(a, b, (((1,), (1,)), ((), ())), preferred_element_type=F32)


def halves(value):
    high = value.astype(BF16)
    return high, (value - high.astype(F32)).astype(BF16)


def encode(value, inverse):
    count = (jnp.abs(value) * inverse + 0.5).astype(jnp.int32)
    shift = jnp.maximum(20 - lax.clz(count), 0)
    code = lax.shift_right_logical(count + lax.shift_right_logical(lax.shift_left(jnp.ones_like(shift), shift), 1), shift)
    code = code + lax.shift_left(shift, 11)
    return jnp.where(value < 0, -code, code).astype(jnp.int16)


def decode(code):
    code = code.astype(jnp.int32)
    size = jnp.abs(code)
    shift = jnp.maximum(lax.shift_right_logical(size, 11) - 1, 0)
    count = lax.shift_left(size - lax.shift_left(shift, 11), shift).astype(F32)
    return jnp.where(code < 0, -count, count)


def kernel(
    slot_ref, modality_ref, rates_ref, grad_hbm, lstat_hbm, rstat_hbm, lroot_hbm, rroot_hbm,
    update_hbm, lnew_hbm, rnew_hbm,
    grad, lstat, rstat, rroot, lfull, parts, got, mixed_out, gfull, gcode, gstep, ghigh, glow,
    rows_out, back, mine, meta_out, meta_plane, meta_mid, meta_mine, meta_own, meta_in, half, final, scale_col, spread, update, lnew, rnew,
    ready, in_sem, out_sem, p_send, p_recv, l_send, l_recv, a_send, a_recv,
    g_send, g_recv, s_send, s_recv, d_send, d_recv, cm_send, cm_recv, dm_send, dm_recv, m_send, m_recv,
    f_send, f_recv,
):
    x = lax.axis_index("rep")
    d = lax.axis_index("dp")
    c = lax.rem(d, 2)
    z = lax.rem(lax.div(d, 2), 8)
    y = lax.div(d, 16)
    def on_plane(to_y, to_z):
        return (16 * to_y + 2 * to_z + c, x)

    def on_column(to_x, to_c):
        return (d - c + to_c, to_x)

    def send(src, dst, s_sem, r_sem, device):
        return pltpu.make_async_remote_copy(
            src_ref=src, dst_ref=dst, send_sem=s_sem, recv_sem=r_sem, device_id=device, device_id_type=MESH
        )

    column = [(dx, dc) for dx in (2, 1, 3, 0) for dc in (0, 1) if (dx, dc) != (0, 0)]

    loads = [
        pltpu.make_async_copy(grad_hbm.at[0], grad, in_sem.at[0]),
        pltpu.make_async_copy(lroot_hbm.at[0], lfull.at[x], in_sem.at[1]),
        pltpu.make_async_copy(rroot_hbm.at[0], rroot, in_sem.at[2]),
        pltpu.make_async_copy(lstat_hbm.at[0], lstat, in_sem.at[3]),
        pltpu.make_async_copy(rstat_hbm.at[0], rstat, in_sem.at[4]),
    ]
    loads[0].start()

    barrier = pltpu.get_barrier_semaphore()
    for dx, dc in column:
        pl.semaphore_signal(
            barrier, inc=1, device_id=on_column(lax.rem(x + dx, 4), lax.rem(c + dc, 2)), device_id_type=MESH
        )
    for e in range(1, 8):
        pl.semaphore_signal(barrier, inc=1, device_id=on_plane(lax.rem(y + e, 8), z), device_id_type=MESH)
        pl.semaphore_signal(barrier, inc=1, device_id=on_plane(y, lax.rem(z + e, 8)), device_id_type=MESH)

    for load in loads[1:]:
        load.start()

    slots = slot_ref[...]
    slots8 = jnp.broadcast_to(slots, (8, 128)).astype(F32).astype(BF16)
    widen = (lax.shift_right_logical(iota((128, 512), 1), 2) == iota((128, 512), 0)).astype(F32).astype(BF16)
    code_row = 4 * dot(slots8, widen)[0:1, :].astype(jnp.int32) + (iota((1, 512), 1) & 3)
    row = iota((512, 128), 0)
    row_y = (y + lax.shift_right_logical(row, 5)) & 7
    row_z = lax.shift_right_logical(row, 2) & 7
    row_slot = 16 * row_y + 2 * row_z + lax.shift_right_logical(row, 8)
    row_code = 4 * row_slot + (row & 3)
    order = jnp.concatenate(
        [(row_code == code_row[:, 128 * t : 128 * t + 128]).astype(F32).astype(BF16) for t in range(4)], axis=1
    )
    loads[0].wait()
    for dx in (2, 1, 3, 0):
        to_x = lax.rem(x + dx, 4)
        flat = grad[:, :, pl.ds(pl.multiple_of(128 * to_x, 128), 128)].reshape(512, 128)
        parts[to_x] = dot(order, flat).astype(BF16).reshape(2, 2, 128, 128)

    pl.semaphore_wait(barrier, len(column) + 14)
    first = []
    for h in range(2):
        for dx, dc in column:
            to_x, to_c = lax.rem(x + dx, 4), lax.rem(c + dc, 2)
            copy = send(
                parts.at[to_x, to_c, h], got.at[x, c, h], p_send.at[dx, dc, h], p_recv.at[dx, c, h], on_column(to_x, to_c)
            )
            copy.start()
            first.append(copy)
    for e in range(1, 8):
        pl.semaphore_signal(ready, inc=1, device_id=on_plane(lax.rem(y + e, 8), z), device_id_type=MESH)
    got[x, c] = parts[x, c]
    loads[1].wait()
    right, left = lax.rem(x + 1, 4), lax.rem(x + 3, 4)

    def root(n, q, rows, to):
        at = lfull.at[q, rows]
        return send(at, at, l_send.at[n], l_recv.at[n], on_column(to, c))

    every, low_half, high_half = pl.ds(0, 128), pl.ds(0, 64), pl.ds(64, 64)
    roots = [root(0, x, every, right), root(1, x, every, left), root(2, left, low_half, right), root(3, right, high_half, left)]
    upper = iota((16, 8, 128), 1) < 4

    def add_up(h):
        for dx, dc in column:
            from_c = lax.rem(c + dc, 2)
            send(parts.at[0, 0, h], got.at[0, 0, h], p_send.at[dx, dc, h], p_recv.at[dx, from_c, h], on_column(x, c)).wait_recv()
        sums = []
        for core in range(2):
            total = got[0, core, h].astype(F32)
            for q in range(1, 4):
                total = total + got[q, core, h].astype(F32)
            sums.append(total.reshape(16, 8, 128))
        even = jnp.where(upper, sums[0], pltpu.roll(sums[1], 4, 1))
        odd = jnp.where(upper, pltpu.roll(sums[0], 4, 1), sums[1])
        mixed_out[4 * h : 4 * h + 4, :, 0] = even.reshape(4, 4, 8, 128)
        mixed_out[4 * h : 4 * h + 4, :, 1] = odd.reshape(4, 4, 8, 128)

    rows_of = mixed_out.reshape(8, 8, 8, 128)

    def scatter(src, dst, g, s_sem, r_sem):
        to_y = lax.rem(y + g, 8)

        def one(e, carry):
            to_z = lax.rem(z + e, 8)
            send(src(to_y).at[to_z], dst, s_sem, r_sem, on_plane(to_y, to_z)).start()
            return carry

        lax.fori_loop(1 if g == 0 else 0, 8, one, 0)

    def tiles_of(ref, g):
        return ref.at[0, 1:8] if g == 0 else ref.at[0]

    lane = iota((8, 128), 1)
    sub = iota((8, 128), 0)
    quarters = []

    def forward(g, steps):
        came = tiles_of(gfull, g)
        send(came, came, a_send.at[g], a_recv.at[g], on_column(x, c)).wait_recv()
        at = lax.rem(y + 8 - g, 8)
        value = gfull[at]
        top = jnp.maximum(jnp.max(jnp.abs(value), axis=2, keepdims=True), 1e-30)
        scaled = value * (32767.0 / top)
        gcode[x, at] = (scaled + jnp.where(scaled < 0, -0.5, 0.5)).astype(jnp.int32).astype(jnp.int16)
        for dx in (2, 1, 3):
            to = lax.rem(x + dx, 4)
            copy = send(gcode.at[x, at], gcode.at[x, at], g_send.at[dx, g], g_recv.at[dx, g], on_column(to, c))
            copy.start()
            quarters.append(copy)
        for t in range(8):
            steps = jnp.where(lane == 8 * at + t, top[t] / 32767.0, steps)
        return steps

    def first_scatter(g):
        scatter(lambda to_y: rows_of.at[g], gfull.at[y, z], g, a_send.at[g], a_recv.at[g])

    add_up(0)
    gfull[y, z] = rows_of[0, z]
    pl.semaphore_wait(ready, 7)
    for g in range(4):
        first_scatter(g)
    add_up(1)
    roots[0].start()
    roots[1].start()
    for g in range(4, 8):
        first_scatter(g)
    steps = jnp.zeros((8, 128), F32)
    for g in range(8):
        steps = forward(g, steps)
        if g == 4:
            roots[0].wait_recv()
            roots[2].start()
            roots[1].wait_recv()
            roots[3].start()
    gstep[x] = steps
    for dx in (2, 1, 3):
        copy = send(gstep.at[x], gstep.at[x], s_send.at[dx], s_recv.at[dx], on_column(lax.rem(x + dx, 4), c))
        copy.start()
        quarters.append(copy)

    def take(q, block):
        high, low = halves(block)
        at = pl.ds(pl.multiple_of(128 * q, 128), 128)
        ghigh[:, at] = high
        glow[:, at] = low
        other = rroot[:, at]
        return dot_nt(high, other) + dot_nt(low, other)

    def other_quarter(dx):
        q = lax.rem(x + 4 - dx, 4)
        for g in range(8):
            send(gcode.at[0, 0], gcode.at[0, 0], g_send.at[dx, g], g_recv.at[dx, g], on_column(x, c)).wait_recv()
        send(gstep.at[0], gstep.at[0], s_send.at[dx], s_recv.at[dx], on_column(x, c)).wait_recv()
        code = gcode[q].astype(jnp.int32).astype(F32).reshape(64, 8, 128)
        step = gstep[q]
        return take(q, jnp.concatenate([code[k] * step[:, k : k + 1] for k in range(64)], axis=0))

    loads[2].wait()
    own = gfull[...].reshape(512, 128)
    grad_sq = jnp.sum(own * own)
    product = take(x, own)
    product = product + other_quarter(1)
    product = product + other_quarter(3)
    product = product + other_quarter(2)
    roots[2].wait_recv()
    roots[3].wait_recv()
    product = jnp.concatenate(halves(product), axis=1)
    prec_sq = jnp.zeros((8, 128), F32)
    peak = jnp.zeros((8, 128), F32)
    for q in range(4):
        rows = dot(lfull[q], product)
        rows = (rows[:, :128] + rows[:, 128:]).reshape(16, 8, 128)
        prec_sq = prec_sq + jnp.sum(rows * rows, axis=0)
        peak = jnp.maximum(peak, jnp.max(jnp.abs(rows), axis=0))
        rows_out[2 * q : 2 * q + 2] = rows.reshape(2, 8, 8, 128)
    peak = jnp.maximum(jnp.max(jnp.max(peak, axis=0, keepdims=True), axis=1, keepdims=True), 1e-30)
    inverse = TOP / peak
    for e in range(8):
        back[e] = encode(rows_out[e], inverse)

    prec_sq = jnp.sum(jnp.sum(prec_sq, axis=0, keepdims=True), axis=1, keepdims=True)
    meta = jnp.where(lane == z, grad_sq, jnp.where(lane == 32 + z, peak / TOP, jnp.where(lane == 64 + z, prec_sq, 0.0)))
    meta_out[...] = jnp.where(sub == y, meta, 0.0)
    meta_plane[y] = meta_out[...]

    mine[0, z] = back[y, z]
    for g in range(4):
        scatter(lambda to_y: back.at[to_y], mine.at[g, z], g, d_send.at[g], d_recv.at[g])
    meta_c = []
    for e in range(1, 8):
        copy = send(meta_out, meta_plane.at[y], cm_send.at[e], cm_recv.at[e], on_plane(lax.rem(y + e, 8), z))
        copy.start()
        meta_c.append(copy)
    upper = iota((8, 8, 128), 1) < 4
    sends = []

    def hand_on(p):
        for g in (2 * p, 2 * p + 1):
            came = tiles_of(mine, g)
            send(came, came, d_send.at[g], d_recv.at[g], on_column(x, c)).wait_recv()
        tiles = mine[2 * p : 2 * p + 2].astype(jnp.int32).reshape(8, 2, 8, 128)
        a, b = tiles[:, 0], tiles[:, 1]
        half[0, p] = jnp.where(upper, a, pltpu.roll(b, 4, 1)).astype(jnp.int16)
        half[1, p] = jnp.where(upper, pltpu.roll(a, 4, 1), b).astype(jnp.int16)
        for dx, dc in column:
            to_x, to_c = lax.rem(x + dx, 4), lax.rem(c + dc, 2)
            copy = send(half.at[to_c, p], final.at[x, c, p], f_send.at[dx, dc, p], f_recv.at[dx, c, p], on_column(to_x, to_c))
            copy.start()
            sends.append(copy)
        final[x, c, p] = half[c, p]

    def came_on(dx, core, p):
        send(half.at[0, p], final.at[0, 0, p], f_send.at[1, 0, p], f_recv.at[dx, core, p], on_column(x, c)).wait_recv()

    def back_scatter(g):
        scatter(lambda to_y: back.at[to_y], mine.at[g, z], g, d_send.at[g], d_recv.at[g])

    back_scatter(4)
    back_scatter(5)
    hand_on(0)
    back_scatter(6)
    back_scatter(7)
    hand_on(1)
    for copy in meta_c:
        copy.wait_recv()
    meta = meta_plane[0]
    for e in range(1, 8):
        meta = meta + meta_plane[e]
    meta_mid[...] = meta
    meta_d = []
    for e in range(1, 8):
        copy = send(meta_mid, meta_mine.at[z], dm_send.at[e], dm_recv.at[e], on_plane(y, lax.rem(z + e, 8)))
        copy.start()
        meta_d.append(copy)
    meta_mine[z] = meta
    hand_on(2)
    hand_on(3)
    for copy in meta_d:
        copy.wait_recv()
    meta = meta_mine[0]
    for e in range(1, 8):
        meta = meta + meta_mine[e]
    meta_own[...] = meta
    metas = []
    for dx, dc in column:
        to_x, to_c = lax.rem(x + dx, 4), lax.rem(c + dc, 2)
        copy = send(meta_own, meta_in.at[x, c], m_send.at[dx, dc], m_recv.at[dx, c], on_column(to_x, to_c))
        copy.start()
        metas.append(copy)
    meta_in[x, c] = meta

    loads[3].wait()
    loads[4].wait()
    gain = (1.0 - DECAY) / BLK
    mine_rows = pl.ds(pl.multiple_of(128 * x, 128), 128)
    high, low = ghigh[...], glow[...]
    high_rows, low_rows = ghigh[mine_rows, :], glow[mine_rows, :]
    lnew[...] = DECAY * lstat[...] + gain * (dot_nt(high_rows, high) + (dot_nt(high_rows, low) + dot_nt(low_rows, high)))
    turned = gfull[...].reshape(512, 128).T
    high_turned, low_turned = halves(turned)
    rnew[...] = DECAY * rstat[...] + gain * (dot(high_turned, high) + (dot(high_turned, low) + dot(low_turned, high)))
    out_l = pltpu.make_async_copy(lnew, lnew_hbm.at[0], out_sem.at[0])
    out_r = pltpu.make_async_copy(rnew, rnew_hbm.at[0], out_sem.at[1])
    out_l.start()
    out_r.start()

    block_of_row = lax.shift_right_logical(row, 2)
    lanes = iota((512, 128), 1)
    is_block = lanes == block_of_row
    slot_col = jnp.sum(jnp.where(is_block, slots.astype(F32), 0.0), axis=1, keepdims=True)
    code_col = 4 * slot_col.astype(jnp.int32) + (iota((512, 1), 0) & 3)
    col = iota((1, 512), 1)
    col_y = (y + 8 - (lax.shift_right_logical(col, 5) & 7)) & 7
    col_z = lax.shift_right_logical(col, 2) & 7
    col_slot = 16 * col_y + 2 * col_z + lax.shift_right_logical(col, 8)
    col_code = 4 * col_slot + (col & 3)
    spread[...] = (code_col == col_code).astype(F32).astype(BF16)

    for dx, dc in column:
        send(meta_own, meta_in.at[0, 0], m_send.at[dx, dc], m_recv.at[dx, lax.rem(c + dc, 2)], on_column(x, c)).wait_recv()
    grad_b = jnp.zeros((8, 128), F32)
    prec_b = jnp.zeros((8, 128), F32)
    step_b = [jnp.zeros((8, 128), F32) for _ in range(4)]
    for core in range(2):
        known = [meta_in[q, core] for q in range(4)]
        both = known[0] + known[1] + known[2] + known[3]
        for e in range(8):
            here = slots == 16 * sub + 2 * e + core
            grad_b = grad_b + jnp.where(here, both[:, e : e + 1], 0.0)
            prec_b = prec_b + jnp.where(here, both[:, 64 + e : 65 + e], 0.0)
            for q in range(4):
                step_b[q] = step_b[q] + jnp.where(here, known[q][:, 32 + e : 33 + e], 0.0)
    grad_b = jnp.sum(grad_b, axis=0, keepdims=True)
    prec_b = jnp.sum(prec_b, axis=0, keepdims=True)
    scale = jnp.zeros((1, 128), F32)
    for m in range(2):
        member = modality_ref[...] == m
        total = jnp.sum(jnp.where(member, grad_b, 0.0), axis=1, keepdims=True)
        count = jnp.sum(jnp.where(member, 1.0, 0.0), axis=1, keepdims=True)
        rms = jnp.sqrt(total / (count * (BLK * BLK)) + 1e-6)
        clip = jnp.minimum(1.0, CLIP / rms)
        scale = jnp.where(member, rates_ref[m] * clip, scale)
    scale = scale * jnp.sqrt(grad_b / (prec_b + 1e-6))
    for q in range(4):
        step = scale * jnp.sum(step_b[q], axis=0, keepdims=True)
        scale_col[q] = jnp.broadcast_to(jnp.sum(jnp.where(is_block, step, 0.0), axis=1, keepdims=True), (512, 128))

    outs = []

    def finish(q):
        high, low = halves(decode(final[q]).reshape(512, 128))
        both = dot(spread[...], jnp.concatenate([high, low], axis=1))
        rows = (both[:, :128] + both[:, 128:]) * scale_col[q]
        at = pl.ds(pl.multiple_of(128 * q, 128), 128)
        update[:, :, at] = rows.reshape(128, 4, 128)
        copy = pltpu.make_async_copy(update.at[:, :, at], update_hbm.at[:, :, at], out_sem.at[2 + len(outs)])
        copy.start()
        outs.append(copy)

    for p in range(PIECES):
        came_on(0, 1 - c, p)
    finish(x)
    for dx in (1, 3, 2):
        for p in range(PIECES):
            for core in range(2):
                came_on(dx, core, p)
        finish(lax.rem(x + 4 - dx, 4))

    for copy in first + roots + quarters + meta_c:
        copy.wait_send()
    for g in range(8):
        for ref, sem in ((rows_of, a_send), (back, d_send)):
            gone = tiles_of(ref, g)
            send(gone, gone, sem.at[g], sem.at[g], on_column(x, c)).wait_send()
    for copy in meta_d + metas + sends:
        copy.wait_send()
    for copy in outs:
        copy.wait()
    out_l.wait()
    out_r.wait()


def place(update, left_new, right_new, update_out, left_out, right_out, sems):
    copies = [pltpu.make_async_copy(update.at[32 * p : 32 * p + 32], update_out.at[32 * p : 32 * p + 32], sems.at[p]) for p in range(4)]
    copies += [pltpu.make_async_copy(left_new, left_out, sems.at[4]), pltpu.make_async_copy(right_new, right_out, sems.at[5])]
    for copy in copies:
        copy.start()
    for copy in copies:
        copy.wait()


def local(grad_parts, left_stat, right_stat, left_root, right_root, block_slot, block_modality, modality_rates):
    vmem = pl.BlockSpec(memory_space=pltpu.VMEM)
    smem = pl.BlockSpec(memory_space=pltpu.SMEM)
    hbm = pl.BlockSpec(memory_space=pltpu.HBM)
    dma = pltpu.SemaphoreType.DMA
    update, left_new, right_new = pl.pallas_call(
        kernel,
        out_shape=(
            jax.ShapeDtypeStruct((128, 4, 512), F32),
            jax.ShapeDtypeStruct(left_stat.shape, F32),
            jax.ShapeDtypeStruct(right_stat.shape, F32),
        ),
        in_specs=[vmem, vmem, smem, hbm, hbm, hbm, hbm, hbm],
        out_specs=(hbm, hbm, hbm),
        scratch_shapes=[
            pltpu.VMEM((128, 4, 512), BF16),
            pltpu.VMEM((128, 512), F32),
            pltpu.VMEM((128, 512), F32),
            pltpu.VMEM((128, 512), BF16),
            pltpu.VMEM((4, 128, 512), BF16),
            pltpu.VMEM((4, 2, 2, 128, 128), BF16),
            pltpu.VMEM((4, 2, 2, 128, 128), BF16),
            pltpu.VMEM((8, 4, 2, 8, 128), F32),
            pltpu.VMEM((8, 8, 8, 128), F32),
            pltpu.VMEM((4, 8, 8, 8, 128), jnp.int16),
            pltpu.VMEM((4, 8, 128), F32),
            pltpu.VMEM((512, 512), BF16),
            pltpu.VMEM((512, 512), BF16),
            pltpu.VMEM((8, 8, 8, 128), F32),
            pltpu.VMEM((8, 8, 8, 128), jnp.int16),
            pltpu.VMEM((8, 8, 8, 128), jnp.int16),
            pltpu.VMEM((8, 128), F32),
            pltpu.VMEM((8, 8, 128), F32),
            pltpu.VMEM((8, 128), F32),
            pltpu.VMEM((8, 8, 128), F32),
            pltpu.VMEM((8, 128), F32),
            pltpu.VMEM((4, 2, 8, 128), F32),
            pltpu.VMEM((2, 4, 8, 8, 128), jnp.int16),
            pltpu.VMEM((4, 2, 4, 8, 8, 128), jnp.int16),
            pltpu.VMEM((4, 512, 128), F32),
            pltpu.VMEM((512, 512), BF16),
            pltpu.VMEM((128, 4, 512), F32),
            pltpu.VMEM((128, 512), F32),
            pltpu.VMEM((128, 512), F32),
            pltpu.SemaphoreType.REGULAR,
            dma((5,)), dma((6,)),
            dma((4, 2, 2)), dma((4, 2, 2)),
            dma((4,)), dma((4,)),
            dma((8,)), dma((8,)),
            dma((4, 8)), dma((4, 8)),
            dma((4,)), dma((4,)),
            dma((8,)), dma((8,)),
            dma((8,)), dma((8,)),
            dma((8,)), dma((8,)),
            dma((4, 2)), dma((4, 2)),
            dma((4, 2, PIECES)), dma((4, 2, PIECES)),
        ],
        compiler_params=pltpu.CompilerParams(
            collective_id=1, has_side_effects=True, vmem_limit_bytes=24 * 2**20
        ),
        name="shampoo_step",
    )(
        *(
            pltpu.with_memory_space_constraint(array, pltpu.HBM)
            for array in (
                block_slot.reshape(1, 128), block_modality.reshape(1, 128), modality_rates,
                grad_parts, left_stat, right_stat, left_root, right_root,
            )
        ),
    )
    results = (update, left_new, right_new)
    return pl.pallas_call(
        place,
        out_shape=tuple(jax.ShapeDtypeStruct(result.shape, F32) for result in results),
        in_specs=[hbm] * 3,
        out_specs=(hbm,) * 3,
        scratch_shapes=[dma((6,))],
        compiler_params=pltpu.CompilerParams(vmem_limit_bytes=4 * 2**20),
        name="place_results",
    )(*results)


def solution(mesh):
    owner = P("dp", "rep", None)
    return jax.shard_map(
        local,
        mesh=mesh,
        in_specs=(P("rep", None, "dp", None), owner, owner, owner, owner, P(), P(), P()),
        out_specs=(P(None, "dp", None), owner, owner),
        check_vma=False,
    )
```

```python
import functools

import jax
import jax.numpy as jnp
from jax import lax
from jax.experimental import pallas as pl
from jax.experimental.pallas import tpu as pltpu
from jax.sharding import PartitionSpec as P

MESH = pl.DeviceIdType.MESH
DECAY = 0.95
CLIP = 0.5
BLK = 512
F32 = jnp.float32
BF16 = jnp.bfloat16
PIECES = 4
TOP = 4094 << 14


def iota(shape, axis):
    return lax.broadcasted_iota(jnp.int32, shape, axis)


def dot(a, b):
    return jnp.dot(a, b, preferred_element_type=F32)


def dot_nt(a, b):
    return lax.dot_general(a, b, (((1,), (1,)), ((), ())), preferred_element_type=F32)


def halves(value):
    high = value.astype(BF16)
    return high, (value - high.astype(F32)).astype(BF16)


def encode(value, inverse):
    count = (jnp.abs(value) * inverse + 0.5).astype(jnp.int32)
    shift = jnp.maximum(20 - lax.clz(count), 0)
    code = lax.shift_right_logical(count + lax.shift_right_logical(lax.shift_left(jnp.ones_like(shift), shift), 1), shift)
    code = code + lax.shift_left(shift, 11)
    return jnp.where(value < 0, -code, code).astype(jnp.int16)


def decode(code):
    code = code.astype(jnp.int32)
    size = jnp.abs(code)
    shift = jnp.maximum(lax.shift_right_logical(size, 11) - 1, 0)
    count = lax.shift_left(size - lax.shift_left(shift, 11), shift).astype(F32)
    return jnp.where(code < 0, -count, count)


def kernel(
    slot_ref, modality_ref, rates_ref, grad_hbm, lstat_hbm, rstat_hbm, lroot_hbm, rroot_hbm,
    update_hbm, lnew_hbm, rnew_hbm,
    grad, lstat, rstat, rroot, lfull, parts, got, code_out, step_out, step_plane, step_mid, step_mine, gown, gcode, gstep, ghigh, glow,
    rows_out, back, mine, meta_out, meta_plane, meta_mid, meta_mine, meta_own, meta_in, half, final, scale_col, spread, update, lnew, rnew,
    ready, in_sem, out_sem, p_send, p_recv, l_send, l_recv, a_send, a_recv,
    t_send, t_recv, u_send, u_recv, g_send, g_recv, s_send, s_recv, d_send, d_recv, cm_send, cm_recv, dm_send, dm_recv, m_send, m_recv,
    f_send, f_recv,
):
    x = lax.axis_index("rep")
    d = lax.axis_index("dp")
    c = lax.rem(d, 2)
    z = lax.rem(lax.div(d, 2), 8)
    y = lax.div(d, 16)
    def on_plane(to_y, to_z):
        return (16 * to_y + 2 * to_z + c, x)

    def on_column(to_x, to_c):
        return (d - c + to_c, to_x)

    def send(src, dst, s_sem, r_sem, device):
        return pltpu.make_async_remote_copy(
            src_ref=src, dst_ref=dst, send_sem=s_sem, recv_sem=r_sem, device_id=device, device_id_type=MESH
        )

    column = [(dx, dc) for dx in (2, 1, 3, 0) for dc in (0, 1) if (dx, dc) != (0, 0)]

    loads = [
        pltpu.make_async_copy(grad_hbm.at[0], grad, in_sem.at[0]),
        pltpu.make_async_copy(lroot_hbm.at[0], lfull.at[x], in_sem.at[1]),
        pltpu.make_async_copy(rroot_hbm.at[0], rroot, in_sem.at[2]),
        pltpu.make_async_copy(lstat_hbm.at[0], lstat, in_sem.at[3]),
        pltpu.make_async_copy(rstat_hbm.at[0], rstat, in_sem.at[4]),
    ]
    loads[0].start()

    barrier = pltpu.get_barrier_semaphore()
    for dx, dc in column:
        pl.semaphore_signal(
            barrier, inc=1, device_id=on_column(lax.rem(x + dx, 4), lax.rem(c + dc, 2)), device_id_type=MESH
        )
    for e in range(1, 8):
        pl.semaphore_signal(barrier, inc=1, device_id=on_plane(lax.rem(y + e, 8), z), device_id_type=MESH)
        pl.semaphore_signal(barrier, inc=1, device_id=on_plane(y, lax.rem(z + e, 8)), device_id_type=MESH)

    for load in loads[1:]:
        load.start()

    slots = slot_ref[...]
    slots8 = jnp.broadcast_to(slots, (8, 128)).astype(F32).astype(BF16)
    widen = (lax.shift_right_logical(iota((128, 512), 1), 2) == iota((128, 512), 0)).astype(F32).astype(BF16)
    code_row = 4 * dot(slots8, widen)[0:1, :].astype(jnp.int32) + (iota((1, 512), 1) & 3)
    row = iota((512, 128), 0)
    row_y = (y + lax.shift_right_logical(row, 5)) & 7
    row_z = lax.shift_right_logical(row, 2) & 7
    row_slot = 16 * row_y + 2 * row_z + lax.shift_right_logical(row, 8)
    row_code = 4 * row_slot + (row & 3)
    order = jnp.concatenate(
        [(row_code == code_row[:, 128 * t : 128 * t + 128]).astype(F32).astype(BF16) for t in range(4)], axis=1
    )
    loads[0].wait()
    flat = grad[...].reshape(512, 512)
    for h in range(2):
        rows = jnp.concatenate([order[128 * h : 128 * h + 128], order[256 + 128 * h : 384 + 128 * h]], axis=0)
        ordered = dot(rows, flat).astype(BF16)
        for q in range(4):
            parts[q, 0, h] = ordered[:128, 128 * q : 128 * q + 128]
            parts[q, 1, h] = ordered[128:, 128 * q : 128 * q + 128]

    pl.semaphore_wait(barrier, len(column) + 14)
    first = []
    for h in range(2):
        for dx, dc in column:
            to_x, to_c = lax.rem(x + dx, 4), lax.rem(c + dc, 2)
            copy = send(
                parts.at[to_x, to_c, h], got.at[x, c, h], p_send.at[dx, dc, h], p_recv.at[dx, c, h], on_column(to_x, to_c)
            )
            copy.start()
            first.append(copy)
    for e in range(1, 8):
        pl.semaphore_signal(ready, inc=1, device_id=on_plane(lax.rem(y + e, 8), z), device_id_type=MESH)
    got[x, c] = parts[x, c]
    loads[1].wait()
    right, left = lax.rem(x + 1, 4), lax.rem(x + 3, 4)

    def root(n, q, rows, to):
        at = lfull.at[q, rows]
        return send(at, at, l_send.at[n], l_recv.at[n], on_column(to, c))

    every, low_half, high_half = pl.ds(0, 128), pl.ds(0, 64), pl.ds(64, 64)
    roots = [root(0, x, every, right), root(1, x, every, left), root(2, left, low_half, right), root(3, right, high_half, left)]
    upper = iota((16, 8, 128), 1) < 4
    lane = iota((8, 128), 1)
    sub = iota((8, 128), 0)

    def add_up(h):
        for dx, dc in column:
            from_c = lax.rem(c + dc, 2)
            send(parts.at[0, 0, h], got.at[0, 0, h], p_send.at[dx, dc, h], p_recv.at[dx, from_c, h], on_column(x, c)).wait_recv()
        sums = []
        for core in range(2):
            total = got[0, core, h].astype(F32)
            for q in range(1, 4):
                total = total + got[q, core, h].astype(F32)
            sums.append(total.reshape(16, 8, 128))
        even = jnp.where(upper, sums[0], pltpu.roll(sums[1], 4, 1))
        odd = jnp.where(upper, pltpu.roll(sums[0], 4, 1), sums[1])
        for which, value in ((0, even), (1, odd)):
            top = jnp.maximum(jnp.max(jnp.abs(value), axis=2, keepdims=True), 1e-30)
            scaled = value * (32767.0 / top)
            code = (scaled + jnp.where(scaled < 0, -0.5, 0.5)).astype(jnp.int32).astype(jnp.int16)
            step = top / 32767.0
            for n in range(4):
                tile = jnp.zeros((8, 128), F32)
                for p in range(4):
                    code_out[4 * h + n, 2 * p + which] = code[4 * n + p]
                    tile = jnp.where(lane == 8 * (2 * p + which) + y, step[4 * n + p], tile)
                if which == 0:
                    step_out[4 * h + n] = tile
                else:
                    step_out[4 * h + n] = step_out[4 * h + n] + tile


    def scatter(src, dst, g, s_sem, r_sem):
        to_y = lax.rem(y + g, 8)

        def one(e, carry):
            to_z = lax.rem(z + e, 8)
            send(src(to_y).at[to_z], dst, s_sem, r_sem, on_plane(to_y, to_z)).start()
            return carry

        lax.fori_loop(1 if g == 0 else 0, 8, one, 0)

    def tiles_of(ref, g):
        return ref.at[0, 1:8] if g == 0 else ref.at[0]

    quarters = []

    def forward(g):
        came = tiles_of(gcode.at[0], g)
        send(came, came, a_send.at[g], a_recv.at[g], on_column(x, c)).wait_recv()
        at = lax.rem(y + 8 - g, 8)
        for dx in (2, 1, 3):
            to = lax.rem(x + dx, 4)
            copy = send(gcode.at[x, at], gcode.at[x, at], g_send.at[dx, g], g_recv.at[dx, g], on_column(to, c))
            copy.start()
            quarters.append(copy)

    def first_scatter(g):
        scatter(lambda to_y: code_out.at[g], gcode.at[x, y, z], g, a_send.at[g], a_recv.at[g])

    add_up(0)
    gcode[x, y, z] = code_out[0, z]
    pl.semaphore_wait(ready, 7)
    for g in range(4):
        first_scatter(g)
    add_up(1)
    steps_a = []
    for g in range(1, 8):
        copy = send(step_out.at[g], step_plane.at[y], t_send.at[g], t_recv.at[g], on_plane(lax.rem(y + g, 8), z))
        copy.start()
        steps_a.append(copy)
    step_plane[y] = step_out[0]
    roots[0].start()
    roots[1].start()
    for g in range(4, 8):
        first_scatter(g)
    for copy in steps_a:
        copy.wait_recv()
    steps = step_plane[0]
    for e in range(1, 8):
        steps = steps + step_plane[e]
    step_mid[...] = steps
    steps_b = []
    for e in range(1, 8):
        copy = send(step_mid, step_mine.at[z], u_send.at[e], u_recv.at[e], on_plane(y, lax.rem(z + e, 8)))
        copy.start()
        steps_b.append(copy)
    step_mine[z] = steps
    for g in range(8):
        forward(g)
        if g == 4:
            roots[0].wait_recv()
            roots[2].start()
            roots[1].wait_recv()
            roots[3].start()
    for copy in steps_b:
        copy.wait_recv()
    steps = jnp.zeros((8, 128), F32)
    for e in range(8):
        turned = pltpu.roll(step_mine[e], lax.rem(8 * e + 128 - 8 * z, 128), 1)
        steps = jnp.where(lax.shift_right_logical(lane, 3) == e, turned, steps)
    gstep[x] = steps
    for dx in (2, 1, 3):
        copy = send(gstep.at[x], gstep.at[x], s_send.at[dx], s_recv.at[dx], on_column(lax.rem(x + dx, 4), c))
        copy.start()
        quarters.append(copy)

    def take(q, block):
        high, low = halves(block)
        at = pl.ds(pl.multiple_of(128 * q, 128), 128)
        ghigh[:, at] = high
        glow[:, at] = low
        other = rroot[:, at]
        return dot_nt(high, other) + dot_nt(low, other)

    def quarter(q):
        code = gcode[q].astype(jnp.int32).astype(F32).reshape(64, 8, 128)
        step = gstep[q]
        at = [8 * (k % 8) + k // 8 for k in range(64)]
        return jnp.concatenate([code[k] * step[:, at[k] : at[k] + 1] for k in range(64)], axis=0)

    def other_quarter(dx):
        q = lax.rem(x + 4 - dx, 4)
        for g in range(8):
            send(gcode.at[0, 0], gcode.at[0, 0], g_send.at[dx, g], g_recv.at[dx, g], on_column(x, c)).wait_recv()
        send(gstep.at[0], gstep.at[0], s_send.at[dx], s_recv.at[dx], on_column(x, c)).wait_recv()
        return take(q, quarter(q))

    loads[2].wait()
    own = quarter(x)
    gown[...] = own
    grad_sq = jnp.sum(own * own)
    product = take(x, own)
    product = product + other_quarter(1)
    product = product + other_quarter(3)
    product = product + other_quarter(2)
    roots[2].wait_recv()
    roots[3].wait_recv()
    product = jnp.concatenate(halves(product), axis=1)
    prec_sq = jnp.zeros((8, 128), F32)
    peak = jnp.zeros((8, 128), F32)
    for q in range(4):
        rows = dot(lfull[q], product)
        rows = (rows[:, :128] + rows[:, 128:]).reshape(16, 8, 128)
        prec_sq = prec_sq + jnp.sum(rows * rows, axis=0)
        peak = jnp.maximum(peak, jnp.max(jnp.abs(rows), axis=0))
        rows_out[2 * q : 2 * q + 2] = rows.reshape(2, 8, 8, 128)
    peak = jnp.maximum(jnp.max(jnp.max(peak, axis=0, keepdims=True), axis=1, keepdims=True), 1e-30)
    inverse = TOP / peak
    for e in range(8):
        back[e] = encode(rows_out[e], inverse)

    prec_sq = jnp.sum(jnp.sum(prec_sq, axis=0, keepdims=True), axis=1, keepdims=True)
    meta = jnp.where(lane == z, grad_sq, jnp.where(lane == 32 + z, peak / TOP, jnp.where(lane == 64 + z, prec_sq, 0.0)))
    meta_out[...] = jnp.where(sub == y, meta, 0.0)
    meta_plane[y] = meta_out[...]

    mine[0, z] = back[y, z]
    for g in range(4):
        scatter(lambda to_y: back.at[to_y], mine.at[g, z], g, d_send.at[g], d_recv.at[g])
    meta_c = []
    for e in range(1, 8):
        copy = send(meta_out, meta_plane.at[y], cm_send.at[e], cm_recv.at[e], on_plane(lax.rem(y + e, 8), z))
        copy.start()
        meta_c.append(copy)
    upper = iota((8, 8, 128), 1) < 4
    sends = []

    def hand_on(p):
        for g in (2 * p, 2 * p + 1):
            came = tiles_of(mine, g)
            send(came, came, d_send.at[g], d_recv.at[g], on_column(x, c)).wait_recv()
        tiles = mine[2 * p : 2 * p + 2].astype(jnp.int32).reshape(8, 2, 8, 128)
        a, b = tiles[:, 0], tiles[:, 1]
        half[0, p] = jnp.where(upper, a, pltpu.roll(b, 4, 1)).astype(jnp.int16)
        half[1, p] = jnp.where(upper, pltpu.roll(a, 4, 1), b).astype(jnp.int16)
        for dx, dc in column:
            to_x, to_c = lax.rem(x + dx, 4), lax.rem(c + dc, 2)
            copy = send(half.at[to_c, p], final.at[x, c, p], f_send.at[dx, dc, p], f_recv.at[dx, c, p], on_column(to_x, to_c))
            copy.start()
            sends.append(copy)
        final[x, c, p] = half[c, p]

    def came_on(dx, core, p):
        send(half.at[0, p], final.at[0, 0, p], f_send.at[1, 0, p], f_recv.at[dx, core, p], on_column(x, c)).wait_recv()

    def back_scatter(g):
        scatter(lambda to_y: back.at[to_y], mine.at[g, z], g, d_send.at[g], d_recv.at[g])

    back_scatter(4)
    back_scatter(5)
    hand_on(0)
    back_scatter(6)
    back_scatter(7)
    hand_on(1)
    for copy in meta_c:
        copy.wait_recv()
    meta = meta_plane[0]
    for e in range(1, 8):
        meta = meta + meta_plane[e]
    meta_mid[...] = meta
    meta_d = []
    for e in range(1, 8):
        copy = send(meta_mid, meta_mine.at[z], dm_send.at[e], dm_recv.at[e], on_plane(y, lax.rem(z + e, 8)))
        copy.start()
        meta_d.append(copy)
    meta_mine[z] = meta
    hand_on(2)
    hand_on(3)
    for copy in meta_d:
        copy.wait_recv()
    meta = meta_mine[0]
    for e in range(1, 8):
        meta = meta + meta_mine[e]
    meta_own[...] = meta
    metas = []
    for dx, dc in column:
        to_x, to_c = lax.rem(x + dx, 4), lax.rem(c + dc, 2)
        copy = send(meta_own, meta_in.at[x, c], m_send.at[dx, dc], m_recv.at[dx, c], on_column(to_x, to_c))
        copy.start()
        metas.append(copy)
    meta_in[x, c] = meta

    loads[3].wait()
    loads[4].wait()
    gain = (1.0 - DECAY) / BLK
    mine_rows = pl.ds(pl.multiple_of(128 * x, 128), 128)
    high, low = ghigh[...], glow[...]
    high_rows, low_rows = ghigh[mine_rows, :], glow[mine_rows, :]
    lnew[...] = DECAY * lstat[...] + gain * (dot_nt(high_rows, high) + (dot_nt(high_rows, low) + dot_nt(low_rows, high)))
    turned = gown[...].T
    high_turned, low_turned = halves(turned)
    rnew[...] = DECAY * rstat[...] + gain * (dot(high_turned, high) + (dot(high_turned, low) + dot(low_turned, high)))
    out_l = pltpu.make_async_copy(lnew, lnew_hbm.at[0], out_sem.at[0])
    out_r = pltpu.make_async_copy(rnew, rnew_hbm.at[0], out_sem.at[1])
    out_l.start()
    out_r.start()

    block_of_row = lax.shift_right_logical(row, 2)
    lanes = iota((512, 128), 1)
    is_block = lanes == block_of_row
    slot_col = jnp.sum(jnp.where(is_block, slots.astype(F32), 0.0), axis=1, keepdims=True)
    code_col = 4 * slot_col.astype(jnp.int32) + (iota((512, 1), 0) & 3)
    col = iota((1, 512), 1)
    col_y = (y + 8 - (lax.shift_right_logical(col, 5) & 7)) & 7
    col_z = lax.shift_right_logical(col, 2) & 7
    col_slot = 16 * col_y + 2 * col_z + lax.shift_right_logical(col, 8)
    col_code = 4 * col_slot + (col & 3)
    spread[...] = (code_col == col_code).astype(F32).astype(BF16)

    for dx, dc in column:
        send(meta_own, meta_in.at[0, 0], m_send.at[dx, dc], m_recv.at[dx, lax.rem(c + dc, 2)], on_column(x, c)).wait_recv()
    grad_b = jnp.zeros((8, 128), F32)
    prec_b = jnp.zeros((8, 128), F32)
    step_b = [jnp.zeros((8, 128), F32) for _ in range(4)]
    for core in range(2):
        known = [meta_in[q, core] for q in range(4)]
        both = known[0] + known[1] + known[2] + known[3]
        for e in range(8):
            here = slots == 16 * sub + 2 * e + core
            grad_b = grad_b + jnp.where(here, both[:, e : e + 1], 0.0)
            prec_b = prec_b + jnp.where(here, both[:, 64 + e : 65 + e], 0.0)
            for q in range(4):
                step_b[q] = step_b[q] + jnp.where(here, known[q][:, 32 + e : 33 + e], 0.0)
    grad_b = jnp.sum(grad_b, axis=0, keepdims=True)
    prec_b = jnp.sum(prec_b, axis=0, keepdims=True)
    scale = jnp.zeros((1, 128), F32)
    for m in range(2):
        member = modality_ref[...] == m
        total = jnp.sum(jnp.where(member, grad_b, 0.0), axis=1, keepdims=True)
        count = jnp.sum(jnp.where(member, 1.0, 0.0), axis=1, keepdims=True)
        rms = jnp.sqrt(total / (count * (BLK * BLK)) + 1e-6)
        clip = jnp.minimum(1.0, CLIP / rms)
        scale = jnp.where(member, rates_ref[m] * clip, scale)
    scale = scale * jnp.sqrt(grad_b / (prec_b + 1e-6))
    for q in range(4):
        step = scale * jnp.sum(step_b[q], axis=0, keepdims=True)
        scale_col[q] = jnp.broadcast_to(jnp.sum(jnp.where(is_block, step, 0.0), axis=1, keepdims=True), (512, 128))

    outs = []

    def finish(q):
        high, low = halves(decode(final[q]).reshape(512, 128))
        both = dot(spread[...], jnp.concatenate([high, low], axis=1))
        rows = (both[:, :128] + both[:, 128:]) * scale_col[q]
        at = pl.ds(pl.multiple_of(128 * q, 128), 128)
        update[:, :, at] = rows.reshape(128, 4, 128)
        copy = pltpu.make_async_copy(update.at[:, :, at], update_hbm.at[:, :, at], out_sem.at[2 + len(outs)])
        copy.start()
        outs.append(copy)

    for p in range(PIECES):
        came_on(0, 1 - c, p)
    finish(x)
    for dx in (1, 3, 2):
        for p in range(PIECES):
            for core in range(2):
                came_on(dx, core, p)
        finish(lax.rem(x + 4 - dx, 4))

    for copy in first + roots + steps_a + steps_b + quarters + meta_c:
        copy.wait_send()
    for g in range(8):
        for ref, sem in ((code_out, a_send), (back, d_send)):
            gone = tiles_of(ref, g)
            send(gone, gone, sem.at[g], sem.at[g], on_column(x, c)).wait_send()
    for copy in meta_d + metas + sends:
        copy.wait_send()
    for copy in outs:
        copy.wait()
    out_l.wait()
    out_r.wait()


def place(update, left_new, right_new, update_out, left_out, right_out, sems):
    copies = [pltpu.make_async_copy(update.at[32 * p : 32 * p + 32], update_out.at[32 * p : 32 * p + 32], sems.at[p]) for p in range(4)]
    copies += [pltpu.make_async_copy(left_new, left_out, sems.at[4]), pltpu.make_async_copy(right_new, right_out, sems.at[5])]
    for copy in copies:
        copy.start()
    for copy in copies:
        copy.wait()


def local(grad_parts, left_stat, right_stat, left_root, right_root, block_slot, block_modality, modality_rates):
    vmem = pl.BlockSpec(memory_space=pltpu.VMEM)
    smem = pl.BlockSpec(memory_space=pltpu.SMEM)
    hbm = pl.BlockSpec(memory_space=pltpu.HBM)
    dma = pltpu.SemaphoreType.DMA
    update, left_new, right_new = pl.pallas_call(
        kernel,
        out_shape=(
            jax.ShapeDtypeStruct((128, 4, 512), F32),
            jax.ShapeDtypeStruct(left_stat.shape, F32),
            jax.ShapeDtypeStruct(right_stat.shape, F32),
        ),
        in_specs=[vmem, vmem, smem, hbm, hbm, hbm, hbm, hbm],
        out_specs=(hbm, hbm, hbm),
        scratch_shapes=[
            pltpu.VMEM((128, 4, 512), BF16),
            pltpu.VMEM((128, 512), F32),
            pltpu.VMEM((128, 512), F32),
            pltpu.VMEM((128, 512), BF16),
            pltpu.VMEM((4, 128, 512), BF16),
            pltpu.VMEM((4, 2, 2, 128, 128), BF16),
            pltpu.VMEM((4, 2, 2, 128, 128), BF16),
            pltpu.VMEM((8, 8, 8, 128), jnp.int16),
            pltpu.VMEM((8, 8, 128), F32),
            pltpu.VMEM((8, 8, 128), F32),
            pltpu.VMEM((8, 128), F32),
            pltpu.VMEM((8, 8, 128), F32),
            pltpu.VMEM((512, 128), F32),
            pltpu.VMEM((4, 8, 8, 8, 128), jnp.int16),
            pltpu.VMEM((4, 8, 128), F32),
            pltpu.VMEM((512, 512), BF16),
            pltpu.VMEM((512, 512), BF16),
            pltpu.VMEM((8, 8, 8, 128), F32),
            pltpu.VMEM((8, 8, 8, 128), jnp.int16),
            pltpu.VMEM((8, 8, 8, 128), jnp.int16),
            pltpu.VMEM((8, 128), F32),
            pltpu.VMEM((8, 8, 128), F32),
            pltpu.VMEM((8, 128), F32),
            pltpu.VMEM((8, 8, 128), F32),
            pltpu.VMEM((8, 128), F32),
            pltpu.VMEM((4, 2, 8, 128), F32),
            pltpu.VMEM((2, 4, 8, 8, 128), jnp.int16),
            pltpu.VMEM((4, 2, 4, 8, 8, 128), jnp.int16),
            pltpu.VMEM((4, 512, 128), F32),
            pltpu.VMEM((512, 512), BF16),
            pltpu.VMEM((128, 4, 512), F32),
            pltpu.VMEM((128, 512), F32),
            pltpu.VMEM((128, 512), F32),
            pltpu.SemaphoreType.REGULAR,
            dma((5,)), dma((6,)),
            dma((4, 2, 2)), dma((4, 2, 2)),
            dma((4,)), dma((4,)),
            dma((8,)), dma((8,)),
            dma((8,)), dma((8,)),
            dma((8,)), dma((8,)),
            dma((4, 8)), dma((4, 8)),
            dma((4,)), dma((4,)),
            dma((8,)), dma((8,)),
            dma((8,)), dma((8,)),
            dma((8,)), dma((8,)),
            dma((4, 2)), dma((4, 2)),
            dma((4, 2, PIECES)), dma((4, 2, PIECES)),
        ],
        compiler_params=pltpu.CompilerParams(
            collective_id=1, has_side_effects=True, vmem_limit_bytes=24 * 2**20
        ),
        name="shampoo_step",
    )(
        *(
            pltpu.with_memory_space_constraint(array, pltpu.HBM)
            for array in (
                block_slot.reshape(1, 128), block_modality.reshape(1, 128), modality_rates,
                grad_parts, left_stat, right_stat, left_root, right_root,
            )
        ),
    )
    results = (update, left_new, right_new)
    return pl.pallas_call(
        place,
        out_shape=tuple(jax.ShapeDtypeStruct(result.shape, F32) for result in results),
        in_specs=[hbm] * 3,
        out_specs=(hbm,) * 3,
        scratch_shapes=[dma((6,))],
        compiler_params=pltpu.CompilerParams(vmem_limit_bytes=4 * 2**20),
        name="place_results",
    )(*results)


def solution(mesh):
    owner = P("dp", "rep", None)
    return jax.shard_map(
        local,
        mesh=mesh,
        in_specs=(P("rep", None, "dp", None), owner, owner, owner, owner, P(), P(), P()),
        out_specs=(P(None, "dp", None), owner, owner),
        check_vma=False,
    )
```

```python
import functools

import jax
import jax.numpy as jnp
from jax import lax
from jax.experimental import pallas as pl
from jax.experimental.pallas import tpu as pltpu
from jax.sharding import PartitionSpec as P

MESH = pl.DeviceIdType.MESH
DECAY = 0.95
CLIP = 0.5
BLK = 512
F32 = jnp.float32
BF16 = jnp.bfloat16
PIECES = 4
TOP = 4094 << 14


def iota(shape, axis):
    return lax.broadcasted_iota(jnp.int32, shape, axis)


def dot(a, b):
    return jnp.dot(a, b, preferred_element_type=F32)


def dot_nt(a, b):
    return lax.dot_general(a, b, (((1,), (1,)), ((), ())), preferred_element_type=F32)


def halves(value):
    high = value.astype(BF16)
    return high, (value - high.astype(F32)).astype(BF16)


def encode(value, inverse):
    count = (jnp.abs(value) * inverse + 0.5).astype(jnp.int32)
    shift = jnp.maximum(20 - lax.clz(count), 0)
    code = lax.shift_right_logical(count + lax.shift_right_logical(lax.shift_left(jnp.ones_like(shift), shift), 1), shift)
    code = code + lax.shift_left(shift, 11)
    return jnp.where(value < 0, -code, code).astype(jnp.int16)


def decode(code):
    code = code.astype(jnp.int32)
    size = jnp.abs(code)
    shift = jnp.maximum(lax.shift_right_logical(size, 11) - 1, 0)
    count = lax.shift_left(size - lax.shift_left(shift, 11), shift).astype(F32)
    return jnp.where(code < 0, -count, count)


def kernel(
    slot_ref, modality_ref, rates_ref, grad_hbm, lstat_hbm, rstat_hbm, lroot_hbm, rroot_hbm,
    update_hbm, lnew_hbm, rnew_hbm,
    grad, lstat, rstat, rroot, lfull, parts, got, code_out, step_out, step_plane, step_mid, step_mine, gown, gcode, gstep, ghigh, glow,
    rows_out, back, mine, meta_out, meta_plane, meta_mid, meta_mine, meta_own, meta_in, half, final, unscaled, scale_col, spread, update, lnew, rnew,
    ready, in_sem, out_sem, p_send, p_recv, l_send, l_recv, a_send, a_recv,
    t_send, t_recv, u_send, u_recv, g_send, g_recv, s_send, s_recv, d_send, d_recv, cm_send, cm_recv, dm_send, dm_recv, m_send, m_recv,
    f_send, f_recv,
):
    x = lax.axis_index("rep")
    d = lax.axis_index("dp")
    c = lax.rem(d, 2)
    z = lax.rem(lax.div(d, 2), 8)
    y = lax.div(d, 16)
    def on_plane(to_y, to_z):
        return (16 * to_y + 2 * to_z + c, x)

    def on_column(to_x, to_c):
        return (d - c + to_c, to_x)

    def send(src, dst, s_sem, r_sem, device):
        return pltpu.make_async_remote_copy(
            src_ref=src, dst_ref=dst, send_sem=s_sem, recv_sem=r_sem, device_id=device, device_id_type=MESH
        )

    column = [(dx, dc) for dx in (2, 1, 3, 0) for dc in (0, 1) if (dx, dc) != (0, 0)]

    loads = [
        pltpu.make_async_copy(grad_hbm.at[0], grad, in_sem.at[0]),
        pltpu.make_async_copy(lroot_hbm.at[0], lfull.at[x], in_sem.at[1]),
        pltpu.make_async_copy(rroot_hbm.at[0], rroot, in_sem.at[2]),
        pltpu.make_async_copy(lstat_hbm.at[0], lstat, in_sem.at[3]),
        pltpu.make_async_copy(rstat_hbm.at[0], rstat, in_sem.at[4]),
    ]
    loads[0].start()

    barrier = pltpu.get_barrier_semaphore()
    for dx, dc in column:
        pl.semaphore_signal(
            barrier, inc=1, device_id=on_column(lax.rem(x + dx, 4), lax.rem(c + dc, 2)), device_id_type=MESH
        )
    for e in range(1, 8):
        pl.semaphore_signal(barrier, inc=1, device_id=on_plane(lax.rem(y + e, 8), z), device_id_type=MESH)
        pl.semaphore_signal(barrier, inc=1, device_id=on_plane(y, lax.rem(z + e, 8)), device_id_type=MESH)

    for load in loads[1:]:
        load.start()

    slots = slot_ref[...]
    slots8 = jnp.broadcast_to(slots, (8, 128)).astype(F32).astype(BF16)
    widen = (lax.shift_right_logical(iota((128, 512), 1), 2) == iota((128, 512), 0)).astype(F32).astype(BF16)
    code_row = 4 * dot(slots8, widen)[0:1, :].astype(jnp.int32) + (iota((1, 512), 1) & 3)
    row = iota((512, 128), 0)
    row_y = (y + lax.shift_right_logical(row, 5)) & 7
    row_z = lax.shift_right_logical(row, 2) & 7
    row_slot = 16 * row_y + 2 * row_z + lax.shift_right_logical(row, 8)
    row_code = 4 * row_slot + (row & 3)
    order = jnp.concatenate(
        [(row_code == code_row[:, 128 * t : 128 * t + 128]).astype(F32).astype(BF16) for t in range(4)], axis=1
    )
    loads[0].wait()
    flat = grad[...].reshape(512, 512)
    for h in range(2):
        rows = jnp.concatenate([order[128 * h : 128 * h + 128], order[256 + 128 * h : 384 + 128 * h]], axis=0)
        ordered = dot(rows, flat).astype(BF16)
        for q in range(4):
            parts[q, 0, h] = ordered[:128, 128 * q : 128 * q + 128]
            parts[q, 1, h] = ordered[128:, 128 * q : 128 * q + 128]

    pl.semaphore_wait(barrier, len(column) + 14)
    first = []
    for h in range(2):
        for dx, dc in column:
            to_x, to_c = lax.rem(x + dx, 4), lax.rem(c + dc, 2)
            copy = send(
                parts.at[to_x, to_c, h], got.at[x, c, h], p_send.at[dx, dc, h], p_recv.at[dx, c, h], on_column(to_x, to_c)
            )
            copy.start()
            first.append(copy)
    for e in range(1, 8):
        pl.semaphore_signal(ready, inc=1, device_id=on_plane(lax.rem(y + e, 8), z), device_id_type=MESH)
    got[x, c] = parts[x, c]
    loads[1].wait()
    right, left = lax.rem(x + 1, 4), lax.rem(x + 3, 4)

    def root(n, q, rows, to):
        at = lfull.at[q, rows]
        return send(at, at, l_send.at[n], l_recv.at[n], on_column(to, c))

    every, low_half, high_half = pl.ds(0, 128), pl.ds(0, 64), pl.ds(64, 64)
    roots = [root(0, x, every, right), root(1, x, every, left), root(2, left, low_half, right), root(3, right, high_half, left)]
    upper = iota((16, 8, 128), 1) < 4
    lane = iota((8, 128), 1)
    sub = iota((8, 128), 0)

    def add_up(h):
        for dx, dc in column:
            from_c = lax.rem(c + dc, 2)
            send(parts.at[0, 0, h], got.at[0, 0, h], p_send.at[dx, dc, h], p_recv.at[dx, from_c, h], on_column(x, c)).wait_recv()
        sums = []
        for core in range(2):
            total = got[0, core, h].astype(F32)
            for q in range(1, 4):
                total = total + got[q, core, h].astype(F32)
            sums.append(total.reshape(16, 8, 128))
        even = jnp.where(upper, sums[0], pltpu.roll(sums[1], 4, 1))
        odd = jnp.where(upper, pltpu.roll(sums[0], 4, 1), sums[1])
        for which, value in ((0, even), (1, odd)):
            top = jnp.maximum(jnp.max(jnp.abs(value), axis=2, keepdims=True), 1e-30)
            scaled = value * (32767.0 / top)
            code = (scaled + jnp.where(scaled < 0, -0.5, 0.5)).astype(jnp.int32).astype(jnp.int16)
            step = top / 32767.0
            for n in range(4):
                tile = jnp.zeros((8, 128), F32)
                for p in range(4):
                    code_out[4 * h + n, 2 * p + which] = code[4 * n + p]
                    tile = jnp.where(lane == 8 * (2 * p + which) + y, step[4 * n + p], tile)
                if which == 0:
                    step_out[4 * h + n] = tile
                else:
                    step_out[4 * h + n] = step_out[4 * h + n] + tile


    def scatter(src, dst, g, s_sem, r_sem):
        to_y = lax.rem(y + g, 8)

        def one(e, carry):
            to_z = lax.rem(z + e, 8)
            send(src(to_y).at[to_z], dst, s_sem, r_sem, on_plane(to_y, to_z)).start()
            return carry

        lax.fori_loop(1 if g == 0 else 0, 8, one, 0)

    def tiles_of(ref, g):
        return ref.at[0, 1:8] if g == 0 else ref.at[0]

    quarters = []

    def forward(g):
        came = tiles_of(gcode.at[0], g)
        send(came, came, a_send.at[g], a_recv.at[g], on_column(x, c)).wait_recv()
        at = lax.rem(y + 8 - g, 8)
        for dx in (2, 1, 3):
            to = lax.rem(x + dx, 4)
            copy = send(gcode.at[x, at], gcode.at[x, at], g_send.at[dx, g], g_recv.at[dx, g], on_column(to, c))
            copy.start()
            quarters.append(copy)

    def first_scatter(g):
        scatter(lambda to_y: code_out.at[g], gcode.at[x, y, z], g, a_send.at[g], a_recv.at[g])

    add_up(0)
    gcode[x, y, z] = code_out[0, z]
    pl.semaphore_wait(ready, 7)
    for g in range(4):
        first_scatter(g)
    add_up(1)
    steps_a = []
    for g in range(1, 8):
        copy = send(step_out.at[g], step_plane.at[y], t_send.at[g], t_recv.at[g], on_plane(lax.rem(y + g, 8), z))
        copy.start()
        steps_a.append(copy)
    step_plane[y] = step_out[0]
    roots[0].start()
    roots[1].start()
    for g in range(4, 8):
        first_scatter(g)
    for copy in steps_a:
        copy.wait_recv()
    steps = step_plane[0]
    for e in range(1, 8):
        steps = steps + step_plane[e]
    step_mid[...] = steps
    steps_b = []
    for e in range(1, 8):
        copy = send(step_mid, step_mine.at[z], u_send.at[e], u_recv.at[e], on_plane(y, lax.rem(z + e, 8)))
        copy.start()
        steps_b.append(copy)
    step_mine[z] = steps
    for g in range(8):
        forward(g)
        if g == 4:
            roots[0].wait_recv()
            roots[2].start()
            roots[1].wait_recv()
            roots[3].start()
    for copy in steps_b:
        copy.wait_recv()
    steps = jnp.zeros((8, 128), F32)
    for e in range(8):
        turned = pltpu.roll(step_mine[e], lax.rem(8 * e + 128 - 8 * z, 128), 1)
        steps = jnp.where(lax.shift_right_logical(lane, 3) == e, turned, steps)
    gstep[x] = steps
    for dx in (2, 1, 3):
        copy = send(gstep.at[x], gstep.at[x], s_send.at[dx], s_recv.at[dx], on_column(lax.rem(x + dx, 4), c))
        copy.start()
        quarters.append(copy)

    def take(q, block):
        high, low = halves(block)
        at = pl.ds(pl.multiple_of(128 * q, 128), 128)
        ghigh[:, at] = high
        glow[:, at] = low
        other = rroot[:, at]
        return dot_nt(high, other) + dot_nt(low, other)

    def quarter(q):
        code = gcode[q].astype(jnp.int32).astype(F32).reshape(64, 8, 128)
        step = gstep[q]
        at = [8 * (k % 8) + k // 8 for k in range(64)]
        return jnp.concatenate([code[k] * step[:, at[k] : at[k] + 1] for k in range(64)], axis=0)

    def other_quarter(dx):
        q = lax.rem(x + 4 - dx, 4)
        for g in range(8):
            send(gcode.at[0, 0], gcode.at[0, 0], g_send.at[dx, g], g_recv.at[dx, g], on_column(x, c)).wait_recv()
        send(gstep.at[0], gstep.at[0], s_send.at[dx], s_recv.at[dx], on_column(x, c)).wait_recv()
        return take(q, quarter(q))

    loads[2].wait()
    own = quarter(x)
    gown[...] = own
    grad_sq = jnp.sum(own * own)
    product = take(x, own)
    product = product + other_quarter(1)
    product = product + other_quarter(3)
    product = product + other_quarter(2)
    roots[2].wait_recv()
    roots[3].wait_recv()
    product = jnp.concatenate(halves(product), axis=1)
    prec_sq = jnp.zeros((8, 128), F32)
    peak = jnp.zeros((8, 128), F32)
    for q in range(4):
        rows = dot(lfull[q], product)
        rows = (rows[:, :128] + rows[:, 128:]).reshape(16, 8, 128)
        prec_sq = prec_sq + jnp.sum(rows * rows, axis=0)
        peak = jnp.maximum(peak, jnp.max(jnp.abs(rows), axis=0))
        rows_out[2 * q : 2 * q + 2] = rows.reshape(2, 8, 8, 128)
    peak = jnp.maximum(jnp.max(jnp.max(peak, axis=0, keepdims=True), axis=1, keepdims=True), 1e-30)
    inverse = TOP / peak
    for e in range(8):
        back[e] = encode(rows_out[e], inverse)

    prec_sq = jnp.sum(jnp.sum(prec_sq, axis=0, keepdims=True), axis=1, keepdims=True)
    meta = jnp.where(lane == z, grad_sq, jnp.where(lane == 32 + z, peak / TOP, jnp.where(lane == 64 + z, prec_sq, 0.0)))
    meta_out[...] = jnp.where(sub == y, meta, 0.0)
    meta_plane[y] = meta_out[...]

    mine[0, z] = back[y, z]
    meta_c = []
    for e in range(1, 8):
        copy = send(meta_out, meta_plane.at[y], cm_send.at[e], cm_recv.at[e], on_plane(lax.rem(y + e, 8), z))
        copy.start()
        meta_c.append(copy)
    for g in range(4):
        scatter(lambda to_y: back.at[to_y], mine.at[g, z], g, d_send.at[g], d_recv.at[g])
    for copy in meta_c:
        copy.wait_recv()
    meta = meta_plane[0]
    for e in range(1, 8):
        meta = meta + meta_plane[e]
    meta_mid[...] = meta
    meta_d = []
    for e in range(1, 8):
        copy = send(meta_mid, meta_mine.at[z], dm_send.at[e], dm_recv.at[e], on_plane(y, lax.rem(z + e, 8)))
        copy.start()
        meta_d.append(copy)
    meta_mine[z] = meta

    upper = iota((8, 8, 128), 1) < 4
    sends = []

    def hand_on(p):
        for g in (2 * p, 2 * p + 1):
            came = tiles_of(mine, g)
            send(came, came, d_send.at[g], d_recv.at[g], on_column(x, c)).wait_recv()
        tiles = mine[2 * p : 2 * p + 2].astype(jnp.int32).reshape(8, 2, 8, 128)
        a, b = tiles[:, 0], tiles[:, 1]
        half[0, p] = jnp.where(upper, a, pltpu.roll(b, 4, 1)).astype(jnp.int16)
        half[1, p] = jnp.where(upper, pltpu.roll(a, 4, 1), b).astype(jnp.int16)
        for dx, dc in column:
            to_x, to_c = lax.rem(x + dx, 4), lax.rem(c + dc, 2)
            copy = send(half.at[to_c, p], final.at[x, c, p], f_send.at[dx, dc, p], f_recv.at[dx, c, p], on_column(to_x, to_c))
            copy.start()
            sends.append(copy)
        final[x, c, p] = half[c, p]

    def came_on(dx, core, p):
        send(half.at[0, p], final.at[0, 0, p], f_send.at[1, 0, p], f_recv.at[dx, core, p], on_column(x, c)).wait_recv()

    def back_scatter(g):
        scatter(lambda to_y: back.at[to_y], mine.at[g, z], g, d_send.at[g], d_recv.at[g])

    back_scatter(4)
    back_scatter(5)
    hand_on(0)
    back_scatter(6)
    back_scatter(7)
    hand_on(1)
    for copy in meta_d:
        copy.wait_recv()
    meta = meta_mine[0]
    for e in range(1, 8):
        meta = meta + meta_mine[e]
    meta_own[...] = meta
    metas = []
    for dx, dc in column:
        to_x, to_c = lax.rem(x + dx, 4), lax.rem(c + dc, 2)
        copy = send(meta_own, meta_in.at[x, c], m_send.at[dx, dc], m_recv.at[dx, c], on_column(to_x, to_c))
        copy.start()
        metas.append(copy)
    meta_in[x, c] = meta
    hand_on(2)
    hand_on(3)

    loads[3].wait()
    loads[4].wait()
    gain = (1.0 - DECAY) / BLK
    mine_rows = pl.ds(pl.multiple_of(128 * x, 128), 128)
    high, low = ghigh[...], glow[...]
    high_rows, low_rows = ghigh[mine_rows, :], glow[mine_rows, :]
    lnew[...] = DECAY * lstat[...] + gain * (dot_nt(high_rows, high) + (dot_nt(high_rows, low) + dot_nt(low_rows, high)))
    turned = gown[...].T
    high_turned, low_turned = halves(turned)
    rnew[...] = DECAY * rstat[...] + gain * (dot(high_turned, high) + (dot(high_turned, low) + dot(low_turned, high)))
    out_l = pltpu.make_async_copy(lnew, lnew_hbm.at[0], out_sem.at[0])
    out_r = pltpu.make_async_copy(rnew, rnew_hbm.at[0], out_sem.at[1])
    out_l.start()
    out_r.start()

    block_of_row = lax.shift_right_logical(row, 2)
    lanes = iota((512, 128), 1)
    is_block = lanes == block_of_row
    slot_col = jnp.sum(jnp.where(is_block, slots.astype(F32), 0.0), axis=1, keepdims=True)
    code_col = 4 * slot_col.astype(jnp.int32) + (iota((512, 1), 0) & 3)
    col = iota((1, 512), 1)
    col_y = (y + 8 - (lax.shift_right_logical(col, 5) & 7)) & 7
    col_z = lax.shift_right_logical(col, 2) & 7
    col_slot = 16 * col_y + 2 * col_z + lax.shift_right_logical(col, 8)
    col_code = 4 * col_slot + (col & 3)
    spread[...] = (code_col == col_code).astype(F32).astype(BF16)

    def gather(n, q):
        high, low = halves(decode(final[q]).reshape(512, 128))
        both = dot(spread[...], jnp.concatenate([high, low], axis=1))
        unscaled[n] = both[:, :128] + both[:, 128:]

    for p in range(PIECES):
        came_on(0, 1 - c, p)
    gather(0, x)
    for dx in (1, 3, 2):
        for p in range(PIECES):
            for core in range(2):
                came_on(dx, core, p)
        gather(dx, lax.rem(x + 4 - dx, 4))

    for dx, dc in column:
        send(meta_own, meta_in.at[0, 0], m_send.at[dx, dc], m_recv.at[dx, lax.rem(c + dc, 2)], on_column(x, c)).wait_recv()
    grad_b = jnp.zeros((8, 128), F32)
    prec_b = jnp.zeros((8, 128), F32)
    step_b = [jnp.zeros((8, 128), F32) for _ in range(4)]
    for core in range(2):
        known = [meta_in[q, core] for q in range(4)]
        both = known[0] + known[1] + known[2] + known[3]
        for e in range(8):
            here = slots == 16 * sub + 2 * e + core
            grad_b = grad_b + jnp.where(here, both[:, e : e + 1], 0.0)
            prec_b = prec_b + jnp.where(here, both[:, 64 + e : 65 + e], 0.0)
            for q in range(4):
                step_b[q] = step_b[q] + jnp.where(here, known[q][:, 32 + e : 33 + e], 0.0)
    grad_b = jnp.sum(grad_b, axis=0, keepdims=True)
    prec_b = jnp.sum(prec_b, axis=0, keepdims=True)
    scale = jnp.zeros((1, 128), F32)
    for m in range(2):
        member = modality_ref[...] == m
        total = jnp.sum(jnp.where(member, grad_b, 0.0), axis=1, keepdims=True)
        count = jnp.sum(jnp.where(member, 1.0, 0.0), axis=1, keepdims=True)
        rms = jnp.sqrt(total / (count * (BLK * BLK)) + 1e-6)
        clip = jnp.minimum(1.0, CLIP / rms)
        scale = jnp.where(member, rates_ref[m] * clip, scale)
    scale = scale * jnp.sqrt(grad_b / (prec_b + 1e-6))
    for q in range(4):
        step = scale * jnp.sum(step_b[q], axis=0, keepdims=True)
        scale_col[q] = jnp.broadcast_to(jnp.sum(jnp.where(is_block, step, 0.0), axis=1, keepdims=True), (512, 128))

    outs = []
    for n in range(4):
        q = lax.rem(x + 4 - n, 4)
        at = pl.ds(pl.multiple_of(128 * q, 128), 128)
        update[:, :, at] = (unscaled[n] * scale_col[q]).reshape(128, 4, 128)
        copy = pltpu.make_async_copy(update.at[:, :, at], update_hbm.at[:, :, at], out_sem.at[2 + n])
        copy.start()
        outs.append(copy)

    for copy in first + roots + steps_a + steps_b + quarters + meta_c:
        copy.wait_send()
    for g in range(8):
        for ref, sem in ((code_out, a_send), (back, d_send)):
            gone = tiles_of(ref, g)
            send(gone, gone, sem.at[g], sem.at[g], on_column(x, c)).wait_send()
    for copy in meta_d + metas + sends:
        copy.wait_send()
    for copy in outs:
        copy.wait()
    out_l.wait()
    out_r.wait()


def place(update, left_new, right_new, update_out, left_out, right_out, sems):
    copies = [pltpu.make_async_copy(update.at[32 * p : 32 * p + 32], update_out.at[32 * p : 32 * p + 32], sems.at[p]) for p in range(4)]
    copies += [pltpu.make_async_copy(left_new, left_out, sems.at[4]), pltpu.make_async_copy(right_new, right_out, sems.at[5])]
    for copy in copies:
        copy.start()
    for copy in copies:
        copy.wait()


def local(grad_parts, left_stat, right_stat, left_root, right_root, block_slot, block_modality, modality_rates):
    vmem = pl.BlockSpec(memory_space=pltpu.VMEM)
    smem = pl.BlockSpec(memory_space=pltpu.SMEM)
    hbm = pl.BlockSpec(memory_space=pltpu.HBM)
    dma = pltpu.SemaphoreType.DMA
    update, left_new, right_new = pl.pallas_call(
        kernel,
        out_shape=(
            jax.ShapeDtypeStruct((128, 4, 512), F32),
            jax.ShapeDtypeStruct(left_stat.shape, F32),
            jax.ShapeDtypeStruct(right_stat.shape, F32),
        ),
        in_specs=[vmem, vmem, smem, hbm, hbm, hbm, hbm, hbm],
        out_specs=(hbm, hbm, hbm),
        scratch_shapes=[
            pltpu.VMEM((128, 4, 512), BF16),
            pltpu.VMEM((128, 512), F32),
            pltpu.VMEM((128, 512), F32),
            pltpu.VMEM((128, 512), BF16),
            pltpu.VMEM((4, 128, 512), BF16),
            pltpu.VMEM((4, 2, 2, 128, 128), BF16),
            pltpu.VMEM((4, 2, 2, 128, 128), BF16),
            pltpu.VMEM((8, 8, 8, 128), jnp.int16),
            pltpu.VMEM((8, 8, 128), F32),
            pltpu.VMEM((8, 8, 128), F32),
            pltpu.VMEM((8, 128), F32),
            pltpu.VMEM((8, 8, 128), F32),
            pltpu.VMEM((512, 128), F32),
            pltpu.VMEM((4, 8, 8, 8, 128), jnp.int16),
            pltpu.VMEM((4, 8, 128), F32),
            pltpu.VMEM((512, 512), BF16),
            pltpu.VMEM((512, 512), BF16),
            pltpu.VMEM((8, 8, 8, 128), F32),
            pltpu.VMEM((8, 8, 8, 128), jnp.int16),
            pltpu.VMEM((8, 8, 8, 128), jnp.int16),
            pltpu.VMEM((8, 128), F32),
            pltpu.VMEM((8, 8, 128), F32),
            pltpu.VMEM((8, 128), F32),
            pltpu.VMEM((8, 8, 128), F32),
            pltpu.VMEM((8, 128), F32),
            pltpu.VMEM((4, 2, 8, 128), F32),
            pltpu.VMEM((2, 4, 8, 8, 128), jnp.int16),
            pltpu.VMEM((4, 2, 4, 8, 8, 128), jnp.int16),
            pltpu.VMEM((4, 512, 128), F32),
            pltpu.VMEM((4, 512, 128), F32),
            pltpu.VMEM((512, 512), BF16),
            pltpu.VMEM((128, 4, 512), F32),
            pltpu.VMEM((128, 512), F32),
            pltpu.VMEM((128, 512), F32),
            pltpu.SemaphoreType.REGULAR,
            dma((5,)), dma((6,)),
            dma((4, 2, 2)), dma((4, 2, 2)),
            dma((4,)), dma((4,)),
            dma((8,)), dma((8,)),
            dma((8,)), dma((8,)),
            dma((8,)), dma((8,)),
            dma((4, 8)), dma((4, 8)),
            dma((4,)), dma((4,)),
            dma((8,)), dma((8,)),
            dma((8,)), dma((8,)),
            dma((8,)), dma((8,)),
            dma((4, 2)), dma((4, 2)),
            dma((4, 2, PIECES)), dma((4, 2, PIECES)),
        ],
        compiler_params=pltpu.CompilerParams(
            collective_id=1, has_side_effects=True, vmem_limit_bytes=24 * 2**20
        ),
        name="shampoo_step",
    )(
        *(
            pltpu.with_memory_space_constraint(array, pltpu.HBM)
            for array in (
                block_slot.reshape(1, 128), block_modality.reshape(1, 128), modality_rates,
                grad_parts, left_stat, right_stat, left_root, right_root,
            )
        ),
    )
    results = (update, left_new, right_new)
    return pl.pallas_call(
        place,
        out_shape=tuple(jax.ShapeDtypeStruct(result.shape, F32) for result in results),
        in_specs=[hbm] * 3,
        out_specs=(hbm,) * 3,
        scratch_shapes=[dma((6,))],
        compiler_params=pltpu.CompilerParams(vmem_limit_bytes=4 * 2**20),
        name="place_results",
    )(*results)


def solution(mesh):
    owner = P("dp", "rep", None)
    return jax.shard_map(
        local,
        mesh=mesh,
        in_specs=(P("rep", None, "dp", None), owner, owner, owner, owner, P(), P(), P()),
        out_specs=(P(None, "dp", None), owner, owner),
        check_vma=False,
    )
```

```python
import functools

import jax
import jax.numpy as jnp
from jax import lax
from jax.experimental import pallas as pl
from jax.experimental.pallas import tpu as pltpu
from jax.sharding import PartitionSpec as P

MESH = pl.DeviceIdType.MESH
DECAY = 0.95
CLIP = 0.5
BLK = 512
F32 = jnp.float32
BF16 = jnp.bfloat16
PIECES = 4
TOP = 4094 << 14


def iota(shape, axis):
    return lax.broadcasted_iota(jnp.int32, shape, axis)


def dot(a, b):
    return jnp.dot(a, b, preferred_element_type=F32)


def dot_nt(a, b):
    return lax.dot_general(a, b, (((1,), (1,)), ((), ())), preferred_element_type=F32)


def halves(value):
    high = value.astype(BF16)
    return high, (value - high.astype(F32)).astype(BF16)


def encode(value, inverse):
    count = (jnp.abs(value) * inverse + 0.5).astype(jnp.int32)
    shift = jnp.maximum(20 - lax.clz(count), 0)
    code = lax.shift_right_logical(count + lax.shift_right_logical(lax.shift_left(jnp.ones_like(shift), shift), 1), shift)
    code = code + lax.shift_left(shift, 11)
    return jnp.where(value < 0, -code, code).astype(jnp.int16)


def decode(code):
    code = code.astype(jnp.int32)
    size = jnp.abs(code)
    shift = jnp.maximum(lax.shift_right_logical(size, 11) - 1, 0)
    count = lax.shift_left(size - lax.shift_left(shift, 11), shift).astype(F32)
    return jnp.where(code < 0, -count, count)


def kernel(
    slot_ref, modality_ref, rates_ref, grad_hbm, lstat_hbm, rstat_hbm, lroot_hbm, rroot_hbm,
    update_hbm, lnew_hbm, rnew_hbm,
    grad, lstat, rstat, rroot, lfull, parts, got, code_out, step_out, step_plane, step_mid, step_mine, gown, gcode, gstep, ghigh, glow,
    rows_out, back, mine, meta_out, meta_plane, meta_mid, meta_mine, meta_own, meta_in, half, final, unscaled, scale_col, spread, update, lnew, rnew,
    ready, in_sem, out_sem, p_send, p_recv, l_send, l_recv, a_send, a_recv,
    t_send, t_recv, u_send, u_recv, g_send, g_recv, s_send, s_recv, d_send, d_recv, cm_send, cm_recv, dm_send, dm_recv, m_send, m_recv,
    f_send, f_recv,
):
    x = lax.axis_index("rep")
    d = lax.axis_index("dp")
    c = lax.rem(d, 2)
    z = lax.rem(lax.div(d, 2), 8)
    y = lax.div(d, 16)
    def on_plane(to_y, to_z):
        return (16 * to_y + 2 * to_z + c, x)

    def on_column(to_x, to_c):
        return (d - c + to_c, to_x)

    def send(src, dst, s_sem, r_sem, device):
        return pltpu.make_async_remote_copy(
            src_ref=src, dst_ref=dst, send_sem=s_sem, recv_sem=r_sem, device_id=device, device_id_type=MESH
        )

    column = [(dx, dc) for dx in (2, 1, 3, 0) for dc in (0, 1) if (dx, dc) != (0, 0)]

    loads = [
        pltpu.make_async_copy(grad_hbm.at[0], grad, in_sem.at[0]),
        pltpu.make_async_copy(lroot_hbm.at[0], lfull.at[x], in_sem.at[1]),
        pltpu.make_async_copy(rroot_hbm.at[0], rroot, in_sem.at[2]),
        pltpu.make_async_copy(lstat_hbm.at[0], lstat, in_sem.at[3]),
        pltpu.make_async_copy(rstat_hbm.at[0], rstat, in_sem.at[4]),
    ]
    loads[0].start()

    barrier = pltpu.get_barrier_semaphore()
    for dx, dc in column:
        pl.semaphore_signal(
            barrier, inc=1, device_id=on_column(lax.rem(x + dx, 4), lax.rem(c + dc, 2)), device_id_type=MESH
        )
    for e in range(1, 8):
        pl.semaphore_signal(barrier, inc=1, device_id=on_plane(lax.rem(y + e, 8), z), device_id_type=MESH)
        pl.semaphore_signal(barrier, inc=1, device_id=on_plane(y, lax.rem(z + e, 8)), device_id_type=MESH)

    for load in loads[1:]:
        load.start()

    slots = slot_ref[...]
    slots8 = jnp.broadcast_to(slots, (8, 128)).astype(F32).astype(BF16)
    widen = (lax.shift_right_logical(iota((128, 512), 1), 2) == iota((128, 512), 0)).astype(F32).astype(BF16)
    code_row = 4 * dot(slots8, widen)[0:1, :].astype(jnp.int32) + (iota((1, 512), 1) & 3)
    row = iota((512, 128), 0)
    row_y = (y + lax.shift_right_logical(row, 5)) & 7
    row_z = lax.shift_right_logical(row, 2) & 7
    row_slot = 16 * row_y + 2 * row_z + lax.shift_right_logical(row, 8)
    row_code = 4 * row_slot + (row & 3)
    order = jnp.concatenate(
        [(row_code == code_row[:, 128 * t : 128 * t + 128]).astype(F32).astype(BF16) for t in range(4)], axis=1
    )
    loads[0].wait()
    flat = grad[...].reshape(512, 512)
    for h in range(2):
        rows = jnp.concatenate([order[128 * h : 128 * h + 128], order[256 + 128 * h : 384 + 128 * h]], axis=0)
        ordered = dot(rows, flat).astype(BF16)
        for q in range(4):
            parts[q, 0, h] = ordered[:128, 128 * q : 128 * q + 128]
            parts[q, 1, h] = ordered[128:, 128 * q : 128 * q + 128]

    pl.semaphore_wait(barrier, len(column) + 14)
    first = []
    for h in range(2):
        for dx, dc in column:
            to_x, to_c = lax.rem(x + dx, 4), lax.rem(c + dc, 2)
            copy = send(
                parts.at[to_x, to_c, h], got.at[x, c, h], p_send.at[dx, dc, h], p_recv.at[dx, c, h], on_column(to_x, to_c)
            )
            copy.start()
            first.append(copy)
    for e in range(1, 8):
        pl.semaphore_signal(ready, inc=1, device_id=on_plane(lax.rem(y + e, 8), z), device_id_type=MESH)
    got[x, c] = parts[x, c]
    loads[1].wait()
    right, left = lax.rem(x + 1, 4), lax.rem(x + 3, 4)

    def root(n, q, rows, to):
        at = lfull.at[q, rows]
        return send(at, at, l_send.at[n], l_recv.at[n], on_column(to, c))

    every, low_half, high_half = pl.ds(0, 128), pl.ds(0, 64), pl.ds(64, 64)
    roots = [root(0, x, every, right), root(1, x, every, left), root(2, left, low_half, right), root(3, right, high_half, left)]
    upper = iota((16, 8, 128), 1) < 4
    lane = iota((8, 128), 1)
    sub = iota((8, 128), 0)

    def add_up(h):
        for dx, dc in column:
            from_c = lax.rem(c + dc, 2)
            send(parts.at[0, 0, h], got.at[0, 0, h], p_send.at[dx, dc, h], p_recv.at[dx, from_c, h], on_column(x, c)).wait_recv()
        sums = []
        for core in range(2):
            total = got[0, core, h].astype(F32)
            for q in range(1, 4):
                total = total + got[q, core, h].astype(F32)
            sums.append(total.reshape(16, 8, 128))
        even = jnp.where(upper, sums[0], pltpu.roll(sums[1], 4, 1))
        odd = jnp.where(upper, pltpu.roll(sums[0], 4, 1), sums[1])
        for which, value in ((0, even), (1, odd)):
            top = jnp.maximum(jnp.max(jnp.abs(value), axis=2, keepdims=True), 1e-30)
            scaled = value * (32767.0 / top)
            code = (scaled + jnp.where(scaled < 0, -0.5, 0.5)).astype(jnp.int32).astype(jnp.int16)
            step = top / 32767.0
            for n in range(4):
                tile = jnp.zeros((8, 128), F32)
                for p in range(4):
                    code_out[4 * h + n, 2 * p + which] = code[4 * n + p]
                    tile = jnp.where(lane == 8 * (2 * p + which) + y, step[4 * n + p], tile)
                if which == 0:
                    step_out[4 * h + n] = tile
                else:
                    step_out[4 * h + n] = step_out[4 * h + n] + tile


    def scatter(src, dst, g, s_sem, r_sem):
        to_y = lax.rem(y + g, 8)

        def one(e, carry):
            to_z = lax.rem(z + e, 8)
            send(src(to_y).at[to_z], dst, s_sem, r_sem, on_plane(to_y, to_z)).start()
            return carry

        lax.fori_loop(1 if g == 0 else 0, 8, one, 0)

    def tiles_of(ref, g):
        return ref.at[0, 1:8] if g == 0 else ref.at[0]

    quarters = []

    def forward(g):
        came = tiles_of(gcode.at[0], g)
        send(came, came, a_send.at[g], a_recv.at[g], on_column(x, c)).wait_recv()
        at = lax.rem(y + 8 - g, 8)
        for dx in (2, 1, 3):
            to = lax.rem(x + dx, 4)
            copy = send(gcode.at[x, at], gcode.at[x, at], g_send.at[dx, g], g_recv.at[dx, g], on_column(to, c))
            copy.start()
            quarters.append(copy)

    def first_scatter(g):
        scatter(lambda to_y: code_out.at[g], gcode.at[x, y, z], g, a_send.at[g], a_recv.at[g])

    add_up(0)
    gcode[x, y, z] = code_out[0, z]
    pl.semaphore_wait(ready, 7)
    for g in range(4):
        first_scatter(g)
    add_up(1)
    steps_a = []
    for g in range(1, 8):
        copy = send(step_out.at[g], step_plane.at[y], t_send.at[g], t_recv.at[g], on_plane(lax.rem(y + g, 8), z))
        copy.start()
        steps_a.append(copy)
    step_plane[y] = step_out[0]
    roots[0].start()
    roots[1].start()
    for g in range(4, 8):
        first_scatter(g)
    for copy in steps_a:
        copy.wait_recv()
    steps = step_plane[0]
    for e in range(1, 8):
        steps = steps + step_plane[e]
    step_mid[...] = steps
    steps_b = []
    for e in range(1, 8):
        copy = send(step_mid, step_mine.at[z], u_send.at[e], u_recv.at[e], on_plane(y, lax.rem(z + e, 8)))
        copy.start()
        steps_b.append(copy)
    step_mine[z] = steps
    for g in range(8):
        forward(g)
        if g == 4:
            roots[0].wait_recv()
            roots[2].start()
            roots[1].wait_recv()
            roots[3].start()
    for copy in steps_b:
        copy.wait_recv()
    steps = jnp.zeros((8, 128), F32)
    for e in range(8):
        turned = pltpu.roll(step_mine[e], lax.rem(8 * e + 128 - 8 * z, 128), 1)
        steps = jnp.where(lax.shift_right_logical(lane, 3) == e, turned, steps)
    gstep[x] = steps
    for dx in (2, 1, 3):
        copy = send(gstep.at[x], gstep.at[x], s_send.at[dx], s_recv.at[dx], on_column(lax.rem(x + dx, 4), c))
        copy.start()
        quarters.append(copy)

    def take(q, block):
        high, low = halves(block)
        at = pl.ds(pl.multiple_of(128 * q, 128), 128)
        ghigh[:, at] = high
        glow[:, at] = low
        other = rroot[:, at]
        return dot_nt(high, other) + dot_nt(low, other)

    def quarter(q):
        code = gcode[q].astype(jnp.int32).astype(F32).reshape(64, 8, 128)
        step = gstep[q]
        at = [8 * (k % 8) + k // 8 for k in range(64)]
        return jnp.concatenate([code[k] * step[:, at[k] : at[k] + 1] for k in range(64)], axis=0)

    def other_quarter(dx):
        q = lax.rem(x + 4 - dx, 4)
        for g in range(8):
            send(gcode.at[0, 0], gcode.at[0, 0], g_send.at[dx, g], g_recv.at[dx, g], on_column(x, c)).wait_recv()
        send(gstep.at[0], gstep.at[0], s_send.at[dx], s_recv.at[dx], on_column(x, c)).wait_recv()
        return take(q, quarter(q))

    loads[2].wait()
    own = quarter(x)
    gown[...] = own
    grad_sq = jnp.sum(own * own)
    product = take(x, own)
    product = product + other_quarter(1)
    product = product + other_quarter(3)
    product = product + other_quarter(2)
    roots[2].wait_recv()
    roots[3].wait_recv()
    product = jnp.concatenate(halves(product), axis=1)
    prec_sq = jnp.zeros((8, 128), F32)
    peak = jnp.zeros((8, 128), F32)
    for q in range(4):
        rows = dot(lfull[q], product)
        rows = (rows[:, :128] + rows[:, 128:]).reshape(16, 8, 128)
        prec_sq = prec_sq + jnp.sum(rows * rows, axis=0)
        peak = jnp.maximum(peak, jnp.max(jnp.abs(rows), axis=0))
        rows_out[2 * q : 2 * q + 2] = rows.reshape(2, 8, 8, 128)
    peak = jnp.maximum(jnp.max(jnp.max(peak, axis=0, keepdims=True), axis=1, keepdims=True), 1e-30)
    inverse = TOP / peak
    for e in range(8):
        back[e] = encode(rows_out[e], inverse)

    prec_sq = jnp.sum(jnp.sum(prec_sq, axis=0, keepdims=True), axis=1, keepdims=True)
    meta = jnp.where(lane == z, grad_sq, jnp.where(lane == 32 + z, peak / TOP, jnp.where(lane == 64 + z, prec_sq, 0.0)))
    meta_out[...] = jnp.where(sub == y, meta, 0.0)
    meta_plane[y] = meta_out[...]

    mine[0, z] = back[y, z]
    for g in range(4):
        scatter(lambda to_y: back.at[to_y], mine.at[g, z], g, d_send.at[g], d_recv.at[g])
    meta_c = []
    for e in range(1, 8):
        copy = send(meta_out, meta_plane.at[y], cm_send.at[e], cm_recv.at[e], on_plane(lax.rem(y + e, 8), z))
        copy.start()
        meta_c.append(copy)
    upper = iota((8, 8, 128), 1) < 4
    sends = []

    def hand_on(p):
        for g in (2 * p, 2 * p + 1):
            came = tiles_of(mine, g)
            send(came, came, d_send.at[g], d_recv.at[g], on_column(x, c)).wait_recv()
        tiles = mine[2 * p : 2 * p + 2].astype(jnp.int32).reshape(8, 2, 8, 128)
        a, b = tiles[:, 0], tiles[:, 1]
        half[0, p] = jnp.where(upper, a, pltpu.roll(b, 4, 1)).astype(jnp.int16)
        half[1, p] = jnp.where(upper, pltpu.roll(a, 4, 1), b).astype(jnp.int16)
        for dx, dc in column:
            to_x, to_c = lax.rem(x + dx, 4), lax.rem(c + dc, 2)
            copy = send(half.at[to_c, p], final.at[x, c, p], f_send.at[dx, dc, p], f_recv.at[dx, c, p], on_column(to_x, to_c))
            copy.start()
            sends.append(copy)
        final[x, c, p] = half[c, p]

    def came_on(dx, core, p):
        send(half.at[0, p], final.at[0, 0, p], f_send.at[1, 0, p], f_recv.at[dx, core, p], on_column(x, c)).wait_recv()

    def back_scatter(g):
        scatter(lambda to_y: back.at[to_y], mine.at[g, z], g, d_send.at[g], d_recv.at[g])

    back_scatter(4)
    back_scatter(5)
    hand_on(0)
    back_scatter(6)
    back_scatter(7)
    hand_on(1)
    for copy in meta_c:
        copy.wait_recv()
    meta = meta_plane[0]
    for e in range(1, 8):
        meta = meta + meta_plane[e]
    meta_mid[...] = meta
    meta_d = []
    for e in range(1, 8):
        copy = send(meta_mid, meta_mine.at[z], dm_send.at[e], dm_recv.at[e], on_plane(y, lax.rem(z + e, 8)))
        copy.start()
        meta_d.append(copy)
    meta_mine[z] = meta
    hand_on(2)
    hand_on(3)
    for copy in meta_d:
        copy.wait_recv()
    meta = meta_mine[0]
    for e in range(1, 8):
        meta = meta + meta_mine[e]
    meta_own[...] = meta
    metas = []
    for dx, dc in column:
        to_x, to_c = lax.rem(x + dx, 4), lax.rem(c + dc, 2)
        copy = send(meta_own, meta_in.at[x, c], m_send.at[dx, dc], m_recv.at[dx, c], on_column(to_x, to_c))
        copy.start()
        metas.append(copy)
    meta_in[x, c] = meta

    loads[3].wait()
    loads[4].wait()
    gain = (1.0 - DECAY) / BLK
    mine_rows = pl.ds(pl.multiple_of(128 * x, 128), 128)
    high, low = ghigh[...], glow[...]
    high_rows, low_rows = ghigh[mine_rows, :], glow[mine_rows, :]
    lnew[...] = DECAY * lstat[...] + gain * (dot_nt(high_rows, high) + (dot_nt(high_rows, low) + dot_nt(low_rows, high)))
    turned = gown[...].T
    high_turned, low_turned = halves(turned)
    rnew[...] = DECAY * rstat[...] + gain * (dot(high_turned, high) + (dot(high_turned, low) + dot(low_turned, high)))
    out_l = pltpu.make_async_copy(lnew, lnew_hbm.at[0], out_sem.at[0])
    out_r = pltpu.make_async_copy(rnew, rnew_hbm.at[0], out_sem.at[1])
    out_l.start()
    out_r.start()

    block_of_row = lax.shift_right_logical(row, 2)
    lanes = iota((512, 128), 1)
    is_block = lanes == block_of_row
    slot_col = jnp.sum(jnp.where(is_block, slots.astype(F32), 0.0), axis=1, keepdims=True)
    code_col = 4 * slot_col.astype(jnp.int32) + (iota((512, 1), 0) & 3)
    col = iota((1, 512), 1)
    col_y = (y + 8 - (lax.shift_right_logical(col, 5) & 7)) & 7
    col_z = lax.shift_right_logical(col, 2) & 7
    col_slot = 16 * col_y + 2 * col_z + lax.shift_right_logical(col, 8)
    col_code = 4 * col_slot + (col & 3)
    spread[...] = (code_col == col_code).astype(F32).astype(BF16)

    def gather(n, q):
        high, low = halves(decode(final[q]).reshape(512, 128))
        both = dot(spread[...], jnp.concatenate([high, low], axis=1))
        unscaled[n] = both[:, :128] + both[:, 128:]

    for p in range(PIECES):
        came_on(0, 1 - c, p)
    gather(0, x)
    for dx in (1, 3, 2):
        for p in range(PIECES):
            for core in range(2):
                came_on(dx, core, p)
        gather(dx, lax.rem(x + 4 - dx, 4))

    for dx, dc in column:
        send(meta_own, meta_in.at[0, 0], m_send.at[dx, dc], m_recv.at[dx, lax.rem(c + dc, 2)], on_column(x, c)).wait_recv()
    grad_b = jnp.zeros((8, 128), F32)
    prec_b = jnp.zeros((8, 128), F32)
    step_b = [jnp.zeros((8, 128), F32) for _ in range(4)]
    for core in range(2):
        known = [meta_in[q, core] for q in range(4)]
        both = known[0] + known[1] + known[2] + known[3]
        for e in range(8):
            here = slots == 16 * sub + 2 * e + core
            grad_b = grad_b + jnp.where(here, both[:, e : e + 1], 0.0)
            prec_b = prec_b + jnp.where(here, both[:, 64 + e : 65 + e], 0.0)
            for q in range(4):
                step_b[q] = step_b[q] + jnp.where(here, known[q][:, 32 + e : 33 + e], 0.0)
    grad_b = jnp.sum(grad_b, axis=0, keepdims=True)
    prec_b = jnp.sum(prec_b, axis=0, keepdims=True)
    scale = jnp.zeros((1, 128), F32)
    for m in range(2):
        member = modality_ref[...] == m
        total = jnp.sum(jnp.where(member, grad_b, 0.0), axis=1, keepdims=True)
        count = jnp.sum(jnp.where(member, 1.0, 0.0), axis=1, keepdims=True)
        rms = jnp.sqrt(total / (count * (BLK * BLK)) + 1e-6)
        clip = jnp.minimum(1.0, CLIP / rms)
        scale = jnp.where(member, rates_ref[m] * clip, scale)
    scale = scale * jnp.sqrt(grad_b / (prec_b + 1e-6))
    for q in range(4):
        step = scale * jnp.sum(step_b[q], axis=0, keepdims=True)
        scale_col[q] = jnp.broadcast_to(jnp.sum(jnp.where(is_block, step, 0.0), axis=1, keepdims=True), (512, 128))

    outs = []
    for n in range(4):
        q = lax.rem(x + 4 - n, 4)
        at = pl.ds(pl.multiple_of(128 * q, 128), 128)
        update[:, :, at] = (unscaled[n] * scale_col[q]).reshape(128, 4, 128)
        copy = pltpu.make_async_copy(update.at[:, :, at], update_hbm.at[:, :, at], out_sem.at[2 + n])
        copy.start()
        outs.append(copy)

    for copy in first + roots + steps_a + steps_b + quarters + meta_c:
        copy.wait_send()
    for g in range(8):
        for ref, sem in ((code_out, a_send), (back, d_send)):
            gone = tiles_of(ref, g)
            send(gone, gone, sem.at[g], sem.at[g], on_column(x, c)).wait_send()
    for copy in meta_d + metas + sends:
        copy.wait_send()
    for copy in outs:
        copy.wait()
    out_l.wait()
    out_r.wait()


def place(update, left_new, right_new, update_out, left_out, right_out, sems):
    copies = [pltpu.make_async_copy(update.at[32 * p : 32 * p + 32], update_out.at[32 * p : 32 * p + 32], sems.at[p]) for p in range(4)]
    copies += [pltpu.make_async_copy(left_new, left_out, sems.at[4]), pltpu.make_async_copy(right_new, right_out, sems.at[5])]
    for copy in copies:
        copy.start()
    for copy in copies:
        copy.wait()


def local(grad_parts, left_stat, right_stat, left_root, right_root, block_slot, block_modality, modality_rates):
    vmem = pl.BlockSpec(memory_space=pltpu.VMEM)
    smem = pl.BlockSpec(memory_space=pltpu.SMEM)
    hbm = pl.BlockSpec(memory_space=pltpu.HBM)
    dma = pltpu.SemaphoreType.DMA
    update, left_new, right_new = pl.pallas_call(
        kernel,
        out_shape=(
            jax.ShapeDtypeStruct((128, 4, 512), F32),
            jax.ShapeDtypeStruct(left_stat.shape, F32),
            jax.ShapeDtypeStruct(right_stat.shape, F32),
        ),
        in_specs=[vmem, vmem, smem, hbm, hbm, hbm, hbm, hbm],
        out_specs=(hbm, hbm, hbm),
        scratch_shapes=[
            pltpu.VMEM((128, 4, 512), BF16),
            pltpu.VMEM((128, 512), F32),
            pltpu.VMEM((128, 512), F32),
            pltpu.VMEM((128, 512), BF16),
            pltpu.VMEM((4, 128, 512), BF16),
            pltpu.VMEM((4, 2, 2, 128, 128), BF16),
            pltpu.VMEM((4, 2, 2, 128, 128), BF16),
            pltpu.VMEM((8, 8, 8, 128), jnp.int16),
            pltpu.VMEM((8, 8, 128), F32),
            pltpu.VMEM((8, 8, 128), F32),
            pltpu.VMEM((8, 128), F32),
            pltpu.VMEM((8, 8, 128), F32),
            pltpu.VMEM((512, 128), F32),
            pltpu.VMEM((4, 8, 8, 8, 128), jnp.int16),
            pltpu.VMEM((4, 8, 128), F32),
            pltpu.VMEM((512, 512), BF16),
            pltpu.VMEM((512, 512), BF16),
            pltpu.VMEM((8, 8, 8, 128), F32),
            pltpu.VMEM((8, 8, 8, 128), jnp.int16),
            pltpu.VMEM((8, 8, 8, 128), jnp.int16),
            pltpu.VMEM((8, 128), F32),
            pltpu.VMEM((8, 8, 128), F32),
            pltpu.VMEM((8, 128), F32),
            pltpu.VMEM((8, 8, 128), F32),
            pltpu.VMEM((8, 128), F32),
            pltpu.VMEM((4, 2, 8, 128), F32),
            pltpu.VMEM((2, 4, 8, 8, 128), jnp.int16),
            pltpu.VMEM((4, 2, 4, 8, 8, 128), jnp.int16),
            pltpu.VMEM((4, 512, 128), F32),
            pltpu.VMEM((4, 512, 128), F32),
            pltpu.VMEM((512, 512), BF16),
            pltpu.VMEM((128, 4, 512), F32),
            pltpu.VMEM((128, 512), F32),
            pltpu.VMEM((128, 512), F32),
            pltpu.SemaphoreType.REGULAR,
            dma((5,)), dma((6,)),
            dma((4, 2, 2)), dma((4, 2, 2)),
            dma((4,)), dma((4,)),
            dma((8,)), dma((8,)),
            dma((8,)), dma((8,)),
            dma((8,)), dma((8,)),
            dma((4, 8)), dma((4, 8)),
            dma((4,)), dma((4,)),
            dma((8,)), dma((8,)),
            dma((8,)), dma((8,)),
            dma((8,)), dma((8,)),
            dma((4, 2)), dma((4, 2)),
            dma((4, 2, PIECES)), dma((4, 2, PIECES)),
        ],
        compiler_params=pltpu.CompilerParams(
            collective_id=1, has_side_effects=True, vmem_limit_bytes=24 * 2**20
        ),
        name="shampoo_step",
    )(
        *(
            pltpu.with_memory_space_constraint(array, pltpu.HBM)
            for array in (
                block_slot.reshape(1, 128), block_modality.reshape(1, 128), modality_rates,
                grad_parts, left_stat, right_stat, left_root, right_root,
            )
        ),
    )
    results = (update, left_new, right_new)
    return pl.pallas_call(
        place,
        out_shape=tuple(jax.ShapeDtypeStruct(result.shape, F32) for result in results),
        in_specs=[hbm] * 3,
        out_specs=(hbm,) * 3,
        scratch_shapes=[dma((6,))],
        compiler_params=pltpu.CompilerParams(vmem_limit_bytes=4 * 2**20),
        name="place_results",
    )(*results)


def solution(mesh):
    owner = P("dp", "rep", None)
    return jax.shard_map(
        local,
        mesh=mesh,
        in_specs=(P("rep", None, "dp", None), owner, owner, owner, owner, P(), P(), P()),
        out_specs=(P(None, "dp", None), owner, owner),
        check_vma=False,
    )
```
